512 devices in a mesh: feat: 8 (over y, core), node: 64 (over x, z).
Axes of the slice: x: 4, y: 4, z: 16, core: 2. Of those that a mesh axis runs over, the one named last changes fastest.
Arguments:
- node_features: bfloat16 [32768, 1024], P('node', 'feat'), may hold values from -6 to 6
- self_one: bfloat16 [1024, 256], P('feat'), may hold values from -0.1875 to 0.1875
- neighbour_one: bfloat16 [1024, 256], P('feat'), may hold values from -0.75 to 0.75
- sample_ids: int32 [64, 64, 32], P('node'), may hold values from 0 to 511
- dest_slots: int32 [64, 64, 32], P('node'), may hold values from 0 to 127
- send_counts: int32 [64, 64], replicated, may hold values from 1 to 32, as said below
- self_ids: int32 [64, 128], P('node'), may hold values from 0 to 511
- tile_blocks: int32 [64, 4], P('node'), may hold values from 0 to 63, as said below
- tile_weights: bfloat16 [64, 4, 128, 128], P('node'), may hold values from -0.25 to 0.25
- self_two: bfloat16 [256, 256], replicated, may hold values from -0.375 to 0.375
- neighbour_two: bfloat16 [256, 256], replicated, may hold values from -0.375 to 0.375
- out_grad: bfloat16 [8192, 256], P('node'), may hold values from -6 to 6
Outputs:
- layer_output: bfloat16 [8192, 256], P('node')
- grad_self_one: float32 [1024, 256], P('feat')
- grad_neighbour_one: float32 [1024, 256], P('feat')
- grad_self_two: float32 [256, 256], replicated
- grad_neighbour_two: float32 [256, 256], replicated
The draws below stay inside these ranges and needn't reach their ends.
Inputs may be any that keep to these rules, and one draw needn't show every extreme that they name: `send_counts`: at most 32 slots go from one partition to one owner; in every draw some owner receives 32 from every partition, and every partition fills 32 slots to some owner. `tile_blocks`: the 4 blocks of one owner are distinct.
All inputs are finite; a program needn't handle non-finite values.
Results may differ from the reference program's by a relative error of at most 0.006.
Values may be sent and summed in bfloat16 or wider, within the bound.
No kernel may reach another device: no remote copies, remote signals or barrier semaphores. Data moves between devices by JAX's collectives and lax.ppermute only.
A program may use at most 128 MiB of HBM per device.

```python
import jax
import jax.numpy as jnp
from jax import lax

FIN = 1024
HID = 256
LOC = 512
CAP = 32
TGT = 128
KB = 4
BLK = 128
NODES = 32768
OWNED = 8192
NBLOCKS = 64
N_FEAT = 8
N_NODE = 64


def draw_send_counts(key, part):
    key = jax.random.fold_in(key, 11)
    first_key, second_key, third_key = jax.random.split(key, 3)
    base_counts = jax.random.randint(first_key, (N_NODE, N_NODE), CAP // 8, CAP // 2 + 1)
    hot_owner = jax.random.randint(second_key, (), 0, N_NODE)
    extra_owner = jax.random.randint(third_key, (N_NODE,), 0, N_NODE)
    owner_ids = jnp.arange(N_NODE)
    filled = (owner_ids[None, :] == hot_owner) | (owner_ids[None, :] == extra_owner[:, None])
    return jnp.where(filled, CAP, base_counts).astype(jnp.int32)


def draw_tile_blocks(key, part):
    key = jax.random.fold_in(key, 23)
    scores = jax.random.randint(key, (N_NODE, NBLOCKS), 0, 2 ** 20) * NBLOCKS + jnp.arange(NBLOCKS)
    top_scores, chosen = lax.top_k(scores, KB)
    return chosen.astype(jnp.int32)


def touch_ends(values, own_key, least, high):
    index_at = [jax.random.randint(jax.random.fold_in(own_key, axis), (), 0, length) for axis, length in enumerate(values.shape)]
    longest = values.shape.index(max(values.shape))
    neighbour = index_at[:longest] + [(index_at[longest] + 1) % values.shape[longest]] + index_at[longest + 1:]
    return values.at[tuple(index_at)].set(least).at[tuple(neighbour)].set(high)


def level_of(own_key, extent, shards, least, top_value):
    factor_of = 1.0
    for dim, shards_of in shards:
        draws = jax.random.uniform(jax.random.fold_in(jax.random.fold_in(own_key, 6), dim), (shards_of,), jnp.float32, least / len(shards), top_value / len(shards))
        factor_of = factor_of * jnp.repeat(jnp.exp(draws), extent[dim] // shards_of).reshape((-1,) + (1,) * (len(extent) - 1 - dim))
    return factor_of


def gaussian(own_key, shape, scale, reach, pieces=(), kind=jnp.bfloat16):
    result = jax.random.normal(own_key, shape, jnp.float32) * scale
    if len(pieces) > 0:
        result = level_of(own_key, shape, pieces, -0.22, 0.18) * result
    return jnp.clip(result, min=-reach, max=reach).astype(kind)


def setup_inputs(seed: int = 0) -> dict:
    arg_keys = jax.random.split(jax.random.key(seed), 13)
    node_features = gaussian(arg_keys[0], (NODES, FIN), 1.0, 6.0, ((0, 64), (1, 8)))
    self_one = gaussian(arg_keys[1], (FIN, HID), FIN ** -0.5, 0.1875, ((0, 8),))
    neighbour_one = gaussian(arg_keys[2], (FIN, HID), (FIN // 16) ** -0.5, 0.75, ((0, 8),))
    sample_ids = touch_ends(jax.random.randint(arg_keys[3], (N_NODE, N_NODE, CAP), 0, LOC), jax.random.fold_in(arg_keys[3], 1), 0, LOC - 1).astype(jnp.int32)
    dest_slots = touch_ends(jax.random.randint(arg_keys[4], (N_NODE, N_NODE, CAP), 0, TGT), jax.random.fold_in(arg_keys[4], 1), 0, TGT - 1).astype(jnp.int32)
    send_counts = draw_send_counts(jax.random.fold_in(arg_keys[12], 71), 0)
    self_ids = touch_ends(jax.random.randint(arg_keys[6], (N_NODE, TGT), 0, LOC), jax.random.fold_in(arg_keys[6], 1), 0, LOC - 1).astype(jnp.int32)
    tile_blocks = draw_tile_blocks(jax.random.fold_in(arg_keys[12], 71), 0)
    tile_weights = gaussian(arg_keys[8], (N_NODE, KB, TGT, BLK), (KB * BLK) ** -0.5, 0.25, ((0, 64),))
    self_two = gaussian(arg_keys[9], (HID, HID), HID ** -0.5, 0.375)
    neighbour_two = gaussian(arg_keys[10], (HID, HID), HID ** -0.5, 0.375)
    out_grad = gaussian(arg_keys[11], (OWNED, HID), 1.0, 6.0, ((0, 64),))
    return {"node_features": node_features, "self_one": self_one, "neighbour_one": neighbour_one, "sample_ids": sample_ids, "dest_slots": dest_slots, "send_counts": send_counts, "self_ids": self_ids, "tile_blocks": tile_blocks, "tile_weights": tile_weights, "self_two": self_two, "neighbour_two": neighbour_two, "out_grad": out_grad}


def silu_slope(values):
    sigma = jax.nn.sigmoid(values)
    return sigma * (1.0 + values * (1.0 - sigma))


def reference(node_features, self_one, neighbour_one, sample_ids, dest_slots, send_counts, self_ids, tile_blocks, tile_weights, self_two, neighbour_two, out_grad):
    slice_width = FIN // N_FEAT
    by_part = node_features.reshape(N_NODE, LOC, FIN)
    weights_sliced = neighbour_one.astype(jnp.float32).reshape(N_FEAT, slice_width, HID)
    slot_ids = jnp.arange(CAP, dtype=jnp.int32)
    owner_base = (jnp.arange(N_NODE, dtype=jnp.int32) * TGT)[:, None]

    def source_rows(source):
        local_rows = lax.dynamic_index_in_dim(by_part, source, 0, keepdims=False)
        picked_ids = lax.dynamic_index_in_dim(sample_ids, source, 0, keepdims=False).astype(jnp.int32)
        counts_row = lax.dynamic_index_in_dim(send_counts, source, 0, keepdims=False)
        valid = (slot_ids[None, :] < counts_row[:, None]).reshape(-1)
        where_to = (lax.dynamic_index_in_dim(dest_slots, source, 0, keepdims=False).astype(jnp.int32) + owner_base).reshape(-1)
        return local_rows[picked_ids.reshape(-1)], valid, where_to

    def forward_step(carry, source):
        sums, degree = carry
        gathered, valid, where_to = source_rows(source)
        sliced = gathered.astype(jnp.float32).reshape(-1, N_FEAT, slice_width)
        partial_msgs = jnp.einsum('rfs,fsh->rfh', sliced, weights_sliced)
        rounded = lax.optimization_barrier(partial_msgs.astype(jnp.bfloat16)).astype(jnp.float32)
        messages = jnp.sum(rounded, axis=1) * valid.astype(jnp.float32)[:, None]
        sums = sums + jax.ops.segment_sum(messages, where_to, N_NODE * TGT)
        degree = degree + jax.ops.segment_sum(valid.astype(jnp.float32), where_to, N_NODE * TGT)
        return (sums, degree), None

    start_sums = jnp.zeros((N_NODE * TGT, HID), jnp.float32)
    start_degree = jnp.zeros((N_NODE * TGT,), jnp.float32)
    sources = jnp.arange(N_NODE, dtype=jnp.int32)
    (sums, degree), _ = lax.scan(forward_step, (start_sums, start_degree), sources)

    owners = jnp.arange(N_NODE, dtype=jnp.int32)[:, None]
    self_rows = by_part[owners, self_ids.astype(jnp.int32)].reshape(-1, FIN)
    pre_one = jnp.dot(self_rows, self_one, preferred_element_type=jnp.float32) + sums / (degree + 1.0)[:, None]
    hidden_one = jax.nn.silu(pre_one).astype(jnp.bfloat16)

    blocks_all = hidden_one.reshape(NBLOCKS, BLK, HID)
    chosen = blocks_all[tile_blocks.astype(jnp.int32)]
    agg_two = jnp.einsum('oktb,okbh->oth', tile_weights.astype(jnp.float32), chosen.astype(jnp.float32)).reshape(-1, HID)
    agg_round = agg_two.astype(jnp.bfloat16)
    layer_output = (jnp.dot(hidden_one, self_two, preferred_element_type=jnp.float32) + jnp.dot(agg_round, neighbour_two, preferred_element_type=jnp.float32)).astype(jnp.bfloat16)

    grad_self_two = jnp.dot(hidden_one.T, out_grad, preferred_element_type=jnp.float32)
    grad_neighbour_two = jnp.dot(agg_round.T, out_grad, preferred_element_type=jnp.float32)
    agg_grad = jnp.dot(out_grad, neighbour_two.T, preferred_element_type=jnp.float32).astype(jnp.bfloat16)
    self_grad = jnp.dot(out_grad, self_two.T, preferred_element_type=jnp.float32)
    spread_back = jnp.einsum('oktb,oth->okbh', tile_weights.astype(jnp.float32), agg_grad.astype(jnp.float32).reshape(N_NODE, TGT, HID))
    row_grad = jnp.zeros((NBLOCKS, BLK, HID), jnp.float32).at[tile_blocks.astype(jnp.int32).reshape(-1)].add(spread_back.reshape(-1, BLK, HID)).reshape(-1, HID)
    pre_grad = (self_grad + row_grad) * silu_slope(pre_one)
    pre_round = pre_grad.astype(jnp.bfloat16)
    mean_grad = (pre_grad / (degree + 1.0)[:, None]).astype(jnp.bfloat16)
    grad_self_one = jnp.dot(self_rows.T, pre_round, preferred_element_type=jnp.float32)

    def backward_step(total, source):
        gathered, valid, where_to = source_rows(source)
        slot_grads = mean_grad[where_to] * valid.astype(mean_grad.dtype)[:, None]
        return total + jnp.dot(gathered.T, slot_grads, preferred_element_type=jnp.float32), None

    grad_neighbour_one, _ = lax.scan(backward_step, jnp.zeros((FIN, HID), jnp.float32), sources)
    return (layer_output, grad_self_one, grad_neighbour_one, grad_self_two, grad_neighbour_two)
```

```python
import jax
import jax.numpy as jnp
from jax import lax
from jax.sharding import PartitionSpec as P

bf16 = jnp.bfloat16
f32 = jnp.float32


def dot(a, b, dims):
    return lax.dot_general(a, b, (dims, ((), ())), preferred_element_type=f32)


def exchange(values, axis, groups=None):
    return lax.all_to_all(
        values, axis, split_axis=0, concat_axis=0, tiled=True, axis_index_groups=groups
    )


def to_all(values, count):
    return jnp.broadcast_to(values[None], (count,) + values.shape)


def pick(table, row_ids):
    local_ids = jnp.arange(table.shape[0], dtype=jnp.int32)
    chosen = (row_ids[:, None] == local_ids[None, :]).astype(table.dtype)
    return dot(chosen, table, ((1,), (0,))).astype(table.dtype)


def shards(
    features,
    self_one,
    neighbour_one,
    sample_ids,
    dest_slots,
    send_counts,
    self_ids,
    tile_blocks,
    tile_weights,
    self_two,
    neighbour_two,
    out_grad,
):
    feats = lax.axis_size("feat")
    nodes = lax.axis_size("node")
    nx = 4
    nz = nodes // nx
    along_x = [[x * nz + z for x in range(nx)] for z in range(nz)]
    along_z = [[x * nz + z for z in range(nz)] for x in range(nx)]
    device = lax.axis_index("node")
    feat = lax.axis_index("feat")
    x_at, z_at = device // nz, device % nz
    capacity = sample_ids.shape[2]
    targets = self_ids.shape[1]
    width = features.shape[1]
    hidden = neighbour_one.shape[1]
    part = hidden // feats
    block_ids = tile_blocks[0]
    tiles = tile_weights[0]

    sent_counts = lax.dynamic_index_in_dim(send_counts, device, 0, keepdims=False)
    used = jnp.arange(capacity, dtype=jnp.int32)[None, :] < sent_counts[:, None]
    slots = jnp.where(used, dest_slots[0], targets).astype(bf16)
    slot_rows = jnp.pad(slots[:, None, :], ((0, 0), (0, 7), (0, width - capacity)))
    rows = pick(features, sample_ids[0].reshape(-1)).reshape(nodes, capacity, width)
    came = exchange(jnp.concatenate([rows, slot_rows], axis=1), "node")
    came_rows = came[:, :capacity].reshape(-1, width)
    came_slots = came[:, capacity, :capacity].reshape(-1).astype(jnp.int32)

    grad_t = lax.dynamic_slice_in_dim(out_grad.T, feat * part, part, 0)
    terms = jnp.einsum("kt,ntb->nkb", grad_t, tiles, preferred_element_type=f32)
    here = block_ids[None, :] == jnp.arange(nodes, dtype=jnp.int32)[:, None]
    placed = sum(
        jnp.where(here[:, n, None, None], terms[n][None], 0.0) for n in range(tiles.shape[0])
    ).astype(bf16)
    placed = exchange(placed, "node", along_x).reshape((nx, nz) + placed.shape[1:])
    placed = exchange(jnp.sum(placed.astype(f32), axis=0).astype(bf16), "node", along_z)
    back_part = jnp.sum(placed.astype(f32), axis=0).astype(bf16)
    back_t = exchange(to_all(back_part, feats), "feat").reshape(hidden, targets)

    self_rows = pick(features, self_ids[0])
    chosen = came_slots[None, :] == jnp.arange(targets, dtype=jnp.int32)[:, None]
    degree = jnp.sum(chosen.astype(f32), axis=1)
    summed = dot(chosen.astype(bf16), came_rows, ((1,), (0,)))
    mean = summed / (degree + 1.0)[:, None]
    mean_high = mean.astype(bf16)
    mean_low = (mean - mean_high.astype(f32)).astype(bf16)
    terms_one = (
        dot(self_one, self_rows, ((0,), (1,)))
        + dot(neighbour_one, mean_high, ((0,), (1,)))
        + dot(neighbour_one, mean_low, ((0,), (1,)))
    )
    pre_one = jnp.sum(exchange(terms_one.reshape(feats, part, targets), "feat"), axis=0)
    sigma = jax.nn.sigmoid(pre_one)
    hidden_part = (pre_one * sigma).astype(bf16)
    slope = sigma * (1.0 + pre_one * (1.0 - sigma))

    self_two_part = lax.dynamic_slice_in_dim(self_two, feat * part, part, 0)
    neighbour_two_part = lax.dynamic_slice_in_dim(neighbour_two, feat * part, part, 0)
    pre_grad = (
        dot(self_two_part, out_grad, ((1,), (1,))) + dot(neighbour_two_part, back_t, ((1,), (0,)))
    ) * slope
    full = exchange(
        to_all(jnp.concatenate([pre_grad.astype(bf16), hidden_part], axis=0), feats), "feat"
    )
    pre_round = full[:, :part].reshape(hidden, targets)
    hidden_t = full[:, part:].reshape(hidden, targets)

    upper_self = dot(hidden_part, out_grad, ((1,), (0,)))
    upper_others = dot(hidden_part, back_t, ((1,), (1,)))
    half = hidden // 2
    upper = jnp.concatenate(
        [upper_self[:, :half], upper_self[:, half:], upper_others[:, :half], upper_others[:, half:]],
        axis=0,
    ).astype(bf16)
    share = upper.shape[0] // nz
    sent = jnp.concatenate([to_all(hidden_part, nz), upper.reshape(nz, share, half)], axis=1)
    got = exchange(sent, "node", along_z)
    upper_sum = jnp.sum(got[:, part:].astype(f32), axis=0).astype(bf16)
    column = jnp.concatenate([got[:, :part].reshape(nz * part, targets), upper_sum], axis=0)
    got = exchange(to_all(column, nx), "node", along_x)
    upper_sum = jnp.sum(got[:, nz * part :].astype(f32), axis=0).astype(bf16)
    all_hidden = got[:, : nz * part].reshape(nodes, part, targets)
    agg_part = sum(
        dot(lax.dynamic_index_in_dim(all_hidden, block_ids[n], 0, keepdims=False), tiles[n], ((1,), (1,)))
        for n in range(tiles.shape[0])
    ).astype(bf16)
    got = exchange(to_all(jnp.concatenate([agg_part, upper_sum], axis=0), feats), "feat")
    agg_t = got[:, :part].reshape(hidden, targets)
    upper_parts = got[:, part:]
    layer_output = (
        dot(hidden_t, self_two, ((0,), (0,))) + dot(agg_t, neighbour_two, ((0,), (0,)))
    ).astype(bf16)

    lower_self = dot(self_rows, pre_round, ((0,), (1,)))
    lower_others = dot(mean_high, pre_round, ((0,), (1,)))
    lower = jnp.concatenate(
        [lower_self[:, :half], lower_self[:, half:], lower_others[:, :half], lower_others[:, half:]],
        axis=0,
    ).astype(bf16)
    rows_each = lower.shape[0] // nodes
    got = exchange(lower.reshape(nodes, rows_each, half), "node")
    lower_sum = jnp.sum(got.astype(f32), axis=0).astype(bf16)
    each = feats // nx
    mine = lax.dynamic_slice_in_dim(upper_parts, x_at * each, each, 0).reshape(each * share, half)
    got = exchange(to_all(jnp.concatenate([lower_sum, mine], axis=0), nodes), "node")
    lower = got[:, :rows_each].reshape(4, width, half).astype(f32)
    upper = got[:, rows_each:].reshape(nx, nz, each, share, half)
    upper = upper.transpose(0, 2, 1, 3, 4).reshape(feats, 4, part, half).astype(f32)
    upper = upper.transpose(1, 0, 2, 3).reshape(4, hidden, half)

    def halves(stack, which):
        return jnp.concatenate([stack[2 * which], stack[2 * which + 1]], axis=1)

    return (layer_output, halves(lower, 0), halves(lower, 1), halves(upper, 0), halves(upper, 1))


def solution(mesh):
    placed = (
        P("node", "feat"),
        P("feat", None),
        P("feat", None),
        P("node", None, None),
        P("node", None, None),
        P(),
        P("node", None),
        P("node", None),
        P("node", None, None, None),
        P(),
        P(),
        P("node", None),
    )
    return jax.shard_map(
        shards,
        mesh=mesh,
        in_specs=placed,
        out_specs=(P("node", None), P("feat", None), P("feat", None), P(), P()),
        check_vma=False,
    )
```

```python
import jax
import jax.numpy as jnp
from jax import lax
from jax.sharding import PartitionSpec as P

bf16 = jnp.bfloat16
f32 = jnp.float32


def dot(a, b, dims):
    return lax.dot_general(a, b, (dims, ((), ())), preferred_element_type=f32)


def exchange(values, axis, groups=None):
    return lax.all_to_all(
        values, axis, split_axis=0, concat_axis=0, tiled=True, axis_index_groups=groups
    )


def to_all(values, count):
    return jnp.broadcast_to(values[None], (count,) + values.shape)


def pick(table, row_ids):
    local_ids = jnp.arange(table.shape[0], dtype=jnp.int32)
    chosen = (row_ids[:, None] == local_ids[None, :]).astype(table.dtype)
    return dot(chosen, table, ((1,), (0,))).astype(table.dtype)


def split(values):
    high = values.astype(bf16)
    return high, (values - high.astype(f32)).astype(bf16)


def quarters(first, second):
    half = first.shape[1] // 2
    parts = [first[:, :half], first[:, half:], second[:, :half], second[:, half:]]
    return jnp.concatenate(parts, axis=0).astype(bf16)


def shards(
    features,
    self_one,
    neighbour_one,
    sample_ids,
    dest_slots,
    send_counts,
    self_ids,
    tile_blocks,
    tile_weights,
    self_two,
    neighbour_two,
    out_grad,
):
    feats = lax.axis_size("feat")
    nodes = lax.axis_size("node")
    nx = 4
    nz = nodes // nx
    along_x = [[x * nz + z for x in range(nx)] for z in range(nz)]
    along_z = [[x * nz + z for z in range(nz)] for x in range(nx)]
    device = lax.axis_index("node")
    feat = lax.axis_index("feat")
    capacity = sample_ids.shape[2]
    targets = self_ids.shape[1]
    width = features.shape[1]
    hidden = neighbour_one.shape[1]
    part = hidden // feats
    block_ids = tile_blocks[0]
    tiles = tile_weights[0]

    sent_counts = lax.dynamic_index_in_dim(send_counts, device, 0, keepdims=False)
    used = jnp.arange(capacity, dtype=jnp.int32)[None, :] < sent_counts[:, None]
    slots = jnp.where(used, dest_slots[0], targets).astype(bf16)
    slot_rows = jnp.pad(slots[:, None, :], ((0, 0), (0, 7), (0, width - capacity)))
    rows = pick(features, sample_ids[0].reshape(-1)).reshape(nodes, capacity, width)

    grad_t = lax.dynamic_slice_in_dim(out_grad.T, feat * part, part, 0)
    terms = jnp.einsum("kt,ntb->nkb", grad_t, tiles, preferred_element_type=f32)
    here = block_ids[None, :] == jnp.arange(nodes, dtype=jnp.int32)[:, None]
    placed = sum(
        jnp.where(here[:, n, None, None], terms[n][None], 0.0) for n in range(tiles.shape[0])
    ).astype(bf16)
    came = exchange(jnp.concatenate([rows, placed, slot_rows], axis=1), "node")
    came_rows = came[:, :capacity].reshape(-1, width)
    came_slots = came[:, capacity + part, :capacity].reshape(-1).astype(jnp.int32)
    back_part = jnp.sum(came[:, capacity : capacity + part].astype(f32), axis=0).astype(bf16)

    self_rows = pick(features, self_ids[0])
    chosen = came_slots[None, :] == jnp.arange(targets, dtype=jnp.int32)[:, None]
    degree = jnp.sum(chosen.astype(f32), axis=1)
    summed = dot(chosen.astype(bf16), came_rows, ((1,), (0,)))
    mean = summed / (degree + 1.0)[:, None]
    mean_high, mean_low = split(mean)
    terms_one = (
        dot(self_one, self_rows, ((0,), (1,)))
        + dot(neighbour_one, mean_high, ((0,), (1,)))
        + dot(neighbour_one, mean_low, ((0,), (1,)))
    )
    high, low = split(terms_one.reshape(feats, part, targets))
    got = exchange(jnp.concatenate([high, low, to_all(back_part, feats)], axis=1), "feat")
    pre_one = jnp.sum(got[:, :part].astype(f32) + got[:, part : 2 * part].astype(f32), axis=0)
    back_t = got[:, 2 * part :].reshape(hidden, targets)
    sigma = jax.nn.sigmoid(pre_one)
    hidden_part = (pre_one * sigma).astype(bf16)
    slope = sigma * (1.0 + pre_one * (1.0 - sigma))

    self_two_part = lax.dynamic_slice_in_dim(self_two, feat * part, part, 0)
    neighbour_two_part = lax.dynamic_slice_in_dim(neighbour_two, feat * part, part, 0)
    pre_grad = (
        dot(self_two_part, out_grad, ((1,), (1,))) + dot(neighbour_two_part, back_t, ((1,), (0,)))
    ) * slope
    full = exchange(
        to_all(jnp.concatenate([pre_grad.astype(bf16), hidden_part], axis=0), feats), "feat"
    )
    pre_round = full[:, :part].reshape(hidden, targets)
    hidden_t = full[:, part:].reshape(hidden, targets)

    half = hidden // 2
    upper = quarters(
        dot(hidden_part, out_grad, ((1,), (0,))), dot(hidden_part, back_t, ((1,), (1,)))
    )
    lower = quarters(
        dot(self_rows, pre_round, ((0,), (1,))), dot(mean_high, pre_round, ((0,), (1,)))
    )
    share = upper.shape[0] // nz
    rows_each = lower.shape[0] // nz
    sent = [to_all(hidden_part, nz), lower.reshape(nz, rows_each, half), upper.reshape(nz, share, half)]
    got = exchange(jnp.concatenate(sent, axis=1), "node", along_z)
    sums = split(jnp.sum(got[:, part:].astype(f32), axis=0))
    column = jnp.concatenate([got[:, :part].reshape(nz * part, targets), *sums], axis=0)
    got = exchange(to_all(column, nx), "node", along_x)
    all_hidden = got[:, : nz * part].reshape(nodes, part, targets)
    sums = got[:, nz * part :].reshape(2 * nx, rows_each + share, half).astype(f32)
    got = exchange(to_all(jnp.sum(sums, axis=0).astype(bf16), nz), "node", along_z)
    lower = got[:, :rows_each].reshape(4, width, half).astype(f32)

    agg_part = sum(
        dot(lax.dynamic_index_in_dim(all_hidden, block_ids[n], 0, keepdims=False), tiles[n], ((1,), (1,)))
        for n in range(tiles.shape[0])
    ).astype(bf16)
    upper = got[:, rows_each:].reshape(nz * share, half)
    got = exchange(to_all(jnp.concatenate([agg_part, upper], axis=0), feats), "feat")
    agg_t = got[:, :part].reshape(hidden, targets)
    layer_output = (
        dot(hidden_t, self_two, ((0,), (0,))) + dot(agg_t, neighbour_two, ((0,), (0,)))
    ).astype(bf16)
    upper = got[:, part:].reshape(feats, 4, part, half).astype(f32)
    upper = upper.transpose(1, 0, 2, 3).reshape(4, hidden, half)

    def halves(stack, which):
        return jnp.concatenate([stack[2 * which], stack[2 * which + 1]], axis=1)

    return (layer_output, halves(lower, 0), halves(lower, 1), halves(upper, 0), halves(upper, 1))


def solution(mesh):
    placed = (
        P("node", "feat"),
        P("feat", None),
        P("feat", None),
        P("node", None, None),
        P("node", None, None),
        P(),
        P("node", None),
        P("node", None),
        P("node", None, None, None),
        P(),
        P(),
        P("node", None),
    )
    return jax.shard_map(
        shards,
        mesh=mesh,
        in_specs=placed,
        out_specs=(P("node", None), P("feat", None), P("feat", None), P(), P()),
        check_vma=False,
    )
```

```python
import jax
import jax.numpy as jnp
from jax import lax
from jax.sharding import PartitionSpec as P

bf16 = jnp.bfloat16
f32 = jnp.float32


def dot(a, b, dims):
    return lax.dot_general(a, b, (dims, ((), ())), preferred_element_type=f32)


def exchange(values, axis, groups=None):
    return lax.all_to_all(
        values, axis, split_axis=0, concat_axis=0, tiled=True, axis_index_groups=groups
    )


def to_all(values, count):
    return jnp.broadcast_to(values[None], (count,) + values.shape)


def pick(table, row_ids):
    local_ids = jnp.arange(table.shape[0], dtype=jnp.int32)
    chosen = (row_ids[:, None] == local_ids[None, :]).astype(table.dtype)
    return dot(chosen, table, ((1,), (0,))).astype(table.dtype)


def split(values):
    high = lax.reduce_precision(values, 8, 7)
    return high.astype(bf16), (values - high).astype(bf16)


def quarters(first, second):
    half = first.shape[1] // 2
    parts = [first[:, :half], first[:, half:], second[:, :half], second[:, half:]]
    return jnp.concatenate(parts, axis=0).astype(bf16)


def shards(
    features,
    self_one,
    neighbour_one,
    sample_ids,
    dest_slots,
    send_counts,
    self_ids,
    tile_blocks,
    tile_weights,
    self_two,
    neighbour_two,
    out_grad,
):
    feats = lax.axis_size("feat")
    nodes = lax.axis_size("node")
    nx = 4
    nz = nodes // nx
    along_x = [[x * nz + z for x in range(nx)] for z in range(nz)]
    along_z = [[x * nz + z for z in range(nz)] for x in range(nx)]
    device = lax.axis_index("node")
    x_at = device // nz
    feat = lax.axis_index("feat")
    capacity = sample_ids.shape[2]
    targets = self_ids.shape[1]
    width = features.shape[1]
    hidden = neighbour_one.shape[1]
    part = hidden // feats
    block_ids = tile_blocks[0]
    tiles = tile_weights[0]

    sent_counts = lax.dynamic_index_in_dim(send_counts, device, 0, keepdims=False)
    used = jnp.arange(capacity, dtype=jnp.int32)[None, :] < sent_counts[:, None]
    slots = jnp.tile(jnp.where(used, dest_slots[0], targets), (1, nx))
    own_lanes = jnp.arange(nx * capacity, dtype=jnp.int32) // capacity == x_at
    slots = jnp.where(own_lanes[None, :], slots, 0).astype(bf16)
    rows = pick(features, sample_ids[0].reshape(-1))
    grad_t = lax.dynamic_slice_in_dim(out_grad.T, feat * part, part, 0)
    terms = jnp.einsum("kt,ntb->nkb", grad_t, tiles, preferred_element_type=f32).astype(bf16)
    count = tiles.shape[0]
    in_x = (block_ids // nz)[None, :] == jnp.arange(nx, dtype=jnp.int32)[:, None]
    terms = jnp.where(in_x[:, :, None, None], terms[None], jnp.zeros((), bf16))
    block_z = jnp.broadcast_to((block_ids % nz)[:, None], (count, targets)).astype(bf16)
    sent = [
        rows.reshape(nx, nz * capacity, width),
        slots.reshape(nx, nz, width),
        terms.reshape(nx, count * part, targets),
        to_all(jnp.pad(block_z, ((0, 8 - count), (0, 0))), nx),
    ]
    got = exchange(jnp.concatenate(sent, axis=1), "node", along_x)

    ends = [nz * capacity, nz * capacity + nz, nz * capacity + nz + count * part]
    rows = got[:, : ends[0]].reshape(nx, nz, capacity, width).transpose(1, 0, 2, 3)
    slots = jnp.sum(got[:, ends[0] : ends[1]].astype(f32), axis=0).astype(bf16)
    terms = got[:, ends[1] : ends[2]].reshape(nx * count, part, targets).astype(f32)
    block_z = got[:, ends[2] : ends[2] + count].reshape(nx * count, 1, targets).astype(jnp.int32)
    z_ids = jnp.arange(nz, dtype=jnp.int32)[:, None, None]
    terms = sum(
        jnp.where(block_z[n][None] == z_ids, terms[n][None], 0.0) for n in range(nx * count)
    ).astype(bf16)
    per_z = nx * capacity
    sent = [
        rows.reshape(nz, per_z, width),
        terms,
        jnp.pad(slots[:, None, :], ((0, 0), (0, 7), (0, 0))),
    ]
    came = exchange(jnp.concatenate(sent, axis=1), "node", along_z)
    back_part = jnp.sum(came[:, per_z : per_z + part].astype(f32), axis=0).astype(bf16)

    self_rows = pick(features, self_ids[0])
    came_slots = came[:, per_z + part].astype(jnp.int32)
    target_ids = jnp.arange(targets, dtype=jnp.int32)
    chosen = came_slots[:, None, :] == target_ids[None, :, None]
    degree = jnp.sum(chosen.astype(f32), axis=(0, 2))
    summed = jnp.einsum(
        "ztr,zrs->ts", chosen.astype(bf16), came[:, :per_z], preferred_element_type=f32
    )
    mean = summed / (degree + 1.0)[:, None]
    mean_high, mean_low = split(mean)
    terms_one = (
        dot(self_one, self_rows, ((0,), (1,)))
        + dot(neighbour_one, mean_high, ((0,), (1,)))
        + dot(neighbour_one, mean_low, ((0,), (1,)))
    )
    high, low = split(terms_one.reshape(feats, part, targets))
    got = exchange(jnp.concatenate([high, low, to_all(back_part, feats)], axis=1), "feat")
    pre_one = jnp.sum(got[:, :part].astype(f32) + got[:, part : 2 * part].astype(f32), axis=0)
    back_t = got[:, 2 * part :].reshape(hidden, targets)
    sigma = jax.nn.sigmoid(pre_one)
    hidden_part = (pre_one * sigma).astype(bf16)
    slope = sigma * (1.0 + pre_one * (1.0 - sigma))

    self_two_part = lax.dynamic_slice_in_dim(self_two, feat * part, part, 0)
    neighbour_two_part = lax.dynamic_slice_in_dim(neighbour_two, feat * part, part, 0)
    pre_grad = (
        dot(self_two_part, out_grad, ((1,), (1,))) + dot(neighbour_two_part, back_t, ((1,), (0,)))
    ) * slope
    full = exchange(
        to_all(jnp.concatenate([pre_grad.astype(bf16), hidden_part], axis=0), feats), "feat"
    )
    pre_round = full[:, :part].reshape(hidden, targets)
    hidden_t = full[:, part:].reshape(hidden, targets)

    half = hidden // 2
    upper = quarters(
        dot(hidden_part, out_grad, ((1,), (0,))), dot(hidden_part, back_t, ((1,), (1,)))
    )
    lower = quarters(
        dot(self_rows, pre_round, ((0,), (1,))), dot(mean_high, pre_round, ((0,), (1,)))
    )
    share = upper.shape[0] // nz
    rows_each = lower.shape[0] // nz
    sent = [to_all(hidden_part, nz), lower.reshape(nz, rows_each, half), upper.reshape(nz, share, half)]
    got = exchange(jnp.concatenate(sent, axis=1), "node", along_z)
    sums = split(jnp.sum(got[:, part:].astype(f32), axis=0))
    column = jnp.concatenate([got[:, :part].reshape(nz * part, targets), *sums], axis=0)
    got = exchange(to_all(column, nx), "node", along_x)
    all_hidden = got[:, : nz * part].reshape(nodes, part, targets)
    sums = got[:, nz * part :].reshape(2 * nx, rows_each + share, half).astype(f32)
    got = exchange(to_all(jnp.sum(sums, axis=0).astype(bf16), nz), "node", along_z)
    lower = got[:, :rows_each].reshape(4, width, half).astype(f32)

    agg_part = sum(
        dot(lax.dynamic_index_in_dim(all_hidden, block_ids[n], 0, keepdims=False), tiles[n], ((1,), (1,)))
        for n in range(tiles.shape[0])
    ).astype(bf16)
    upper = got[:, rows_each:].reshape(nz * share, half)
    got = exchange(to_all(jnp.concatenate([agg_part, upper], axis=0), feats), "feat")
    agg_t = got[:, :part].reshape(hidden, targets)
    layer_output = (
        dot(hidden_t, self_two, ((0,), (0,))) + dot(agg_t, neighbour_two, ((0,), (0,)))
    ).astype(bf16)
    upper = got[:, part:].reshape(feats, 4, part, half).astype(f32)
    upper = upper.transpose(1, 0, 2, 3).reshape(4, hidden, half)

    def halves(stack, which):
        return jnp.concatenate([stack[2 * which], stack[2 * which + 1]], axis=1)

    return (layer_output, halves(lower, 0), halves(lower, 1), halves(upper, 0), halves(upper, 1))


def solution(mesh):
    placed = (
        P("node", "feat"),
        P("feat", None),
        P("feat", None),
        P("node", None, None),
        P("node", None, None),
        P(),
        P("node", None),
        P("node", None),
        P("node", None, None, None),
        P(),
        P(),
        P("node", None),
    )
    return jax.shard_map(
        shards,
        mesh=mesh,
        in_specs=placed,
        out_specs=(P("node", None), P("feat", None), P("feat", None), P(), P()),
        check_vma=False,
    )
```

```python
import jax
import jax.numpy as jnp
from jax import lax
from jax.sharding import PartitionSpec as P

bf16 = jnp.bfloat16
f32 = jnp.float32


def dot(a, b, dims):
    return lax.dot_general(a, b, (dims, ((), ())), preferred_element_type=f32)


def exchange(values, axis, groups=None):
    return lax.all_to_all(
        values, axis, split_axis=0, concat_axis=0, tiled=True, axis_index_groups=groups
    )


def to_all(values, count):
    return jnp.broadcast_to(values[None], (count,) + values.shape)


def pick(table, row_ids):
    local_ids = jnp.arange(table.shape[0], dtype=jnp.int32)
    chosen = (row_ids[:, None] == local_ids[None, :]).astype(table.dtype)
    return dot(chosen, table, ((1,), (0,))).astype(table.dtype)


def split(values):
    high = lax.reduce_precision(values, 8, 7)
    return high.astype(bf16), (values - high).astype(bf16)


def quarters(first, second):
    half = first.shape[1] // 2
    parts = [first[:, :half], first[:, half:], second[:, :half], second[:, half:]]
    return jnp.concatenate(parts, axis=0).astype(bf16)


def shards(
    features,
    self_one,
    neighbour_one,
    sample_ids,
    dest_slots,
    send_counts,
    self_ids,
    tile_blocks,
    tile_weights,
    self_two,
    neighbour_two,
    out_grad,
):
    feats = lax.axis_size("feat")
    nodes = lax.axis_size("node")
    nx, nb = 4, 2
    na = nodes // (nx * nb)
    near = nx * nb
    near_ids = [(x * na + a) * nb + b for a in range(na) for x in range(nx) for b in range(nb)]
    near_groups = [near_ids[a * near : (a + 1) * near] for a in range(na)]
    far_groups = [list(group) for group in zip(*near_groups)]
    device = lax.axis_index("node")
    feat = lax.axis_index("feat")
    near_at = device // (na * nb) * nb + device % nb
    capacity = sample_ids.shape[2]
    targets = self_ids.shape[1]
    width = features.shape[1]
    hidden = neighbour_one.shape[1]
    part = hidden // feats
    block_ids = tile_blocks[0]
    block_near = block_ids // (na * nb) * nb + block_ids % nb
    block_far = block_ids % (na * nb) // nb
    tiles = tile_weights[0]
    count = tiles.shape[0]
    lanes = targets // capacity

    def by_near(values):
        values = values.reshape((nx, na, nb) + values.shape[1:])
        return jnp.swapaxes(values, 1, 2).reshape((near, na) + values.shape[3:])

    sent_counts = lax.dynamic_index_in_dim(send_counts, device, 0, keepdims=False)
    used = jnp.arange(capacity, dtype=jnp.int32)[None, :] < sent_counts[:, None]
    slots = jnp.tile(by_near(jnp.where(used, dest_slots[0], targets)), (1, 1, lanes))
    own_lanes = jnp.arange(targets, dtype=jnp.int32) // capacity == near_at % lanes
    slots = jnp.where(own_lanes, slots, 0).astype(bf16)
    rows = pick(features, by_near(sample_ids[0]).reshape(-1))
    grad_t = lax.dynamic_slice_in_dim(out_grad.T, feat * part, part, 0)
    terms = jnp.einsum("kt,ntb->nkb", grad_t, tiles, preferred_element_type=f32).astype(bf16)
    there = block_near[None, :] == jnp.arange(near, dtype=jnp.int32)[:, None]
    terms = jnp.where(there[:, :, None, None], terms[None], jnp.zeros((), bf16))
    term_far = jnp.broadcast_to(block_far[:, None], (count, targets)).astype(bf16)
    sent = [
        rows.reshape(near, na * capacity, width),
        slots,
        terms.reshape(near, count * part, targets),
        to_all(jnp.pad(term_far, ((0, 8 - count), (0, 0))), near),
    ]
    got = exchange(jnp.concatenate(sent, axis=1), "node", near_groups)

    ends = [na * capacity, na * capacity + na, na * capacity + na + count * part]
    rows = got[:, : ends[0]].reshape(near, na, capacity, width).transpose(1, 0, 2, 3)
    rows = rows.reshape(na, near * capacity, width)
    slots = got[:, ends[0] : ends[1]].astype(f32).reshape(near // lanes, lanes, na, targets)
    slots = jnp.sum(slots, axis=1).astype(jnp.int32).transpose(1, 0, 2)
    target_ids = jnp.arange(targets, dtype=jnp.int32)
    chosen = slots.reshape(na, 1, near * capacity) == target_ids[None, :, None]
    degree = jnp.sum(chosen.astype(f32), axis=2).astype(bf16)
    summed = jnp.einsum("atr,ars->ats", chosen.astype(bf16), rows, preferred_element_type=f32)
    terms = got[:, ends[1] : ends[2]].reshape(near * count, part, targets).astype(f32)
    term_far = got[:, ends[2] : ends[2] + count].reshape(near * count, 1, targets).astype(jnp.int32)
    far_ids = jnp.arange(na, dtype=jnp.int32)[:, None, None]
    terms = sum(
        jnp.where(term_far[n][None] == far_ids, terms[n][None], 0.0) for n in range(near * count)
    ).astype(bf16)
    sent = [summed.astype(bf16), terms, jnp.pad(degree[:, None, :], ((0, 0), (0, 7), (0, 0)))]
    came = exchange(jnp.concatenate(sent, axis=1), "node", far_groups).astype(f32)
    summed = jnp.sum(came[:, :targets], axis=0)
    back_high, back_low = split(jnp.sum(came[:, targets : targets + part], axis=0))
    degree = jnp.sum(came[:, targets + part], axis=0)

    self_rows = pick(features, self_ids[0])
    mean = summed / (degree + 1.0)[:, None]
    mean_high, mean_low = split(mean)
    terms_one = (
        dot(self_one, self_rows, ((0,), (1,)))
        + dot(neighbour_one, mean_high, ((0,), (1,)))
        + dot(neighbour_one, mean_low, ((0,), (1,)))
    )
    high, low = split(terms_one.reshape(feats, part, targets))
    sent = [high, low, to_all(back_high, feats), to_all(back_low, feats)]
    got = exchange(jnp.concatenate(sent, axis=1), "feat")
    pre_one = jnp.sum(got[:, :part].astype(f32) + got[:, part : 2 * part].astype(f32), axis=0)
    back_high = got[:, 2 * part : 3 * part].reshape(hidden, targets)
    back_low = got[:, 3 * part :].reshape(hidden, targets)
    sigma = jax.nn.sigmoid(pre_one)
    hidden_part = (pre_one * sigma).astype(bf16)
    slope = sigma * (1.0 + pre_one * (1.0 - sigma))

    self_two_part = lax.dynamic_slice_in_dim(self_two, feat * part, part, 0)
    neighbour_two_part = lax.dynamic_slice_in_dim(neighbour_two, feat * part, part, 0)
    pre_grad = (
        dot(self_two_part, out_grad, ((1,), (1,)))
        + dot(neighbour_two_part, back_high, ((1,), (0,)))
        + dot(neighbour_two_part, back_low, ((1,), (0,)))
    ) * slope
    full = exchange(
        to_all(jnp.concatenate([pre_grad.astype(bf16), hidden_part], axis=0), feats), "feat"
    )
    pre_round = full[:, :part].reshape(hidden, targets)
    hidden_t = full[:, part:].reshape(hidden, targets)

    half = hidden // 2
    upper = quarters(
        dot(hidden_part, out_grad, ((1,), (0,))),
        dot(hidden_part, back_high, ((1,), (1,))) + dot(hidden_part, back_low, ((1,), (1,))),
    )
    lower = quarters(
        dot(self_rows, pre_round, ((0,), (1,))), dot(mean_high, pre_round, ((0,), (1,)))
    )
    share = upper.shape[0] // near
    rows_each = lower.shape[0] // near
    sent = [lower.reshape(near, rows_each, half), upper.reshape(near, share, half)]
    got = exchange(jnp.concatenate(sent, axis=1), "node", near_groups).astype(f32)
    sent = [jnp.sum(got, axis=0).astype(bf16), hidden_part]
    got = exchange(to_all(jnp.concatenate(sent, axis=0), na), "node", far_groups)
    sums = jnp.sum(got[:, : rows_each + share].astype(f32), axis=0).astype(bf16)
    sent = [sums, got[:, rows_each + share :].reshape(na * part, targets)]
    got = exchange(to_all(jnp.concatenate(sent, axis=0), near), "node", near_groups)
    lower = got[:, :rows_each].reshape(4, width, half).astype(f32)
    upper = got[:, rows_each : rows_each + share].reshape(near * share, half)
    all_hidden = got[:, rows_each + share :].reshape(near * na, part, targets)

    places = block_near * na + block_far
    agg_part = sum(
        dot(lax.dynamic_index_in_dim(all_hidden, places[n], 0, keepdims=False), tiles[n], ((1,), (1,)))
        for n in range(tiles.shape[0])
    ).astype(bf16)
    got = exchange(to_all(jnp.concatenate([agg_part, upper], axis=0), feats), "feat")
    agg_t = got[:, :part].reshape(hidden, targets)
    layer_output = (
        dot(hidden_t, self_two, ((0,), (0,))) + dot(agg_t, neighbour_two, ((0,), (0,)))
    ).astype(bf16)
    upper = got[:, part:].reshape(feats, 4, part, half).astype(f32)
    upper = upper.transpose(1, 0, 2, 3).reshape(4, hidden, half)

    def halves(stack, which):
        return jnp.concatenate([stack[2 * which], stack[2 * which + 1]], axis=1)

    return (layer_output, halves(lower, 0), halves(lower, 1), halves(upper, 0), halves(upper, 1))


def solution(mesh):
    placed = (
        P("node", "feat"),
        P("feat", None),
        P("feat", None),
        P("node", None, None),
        P("node", None, None),
        P(),
        P("node", None),
        P("node", None),
        P("node", None, None, None),
        P(),
        P(),
        P("node", None),
    )
    return jax.shard_map(
        shards,
        mesh=mesh,
        in_specs=placed,
        out_specs=(P("node", None), P("feat", None), P("feat", None), P(), P()),
        check_vma=False,
    )
```

```python
import functools

import jax
import jax.numpy as jnp
from jax import lax
from jax.experimental import pallas as pl
from jax.experimental.pallas import tpu as pltpu
from jax.sharding import PartitionSpec as P

bf16 = jnp.bfloat16
f32 = jnp.float32


def dot(a, b, dims):
    return lax.dot_general(a, b, (dims, ((), ())), preferred_element_type=f32)


def exchange(values, axis, groups=None):
    return lax.all_to_all(
        values, axis, split_axis=0, concat_axis=0, tiled=True, axis_index_groups=groups
    )


def to_all(values, count):
    return jnp.broadcast_to(values[None], (count,) + values.shape)


def pick(table, row_ids):
    local_ids = jnp.arange(table.shape[0], dtype=jnp.int32)
    chosen = (row_ids[:, None] == local_ids[None, :]).astype(table.dtype)
    return dot(chosen, table, ((1,), (0,))).astype(table.dtype)


def split(values):
    high = lax.reduce_precision(values, 8, 7)
    return high.astype(bf16), (values - high).astype(bf16)


def quarters(first, second):
    half = first.shape[1] // 2
    parts = [first[:, :half], first[:, half:], second[:, :half], second[:, half:]]
    return jnp.concatenate(parts, axis=0).astype(bf16)


def where_am_i():
    return lax.axis_index("node"), lax.axis_index("feat")


def pack_kernel(
    ids_ref,
    slots_ref,
    counts_ref,
    blocks_ref,
    features_ref,
    tiles_ref,
    grad_ref,
    sent_ref,
    slots_scratch,
    grad_scratch,
    *,
    nx,
    na,
    nb,
    place,
):
    device, feat = place()
    near = nx * nb
    capacity, nodes = ids_ref.shape
    locals_, width = features_ref.shape
    count, targets, _ = tiles_ref.shape
    part = sent_ref.shape[1] - na * capacity - na - 8
    part = part // count
    lanes = targets // capacity
    near_at = (device // (na * nb)) * nb + device % nb

    used = lax.broadcasted_iota(jnp.int32, (capacity, nodes), 0) < counts_ref[pl.ds(device, 1), :]
    slots = jnp.where(used, slots_ref[...], targets).astype(f32)
    slots = jnp.concatenate([slots] * lanes, axis=0)
    slots = jnp.concatenate([slots, jnp.zeros((targets, targets - nodes), f32)], axis=1).T
    group = lax.broadcasted_iota(jnp.int32, (targets, targets), 1) // capacity
    slots_scratch[...] = jnp.where(group == near_at % lanes, slots, 0.0)
    grad_scratch[...] = grad_ref[...].astype(f32).T
    grad_t = grad_scratch[pl.ds(pl.multiple_of(feat * part, part), part), :].astype(bf16)
    terms = [dot(grad_t, tiles_ref[k], ((1,), (0,))) for k in range(count)]
    blocks = [blocks_ref[0, k] for k in range(count)]
    row = lax.broadcasted_iota(jnp.int32, (8, targets), 0)
    far_rows = jnp.zeros((8, targets), jnp.int32)
    for k in range(count):
        far_rows = jnp.where(row == k, blocks[k] % (na * nb) // nb, far_rows)
    far_rows = far_rows.astype(f32)
    local_ids = lax.broadcasted_iota(jnp.int32, (capacity, locals_), 1)
    for x in range(nx):
        for b in range(nb):
            to = x * nb + b
            owners = [(x * na + a) * nb + b for a in range(na)]
            chosen = jnp.concatenate(
                [jnp.where(ids_ref[:, o : o + 1] == local_ids, 1.0, 0.0).astype(bf16) for o in owners],
                axis=0,
            )
            rows = dot(chosen, features_ref[...], ((1,), (0,)))
            sent_ref[to, : na * capacity, :] = rows.astype(bf16)
            at = na * capacity
            for k in range(count):
                there = blocks[k] // (na * nb) * nb + blocks[k] % nb == to
                term = jnp.where(there, terms[k], 0.0)
                sent_ref[to, at : at + part, :] = term.astype(bf16)
                at += part
            slot_rows = slots_scratch[pl.ds(owners[0], na, stride=nb), :]
            sent_ref[to, at : at + na + 8, :] = jnp.concatenate([slot_rows, far_rows], 0).astype(bf16)


def pack(sample_ids, dest_slots, counts, blocks, features, tiles, grad, nx, na, nb, part, place):
    count, targets, _ = tiles.shape
    capacity, nodes = sample_ids.shape
    total = na * capacity + count * part + na + 8
    kernel = functools.partial(pack_kernel, nx=nx, na=na, nb=nb, place=place)
    vmem = pl.BlockSpec(memory_space=pltpu.VMEM)
    return pl.pallas_call(
        kernel,
        out_shape=jax.ShapeDtypeStruct((nx * nb, total, features.shape[1]), bf16),
        in_specs=[vmem] * 3 + [pl.BlockSpec(memory_space=pltpu.SMEM)] + [vmem] * 3,
        out_specs=vmem,
        scratch_shapes=[
            pltpu.VMEM((targets, targets), f32),
            pltpu.VMEM((grad.shape[1], targets), f32),
        ],
        compiler_params=pltpu.CompilerParams(vmem_limit_bytes=24 * 1024 * 1024),
    )(sample_ids, dest_slots, counts, blocks, features, tiles, grad)


def shards(
    features,
    self_one,
    neighbour_one,
    sample_ids,
    dest_slots,
    send_counts,
    self_ids,
    tile_blocks,
    tile_weights,
    self_two,
    neighbour_two,
    out_grad,
):
    feats = lax.axis_size("feat")
    nodes = lax.axis_size("node")
    nx, nb = 4, 2
    na = nodes // (nx * nb)
    near = nx * nb
    near_ids = [(x * na + a) * nb + b for a in range(na) for x in range(nx) for b in range(nb)]
    near_groups = [near_ids[a * near : (a + 1) * near] for a in range(na)]
    far_groups = [list(group) for group in zip(*near_groups)]
    feat = lax.axis_index("feat")
    capacity = sample_ids.shape[2]
    targets = self_ids.shape[1]
    width = features.shape[1]
    hidden = neighbour_one.shape[1]
    part = hidden // feats
    block_ids = tile_blocks[0]
    block_near = block_ids // (na * nb) * nb + block_ids % nb
    block_far = block_ids % (na * nb) // nb
    tiles = tile_weights[0]
    count = tiles.shape[0]
    lanes = targets // capacity

    sent = pack(
        sample_ids[0].T,
        dest_slots[0].T,
        send_counts,
        tile_blocks,
        features,
        tiles,
        out_grad,
        nx,
        na,
        nb,
        part,
        where_am_i,
    )
    got = exchange(sent, "node", near_groups)

    ends = [na * capacity, na * capacity + count * part, na * capacity + count * part + na]
    rows = got[:, : ends[0]].reshape(near, na, capacity, width).transpose(1, 0, 2, 3)
    rows = rows.reshape(na, near * capacity, width)
    slots = got[:, ends[1] : ends[2]].astype(f32).reshape(near // lanes, lanes, na, targets)
    slots = jnp.sum(slots, axis=1).astype(jnp.int32).transpose(1, 0, 2)
    target_ids = jnp.arange(targets, dtype=jnp.int32)
    chosen = slots.reshape(na, 1, near * capacity) == target_ids[None, :, None]
    degree = jnp.sum(chosen.astype(f32), axis=2).astype(bf16)
    summed = jnp.einsum("atr,ars->ats", chosen.astype(bf16), rows, preferred_element_type=f32)
    terms = got[:, ends[0] : ends[1]].reshape(near * count, part, targets).astype(f32)
    term_far = got[:, ends[2] : ends[2] + count].reshape(near * count, 1, targets).astype(jnp.int32)
    far_ids = jnp.arange(na, dtype=jnp.int32)[:, None, None]
    terms = sum(
        jnp.where(term_far[n][None] == far_ids, terms[n][None], 0.0) for n in range(near * count)
    ).astype(bf16)
    sent = [summed.astype(bf16), terms, jnp.pad(degree[:, None, :], ((0, 0), (0, 7), (0, 0)))]
    came = exchange(jnp.concatenate(sent, axis=1), "node", far_groups).astype(f32)
    summed = jnp.sum(came[:, :targets], axis=0)
    back_high, back_low = split(jnp.sum(came[:, targets : targets + part], axis=0))
    degree = jnp.sum(came[:, targets + part], axis=0)

    self_rows = pick(features, self_ids[0])
    mean = summed / (degree + 1.0)[:, None]
    mean_high, mean_low = split(mean)
    terms_one = (
        dot(self_one, self_rows, ((0,), (1,)))
        + dot(neighbour_one, mean_high, ((0,), (1,)))
        + dot(neighbour_one, mean_low, ((0,), (1,)))
    )
    high, low = split(terms_one.reshape(feats, part, targets))
    sent = [high, low, to_all(back_high, feats), to_all(back_low, feats)]
    got = exchange(jnp.concatenate(sent, axis=1), "feat")
    pre_one = jnp.sum(got[:, :part].astype(f32) + got[:, part : 2 * part].astype(f32), axis=0)
    back_high = got[:, 2 * part : 3 * part].reshape(hidden, targets)
    back_low = got[:, 3 * part :].reshape(hidden, targets)
    sigma = jax.nn.sigmoid(pre_one)
    hidden_part = (pre_one * sigma).astype(bf16)
    slope = sigma * (1.0 + pre_one * (1.0 - sigma))

    self_two_part = lax.dynamic_slice_in_dim(self_two, feat * part, part, 0)
    neighbour_two_part = lax.dynamic_slice_in_dim(neighbour_two, feat * part, part, 0)
    pre_grad = (
        dot(self_two_part, out_grad, ((1,), (1,)))
        + dot(neighbour_two_part, back_high, ((1,), (0,)))
        + dot(neighbour_two_part, back_low, ((1,), (0,)))
    ) * slope
    full = exchange(
        to_all(jnp.concatenate([pre_grad.astype(bf16), hidden_part], axis=0), feats), "feat"
    )
    pre_round = full[:, :part].reshape(hidden, targets)
    hidden_t = full[:, part:].reshape(hidden, targets)

    half = hidden // 2
    upper = quarters(
        dot(hidden_part, out_grad, ((1,), (0,))),
        dot(hidden_part, back_high, ((1,), (1,))) + dot(hidden_part, back_low, ((1,), (1,))),
    )
    lower = quarters(
        dot(self_rows, pre_round, ((0,), (1,))), dot(mean_high, pre_round, ((0,), (1,)))
    )
    share = upper.shape[0] // near
    rows_each = lower.shape[0] // near
    sent = [lower.reshape(near, rows_each, half), upper.reshape(near, share, half)]
    got = exchange(jnp.concatenate(sent, axis=1), "node", near_groups).astype(f32)
    sent = [jnp.sum(got, axis=0).astype(bf16), hidden_part]
    got = exchange(to_all(jnp.concatenate(sent, axis=0), na), "node", far_groups)
    sums = jnp.sum(got[:, : rows_each + share].astype(f32), axis=0).astype(bf16)
    sent = [sums, got[:, rows_each + share :].reshape(na * part, targets)]
    got = exchange(to_all(jnp.concatenate(sent, axis=0), near), "node", near_groups)
    lower = got[:, :rows_each].reshape(4, width, half).astype(f32)
    upper = got[:, rows_each : rows_each + share].reshape(near * share, half)
    all_hidden = got[:, rows_each + share :].reshape(near * na, part, targets)

    places = block_near * na + block_far
    agg_part = sum(
        dot(lax.dynamic_index_in_dim(all_hidden, places[n], 0, keepdims=False), tiles[n], ((1,), (1,)))
        for n in range(tiles.shape[0])
    ).astype(bf16)
    got = exchange(to_all(jnp.concatenate([agg_part, upper], axis=0), feats), "feat")
    agg_t = got[:, :part].reshape(hidden, targets)
    layer_output = (
        dot(hidden_t, self_two, ((0,), (0,))) + dot(agg_t, neighbour_two, ((0,), (0,)))
    ).astype(bf16)
    upper = got[:, part:].reshape(feats, 4, part, half).astype(f32)
    upper = upper.transpose(1, 0, 2, 3).reshape(4, hidden, half)

    def halves(stack, which):
        return jnp.concatenate([stack[2 * which], stack[2 * which + 1]], axis=1)

    return (layer_output, halves(lower, 0), halves(lower, 1), halves(upper, 0), halves(upper, 1))


def solution(mesh):
    placed = (
        P("node", "feat"),
        P("feat", None),
        P("feat", None),
        P("node", None, None),
        P("node", None, None),
        P(),
        P("node", None),
        P("node", None),
        P("node", None, None, None),
        P(),
        P(),
        P("node", None),
    )
    return jax.shard_map(
        shards,
        mesh=mesh,
        in_specs=placed,
        out_specs=(P("node", None), P("feat", None), P("feat", None), P(), P()),
        check_vma=False,
    )
```

```python
import functools

import jax
import jax.numpy as jnp
from jax import lax
from jax.experimental import pallas as pl
from jax.experimental.pallas import tpu as pltpu
from jax.sharding import PartitionSpec as P

bf16 = jnp.bfloat16
f32 = jnp.float32
VMEM_LIMIT = 16 * 1024 * 1024


def dot(a, b, dims):
    return lax.dot_general(a, b, (dims, ((), ())), preferred_element_type=f32)


def exchange(values, axis, groups=None):
    return lax.all_to_all(
        values, axis, split_axis=0, concat_axis=0, tiled=True, axis_index_groups=groups
    )


def to_all(values, count):
    return jnp.broadcast_to(values[None], (count,) + values.shape)


def pick(table, row_ids):
    local_ids = jnp.arange(table.shape[0], dtype=jnp.int32)
    chosen = (row_ids[:, None] == local_ids[None, :]).astype(table.dtype)
    return dot(chosen, table, ((1,), (0,))).astype(table.dtype)


def quarters(first, second):
    half = first.shape[1] // 2
    parts = [first[:, :half], first[:, half:], second[:, :half], second[:, half:]]
    return jnp.concatenate(parts, axis=0).astype(bf16)


def near_index(device, na, nb):
    return device // (na * nb) * nb + device % nb


def where_am_i():
    return lax.axis_index("node"), lax.axis_index("feat")


def pack_kernel(
    ids_hbm,
    slots_hbm,
    counts_hbm,
    blocks_hbm,
    features_hbm,
    tiles_hbm,
    grad_hbm,
    sent_ref,
    ids_ref,
    slots_ref,
    counts_ref,
    blocks_ref,
    features_ref,
    tiles_ref,
    grad_ref,
    slots_scratch,
    grad_scratch,
    sems,
    *,
    nx,
    na,
    nb,
    place,
):
    copies = [
        pltpu.make_async_copy(source, target, sems.at[n])
        for n, (source, target) in enumerate(
            [
                (ids_hbm, ids_ref),
                (slots_hbm, slots_ref),
                (counts_hbm, counts_ref),
                (blocks_hbm, blocks_ref),
                (features_hbm, features_ref),
                (tiles_hbm, tiles_ref),
                (grad_hbm, grad_ref),
            ]
        )
    ]
    for copy in copies:
        copy.start()
    for copy in copies:
        copy.wait()
    device, feat = place()
    near = nx * nb
    capacity, nodes = ids_ref.shape
    locals_, width = features_ref.shape
    count, targets, _ = tiles_ref.shape
    part = sent_ref.shape[1] - na * capacity - na - 8
    part = part // count
    lanes = targets // capacity
    near_at = near_index(device, na, nb)

    used = lax.broadcasted_iota(jnp.int32, (capacity, nodes), 0) < counts_ref[pl.ds(device, 1), :]
    slots = jnp.where(used, slots_ref[...], targets).astype(f32)
    slots = jnp.concatenate([slots] * lanes, axis=0)
    slots = jnp.concatenate([slots, jnp.zeros((targets, targets - nodes), f32)], axis=1).T
    group = lax.broadcasted_iota(jnp.int32, (targets, targets), 1) // capacity
    slots_scratch[...] = jnp.where(group == near_at % lanes, slots, 0.0)
    grad_scratch[...] = grad_ref[...].astype(f32).T
    grad_t = grad_scratch[pl.ds(pl.multiple_of(feat * part, part), part), :].astype(bf16)
    terms = [dot(grad_t, tiles_ref[k], ((1,), (0,))) for k in range(count)]
    blocks = [blocks_ref[0, k] for k in range(count)]
    row = lax.broadcasted_iota(jnp.int32, (8, targets), 0)
    far_rows = jnp.zeros((8, targets), jnp.int32)
    for k in range(count):
        far_rows = jnp.where(row == k, blocks[k] % (na * nb) // nb, far_rows)
        far_rows = jnp.where(row == count + k, blocks[k] // (na * nb) * nb + blocks[k] % nb, far_rows)
    far_rows = far_rows.astype(f32)
    local_ids = lax.broadcasted_iota(jnp.int32, (capacity, locals_), 1)
    for x in range(nx):
        for b in range(nb):
            to = x * nb + b
            owners = [(x * na + a) * nb + b for a in range(na)]
            chosen = jnp.concatenate(
                [jnp.where(ids_ref[:, o : o + 1] == local_ids, 1.0, 0.0).astype(bf16) for o in owners],
                axis=0,
            )
            rows = dot(chosen, features_ref[...], ((1,), (0,)))
            sent_ref[to, : na * capacity, :] = rows.astype(bf16)
            at = na * capacity
            for k in range(count):
                there = blocks[k] // (na * nb) * nb + blocks[k] % nb == to
                term = jnp.where(there, terms[k], 0.0)
                sent_ref[to, at : at + part, :] = term.astype(bf16)
                at += part
            slot_rows = slots_scratch[pl.ds(owners[0], na, stride=nb), :]
            sent_ref[to, at : at + na + 8, :] = jnp.concatenate([slot_rows, far_rows], 0).astype(bf16)


def pack(sample_ids, dest_slots, counts, blocks, features, tiles, grad, nx, na, nb, part, place):
    count, targets, _ = tiles.shape
    capacity, nodes = sample_ids.shape
    total = na * capacity + count * part + na + 8
    kernel = functools.partial(pack_kernel, nx=nx, na=na, nb=nb, place=place)
    args = (sample_ids, dest_slots, counts, blocks, features, tiles, grad)
    held = [pltpu.VMEM(arg.shape, arg.dtype) for arg in args]
    held[3] = pltpu.SMEM(blocks.shape, blocks.dtype)
    return pl.pallas_call(
        kernel,
        out_shape=jax.ShapeDtypeStruct((nx * nb, total, features.shape[1]), bf16),
        in_specs=[pl.BlockSpec(memory_space=pltpu.HBM)] * len(args),
        out_specs=pl.BlockSpec(memory_space=pltpu.VMEM),
        scratch_shapes=held
        + [
            pltpu.VMEM((targets, targets), f32),
            pltpu.VMEM((grad.shape[1], targets), f32),
            pltpu.SemaphoreType.DMA((len(args),)),
        ],
        compiler_params=pltpu.CompilerParams(vmem_limit_bytes=VMEM_LIMIT),
    )(*args)


def in_vmem(kernel, out_shape, *args):
    vmem = pl.BlockSpec(memory_space=pltpu.VMEM)
    many = isinstance(out_shape, (list, tuple))
    return pl.pallas_call(
        kernel,
        out_shape=out_shape,
        in_specs=[vmem] * len(args),
        out_specs=[vmem] * len(out_shape) if many else vmem,
        compiler_params=pltpu.CompilerParams(vmem_limit_bytes=VMEM_LIMIT),
    )(*args)


def halve(values):
    high = values.astype(bf16)
    return high, (values - high.astype(f32)).astype(bf16)


def gather_kernel(got_ref, sent_ref, *, capacity, part, count):
    near = got_ref.shape[0]
    far, _, targets = sent_ref.shape
    lanes = targets // capacity
    at = far * capacity + count * part
    marks = [got_ref[n, at : at + far + 8, :].astype(f32) for n in range(near)]
    slots = [sum(marks[h : h + lanes])[:far] for h in range(0, near, lanes)]
    nodes = lax.broadcasted_iota(jnp.int32, (targets, targets), 0).astype(f32)
    ones = jnp.ones((8, targets), bf16)
    back = [jnp.zeros((part, targets), f32) for _ in range(far)]
    for n in range(near):
        for k in range(count):
            start = far * capacity + k * part
            term = got_ref[n, start : start + part, :].astype(f32)
            mark = jnp.broadcast_to(marks[n][far + k : far + k + 1, :], (part, targets))
            back = [back[a] + jnp.where(mark == float(a), term, 0.0) for a in range(far)]
    for a in range(far):
        total = jnp.zeros((targets, targets), f32)
        degree = jnp.zeros((8, targets), f32)
        for h in range(near // lanes):
            chosen = jnp.where(slots[h][a : a + 1, :] == nodes, 1.0, 0.0).astype(bf16)
            rows = [
                got_ref[h * lanes + n, a * capacity : (a + 1) * capacity, :] for n in range(lanes)
            ]
            total += dot(chosen, jnp.concatenate(rows, axis=0), ((1,), (0,)))
            degree += dot(ones, chosen, ((1,), (1,)))
        sent_ref[a] = jnp.concatenate([total, back[a], degree], axis=0).astype(bf16)


def first_kernel(came_ref, rows_ref, self_ref, other_ref, sent_ref, mean_ref, *, part):
    targets = rows_ref.shape[0]
    came = came_ref[0].astype(f32)
    for a in range(1, came_ref.shape[0]):
        came += came_ref[a].astype(f32)
    degree = jnp.broadcast_to(came[targets + part : targets + part + 1, :], (targets, targets)).T
    high, low = halve(came[:targets] / (degree + 1.0))
    mean_ref[...] = high
    pre = dot(rows_ref[...], self_ref[...], ((1,), (0,)))
    pre += dot(high, other_ref[...], ((1,), (0,)))
    pre += dot(low, other_ref[...], ((1,), (0,)))
    pre_high, pre_low = halve(pre.T)
    back = jnp.concatenate(halve(came[targets : targets + part]), axis=0)
    for f in range(sent_ref.shape[0]):
        mine = slice(f * part, (f + 1) * part)
        sent_ref[f] = jnp.concatenate([pre_high[mine], pre_low[mine], back], axis=0)


def hidden_kernel(got_ref, self_ref, other_ref, grad_ref, sent_ref, *, part):
    feats = got_ref.shape[0]
    pre = jnp.zeros((part, got_ref.shape[2]), f32)
    for f in range(feats):
        pre += got_ref[f, :part, :].astype(f32) + got_ref[f, part : 2 * part, :].astype(f32)
    sigma = 1.0 / (1.0 + jnp.exp(-pre))
    slope = sigma * (1.0 + pre * (1.0 - sigma))
    back_high = jnp.concatenate([got_ref[f, 2 * part : 3 * part, :] for f in range(feats)], axis=0)
    back_low = jnp.concatenate([got_ref[f, 3 * part :, :] for f in range(feats)], axis=0)
    grad = dot(self_ref[...], grad_ref[...], ((1,), (1,)))
    grad += dot(other_ref[...], back_high, ((1,), (0,)))
    grad += dot(other_ref[...], back_low, ((1,), (0,)))
    both = jnp.concatenate([grad * slope, pre * sigma], axis=0).astype(bf16)
    for f in range(feats):
        sent_ref[f] = both


def near_kernel(got_ref, marks_ref, sent_ref, *, sums, part, count, where):
    far = got_ref.shape[0]
    total = got_ref[0, :sums, :].astype(f32)
    for a in range(1, far):
        total += got_ref[a, :sums, :].astype(f32)
    total = total.astype(bf16)
    here = where().astype(f32)
    blocks = [got_ref[a, sums:, :].astype(f32) for a in range(far)]
    for n in range(sent_ref.shape[0]):
        sent_ref[n, :sums, :] = total
        marks = marks_ref[n].astype(f32)
        for k in range(count):
            mark = jnp.where(marks[far + count + k :][:1] == here, marks[far + k :][:1], -1.0)
            mark = jnp.broadcast_to(mark, blocks[0].shape)
            block = jnp.zeros_like(blocks[0])
            for a in range(far):
                block = jnp.where(mark == float(a), blocks[a], block)
            at = sums + k * part
            sent_ref[n, at : at + part, :] = block.astype(bf16)


def second_kernel(got_ref, tiles_ref, sent_ref, *, rows_each, share, part):
    near = got_ref.shape[0]
    agg = jnp.zeros((part, tiles_ref.shape[1]), f32)
    for k in range(tiles_ref.shape[0]):
        at = rows_each + share + k * part
        block = got_ref[0, at : at + part, :].astype(f32)
        for n in range(1, near):
            block += got_ref[n, at : at + part, :].astype(f32)
        agg += dot(block.astype(bf16), tiles_ref[k], ((1,), (1,)))
    rows = [got_ref[n, rows_each : rows_each + share, :] for n in range(near)]
    both = jnp.concatenate([agg.astype(bf16)] + rows, axis=0)
    for f in range(sent_ref.shape[0]):
        sent_ref[f] = both


def last_kernel(got_ref, hidden_ref, self_ref, other_ref, out_ref, first_ref, second_ref, *, part):
    feats = got_ref.shape[0]
    half = first_ref.shape[1] // 2
    agg = jnp.concatenate([got_ref[f, :part, :] for f in range(feats)], axis=0)
    out = dot(hidden_ref[...], self_ref[...], ((0,), (0,))) + dot(agg, other_ref[...], ((0,), (0,)))
    out_ref[...] = out.astype(bf16)
    for f in range(feats):
        at = f * part
        for n, ref in enumerate([first_ref, second_ref]):
            start = part * (1 + 2 * n)
            ref[at : at + part, :half] = got_ref[f, start : start + part, :].astype(f32)
            ref[at : at + part, half:] = got_ref[f, start + part : start + 2 * part, :].astype(f32)


def shards(
    features,
    self_one,
    neighbour_one,
    sample_ids,
    dest_slots,
    send_counts,
    self_ids,
    tile_blocks,
    tile_weights,
    self_two,
    neighbour_two,
    out_grad,
):
    feats = lax.axis_size("feat")
    nodes = lax.axis_size("node")
    nx, nb = 4, 2
    na = nodes // (nx * nb)
    near = nx * nb
    near_ids = [(x * na + a) * nb + b for a in range(na) for x in range(nx) for b in range(nb)]
    near_groups = [near_ids[a * near : (a + 1) * near] for a in range(na)]
    far_groups = [list(group) for group in zip(*near_groups)]
    feat = lax.axis_index("feat")
    capacity = sample_ids.shape[2]
    targets = self_ids.shape[1]
    width = features.shape[1]
    hidden = neighbour_one.shape[1]
    part = hidden // feats
    tiles = tile_weights[0]
    count = tiles.shape[0]

    sent = pack(
        sample_ids[0].T,
        dest_slots[0].T,
        send_counts,
        tile_blocks,
        features,
        tiles,
        out_grad,
        nx,
        na,
        nb,
        part,
        where_am_i,
    )
    got = exchange(sent, "node", near_groups)

    marks = got[:, na * capacity + count * part :]
    sent = in_vmem(
        functools.partial(gather_kernel, capacity=capacity, part=part, count=count),
        jax.ShapeDtypeStruct((na, targets + part + 8, width), bf16),
        got,
    )
    came = exchange(sent, "node", far_groups)

    self_rows = pick(features, self_ids[0])
    sent, mean_high = in_vmem(
        functools.partial(first_kernel, part=part),
        [
            jax.ShapeDtypeStruct((feats, 4 * part, targets), bf16),
            jax.ShapeDtypeStruct((targets, width), bf16),
        ],
        came,
        self_rows,
        self_one,
        neighbour_one,
    )
    got = exchange(sent, "feat")
    back_high = got[:, 2 * part : 3 * part].reshape(hidden, targets)
    back_low = got[:, 3 * part :].reshape(hidden, targets)

    self_two_part = lax.dynamic_slice_in_dim(self_two, feat * part, part, 0)
    neighbour_two_part = lax.dynamic_slice_in_dim(neighbour_two, feat * part, part, 0)
    sent = in_vmem(
        functools.partial(hidden_kernel, part=part),
        jax.ShapeDtypeStruct((feats, 2 * part, targets), bf16),
        got,
        self_two_part,
        neighbour_two_part,
        out_grad,
    )
    hidden_part = sent[0, part:]
    full = exchange(sent, "feat")
    pre_round = full[:, :part].reshape(hidden, targets)
    hidden_t = full[:, part:].reshape(hidden, targets)

    half = hidden // 2
    upper = quarters(
        dot(hidden_part, out_grad, ((1,), (0,))),
        dot(hidden_part, back_high, ((1,), (1,))) + dot(hidden_part, back_low, ((1,), (1,))),
    )
    lower = quarters(
        dot(self_rows, pre_round, ((0,), (1,))), dot(mean_high, pre_round, ((0,), (1,)))
    )
    share = upper.shape[0] // near
    rows_each = lower.shape[0] // near
    sent = [lower.reshape(near, rows_each, half), upper.reshape(near, share, half)]
    got = exchange(jnp.concatenate(sent, axis=1), "node", near_groups).astype(f32)
    sent = [jnp.sum(got, axis=0).astype(bf16), hidden_part]
    got = exchange(to_all(jnp.concatenate(sent, axis=0), na), "node", far_groups)
    sums = rows_each + share
    sent = in_vmem(
        functools.partial(
            near_kernel,
            sums=sums,
            part=part,
            count=count,
            where=lambda: near_index(lax.axis_index("node"), na, nb),
        ),
        jax.ShapeDtypeStruct((near, sums + count * part, half), bf16),
        got,
        marks,
    )
    got = exchange(sent, "node", near_groups)
    lower = got[:, :rows_each].reshape(4, width, half).astype(f32)

    sent = in_vmem(
        functools.partial(second_kernel, rows_each=rows_each, share=share, part=part),
        jax.ShapeDtypeStruct((feats, part + near * share, targets), bf16),
        got,
        tiles,
    )
    got = exchange(sent, "feat")
    layer_output, upper_self, upper_others = in_vmem(
        functools.partial(last_kernel, part=part),
        [
            jax.ShapeDtypeStruct((targets, hidden), bf16),
            jax.ShapeDtypeStruct((hidden, hidden), f32),
            jax.ShapeDtypeStruct((hidden, hidden), f32),
        ],
        got,
        hidden_t,
        self_two,
        neighbour_two,
    )

    def halves(which):
        return jnp.concatenate([lower[2 * which], lower[2 * which + 1]], axis=1)

    return (layer_output, halves(0), halves(1), upper_self, upper_others)


def solution(mesh):
    placed = (
        P("node", "feat"),
        P("feat", None),
        P("feat", None),
        P("node", None, None),
        P("node", None, None),
        P(),
        P("node", None),
        P("node", None),
        P("node", None, None, None),
        P(),
        P(),
        P("node", None),
    )
    return jax.shard_map(
        shards,
        mesh=mesh,
        in_specs=placed,
        out_specs=(P("node", None), P("feat", None), P("feat", None), P(), P()),
        check_vma=False,
    )
```

```python
import functools

import jax
import jax.numpy as jnp
from jax import lax
from jax.experimental import pallas as pl
from jax.experimental.pallas import tpu as pltpu
from jax.sharding import PartitionSpec as P

bf16 = jnp.bfloat16
f32 = jnp.float32
VMEM_LIMIT = 16 * 1024 * 1024
PACK_LIMIT = 60 * 1024 * 1024


def dot(a, b, dims):
    return lax.dot_general(a, b, (dims, ((), ())), preferred_element_type=f32)


def exchange(values, axis, groups=None):
    return lax.all_to_all(
        values, axis, split_axis=0, concat_axis=0, tiled=True, axis_index_groups=groups
    )


def pick(table, row_ids):
    local_ids = jnp.arange(table.shape[0], dtype=jnp.int32)
    chosen = (row_ids[:, None] == local_ids[None, :]).astype(table.dtype)
    return dot(chosen, table, ((1,), (0,))).astype(table.dtype)


def quarters(first, second):
    half = first.shape[1] // 2
    parts = [first[:, :half], first[:, half:], second[:, :half], second[:, half:]]
    return jnp.concatenate(parts, axis=0).astype(bf16)


def near_index(device, na, nb):
    return device // (na * nb) * nb + device % nb


def where_am_i():
    return lax.axis_index("node"), lax.axis_index("feat")


def pack_kernel(
    ids_hbm,
    slots_hbm,
    counts_hbm,
    blocks_hbm,
    features_hbm,
    tiles_hbm,
    grad_hbm,
    sent_ref,
    ids_ref,
    slots_ref,
    counts_ref,
    blocks_ref,
    features_ref,
    tiles_ref,
    grad_ref,
    slots_scratch,
    grad_scratch,
    sems,
    *,
    nx,
    na,
    nb,
    place,
):
    copies = [
        pltpu.make_async_copy(source, target, sems.at[n])
        for n, (source, target) in enumerate(
            [
                (ids_hbm, ids_ref),
                (slots_hbm, slots_ref),
                (counts_hbm, counts_ref),
                (blocks_hbm, blocks_ref),
                (features_hbm, features_ref),
                (tiles_hbm, tiles_ref),
                (grad_hbm, grad_ref),
            ]
        )
    ]
    for copy in copies:
        copy.start()
    for copy in copies:
        copy.wait()
    device, feat = place()
    near = nx * nb
    capacity, nodes = ids_ref.shape
    locals_, width = features_ref.shape
    count, targets, _ = tiles_ref.shape
    part = sent_ref.shape[1] - na * capacity - na - 8
    part = part // count
    lanes = targets // capacity
    near_at = near_index(device, na, nb)

    used = lax.broadcasted_iota(jnp.int32, (capacity, nodes), 0) < counts_ref[pl.ds(device, 1), :]
    slots = jnp.where(used, slots_ref[...], targets).astype(f32)
    slots = jnp.concatenate([slots] * lanes, axis=0)
    slots = jnp.concatenate([slots, jnp.zeros((targets, targets - nodes), f32)], axis=1).T
    group = lax.broadcasted_iota(jnp.int32, (targets, targets), 1) // capacity
    slots_scratch[...] = jnp.where(group == near_at % lanes, slots, 0.0)
    grad_scratch[...] = grad_ref[...].astype(f32).T
    grad_t = grad_scratch[pl.ds(pl.multiple_of(feat * part, part), part), :].astype(bf16)
    terms = [dot(grad_t, tiles_ref[k], ((1,), (0,))) for k in range(count)]
    blocks = [blocks_ref[0, k] for k in range(count)]
    row = lax.broadcasted_iota(jnp.int32, (8, targets), 0)
    far_rows = jnp.zeros((8, targets), jnp.int32)
    for k in range(count):
        far_rows = jnp.where(row == k, blocks[k] % (na * nb) // nb, far_rows)
        far_rows = jnp.where(row == count + k, blocks[k] // (na * nb) * nb + blocks[k] % nb, far_rows)
    far_rows = far_rows.astype(f32)
    local_ids = lax.broadcasted_iota(jnp.int32, (capacity, locals_), 1)
    for x in range(nx):
        for b in range(nb):
            to = x * nb + b
            owners = [(x * na + a) * nb + b for a in range(na)]
            chosen = jnp.concatenate(
                [jnp.where(ids_ref[:, o : o + 1] == local_ids, 1.0, 0.0).astype(bf16) for o in owners],
                axis=0,
            )
            rows = dot(chosen, features_ref[...], ((1,), (0,)))
            sent_ref[to, : na * capacity, :] = rows.astype(bf16)
            at = na * capacity
            for k in range(count):
                there = blocks[k] // (na * nb) * nb + blocks[k] % nb == to
                term = jnp.where(there, terms[k], 0.0)
                sent_ref[to, at : at + part, :] = term.astype(bf16)
                at += part
            slot_rows = slots_scratch[pl.ds(owners[0], na, stride=nb), :]
            sent_ref[to, at : at + na + 8, :] = jnp.concatenate([slot_rows, far_rows], 0).astype(bf16)


def pack(sample_ids, dest_slots, counts, blocks, features, tiles, grad, nx, na, nb, part, place):
    count, targets, _ = tiles.shape
    capacity, nodes = sample_ids.shape
    total = na * capacity + count * part + na + 8
    kernel = functools.partial(pack_kernel, nx=nx, na=na, nb=nb, place=place)
    args = (sample_ids, dest_slots, counts, blocks, features, tiles, grad)
    held = [pltpu.VMEM(arg.shape, arg.dtype) for arg in args]
    held[3] = pltpu.SMEM(blocks.shape, blocks.dtype)
    return pl.pallas_call(
        kernel,
        out_shape=jax.ShapeDtypeStruct((nx * nb, total, features.shape[1]), bf16),
        in_specs=[pl.BlockSpec(memory_space=pltpu.HBM)] * len(args),
        out_specs=pl.BlockSpec(memory_space=pltpu.VMEM),
        scratch_shapes=held
        + [
            pltpu.VMEM((targets, targets), f32),
            pltpu.VMEM((grad.shape[1], targets), f32),
            pltpu.SemaphoreType.DMA((len(args),)),
        ],
        compiler_params=pltpu.CompilerParams(vmem_limit_bytes=PACK_LIMIT),
    )(*args)


def in_vmem(kernel, out_shape, *args):
    vmem = pl.BlockSpec(memory_space=pltpu.VMEM)
    many = isinstance(out_shape, (list, tuple))
    return pl.pallas_call(
        kernel,
        out_shape=out_shape,
        in_specs=[vmem] * len(args),
        out_specs=[vmem] * len(out_shape) if many else vmem,
        compiler_params=pltpu.CompilerParams(vmem_limit_bytes=VMEM_LIMIT),
    )(*args)


def halve(values):
    high = values.astype(bf16)
    return high, (values - high.astype(f32)).astype(bf16)


def gather_kernel(got_ref, sent_ref, *, capacity, part, count):
    near = got_ref.shape[0]
    far, _, targets = sent_ref.shape
    lanes = targets // capacity
    at = far * capacity + count * part
    marks = [got_ref[n, at : at + far + 8, :].astype(f32) for n in range(near)]
    slots = [sum(marks[h : h + lanes])[:far] for h in range(0, near, lanes)]
    nodes = lax.broadcasted_iota(jnp.int32, (targets, targets), 0).astype(f32)
    ones = jnp.ones((8, targets), bf16)
    back = [jnp.zeros((part, targets), f32) for _ in range(far)]
    for n in range(near):
        for k in range(count):
            start = far * capacity + k * part
            term = got_ref[n, start : start + part, :].astype(f32)
            mark = jnp.broadcast_to(marks[n][far + k : far + k + 1, :], (part, targets))
            back = [back[a] + jnp.where(mark == float(a), term, 0.0) for a in range(far)]
    for a in range(far):
        total = jnp.zeros((targets, targets), f32)
        degree = jnp.zeros((8, targets), f32)
        for h in range(near // lanes):
            chosen = jnp.where(slots[h][a : a + 1, :] == nodes, 1.0, 0.0).astype(bf16)
            rows = [
                got_ref[h * lanes + n, a * capacity : (a + 1) * capacity, :] for n in range(lanes)
            ]
            total += dot(chosen, jnp.concatenate(rows, axis=0), ((1,), (0,)))
            degree += dot(ones, chosen, ((1,), (1,)))
        sent_ref[a] = jnp.concatenate([total, back[a], degree], axis=0).astype(bf16)


def first_kernel(came_ref, rows_ref, self_ref, other_ref, sent_ref, mean_ref, *, part):
    targets = rows_ref.shape[0]
    came = came_ref[0].astype(f32)
    for a in range(1, came_ref.shape[0]):
        came += came_ref[a].astype(f32)
    degree = jnp.broadcast_to(came[targets + part : targets + part + 1, :], (targets, targets)).T
    high, low = halve(came[:targets] / (degree + 1.0))
    mean_ref[...] = high
    pre = dot(rows_ref[...], self_ref[...], ((1,), (0,)))
    pre += dot(high, other_ref[...], ((1,), (0,)))
    pre += dot(low, other_ref[...], ((1,), (0,)))
    pre_high, pre_low = halve(pre.T)
    back = jnp.concatenate(halve(came[targets : targets + part]), axis=0)
    for f in range(sent_ref.shape[0]):
        mine = slice(f * part, (f + 1) * part)
        sent_ref[f] = jnp.concatenate([pre_high[mine], pre_low[mine], back], axis=0)


def hidden_kernel(got_ref, self_ref, other_ref, grad_ref, sent_ref, *, part):
    feats = got_ref.shape[0]
    pre = jnp.zeros((part, got_ref.shape[2]), f32)
    for f in range(feats):
        pre += got_ref[f, :part, :].astype(f32) + got_ref[f, part : 2 * part, :].astype(f32)
    sigma = 1.0 / (1.0 + jnp.exp(-pre))
    slope = sigma * (1.0 + pre * (1.0 - sigma))
    back_high = jnp.concatenate([got_ref[f, 2 * part : 3 * part, :] for f in range(feats)], axis=0)
    back_low = jnp.concatenate([got_ref[f, 3 * part :, :] for f in range(feats)], axis=0)
    grad = dot(self_ref[...], grad_ref[...], ((1,), (1,)))
    grad += dot(other_ref[...], back_high, ((1,), (0,)))
    grad += dot(other_ref[...], back_low, ((1,), (0,)))
    both = jnp.concatenate([grad * slope, pre * sigma], axis=0).astype(bf16)
    for f in range(feats):
        sent_ref[f] = both


def grads_kernel(
    full_ref, rows_ref, mean_ref, hidden_ref, back_ref, grad_ref, sent_ref, *, part
):
    feats, near = full_ref.shape[0], sent_ref.shape[0]
    half = sent_ref.shape[2]
    pre = jnp.concatenate([full_ref[f, :part, :] for f in range(feats)], axis=0)
    hidden = hidden_ref[0, part:, :]
    back_high = jnp.concatenate(
        [back_ref[f, 2 * part : 3 * part, :] for f in range(feats)], axis=0
    )
    back_low = jnp.concatenate([back_ref[f, 3 * part :, :] for f in range(feats)], axis=0)
    rows_t = rows_ref[...].astype(f32).T.astype(bf16)
    mean_t = mean_ref[...].astype(f32).T.astype(bf16)
    lower = quarters(dot(rows_t, pre, ((1,), (1,))), dot(mean_t, pre, ((1,), (1,))))
    upper = quarters(
        dot(hidden, grad_ref[...], ((1,), (0,))),
        dot(hidden, back_high, ((1,), (1,))) + dot(hidden, back_low, ((1,), (1,))),
    )
    rows_each, share = lower.shape[0] // near, upper.shape[0] // near
    for n in range(near):
        sent_ref[n, :rows_each, :] = lower[n * rows_each : (n + 1) * rows_each]
        sent_ref[n, rows_each:, :] = upper[n * share : (n + 1) * share]


def far_kernel(got_ref, hidden_ref, sent_ref, *, part):
    total = got_ref[0].astype(f32)
    for n in range(1, got_ref.shape[0]):
        total += got_ref[n].astype(f32)
    total = total.astype(bf16)
    sums = total.shape[0]
    for a in range(sent_ref.shape[0]):
        sent_ref[a, :sums, :] = total
        sent_ref[a, sums:, :] = hidden_ref[0, part:, :]


def near_kernel(got_ref, marks_ref, sent_ref, *, sums, part, count, where):
    far = got_ref.shape[0]
    total = got_ref[0, :sums, :].astype(f32)
    for a in range(1, far):
        total += got_ref[a, :sums, :].astype(f32)
    total = total.astype(bf16)
    here = where().astype(f32)
    blocks = [got_ref[a, sums:, :].astype(f32) for a in range(far)]
    for n in range(sent_ref.shape[0]):
        sent_ref[n, :sums, :] = total
        marks = marks_ref[n].astype(f32)
        for k in range(count):
            mark = jnp.where(marks[far + count + k :][:1] == here, marks[far + k :][:1], -1.0)
            mark = jnp.broadcast_to(mark, blocks[0].shape)
            block = jnp.zeros_like(blocks[0])
            for a in range(far):
                block = jnp.where(mark == float(a), blocks[a], block)
            at = sums + k * part
            sent_ref[n, at : at + part, :] = block.astype(bf16)


def second_kernel(got_ref, tiles_ref, sent_ref, *, rows_each, share, part):
    near = got_ref.shape[0]
    agg = jnp.zeros((part, tiles_ref.shape[1]), f32)
    for k in range(tiles_ref.shape[0]):
        at = rows_each + share + k * part
        block = got_ref[0, at : at + part, :].astype(f32)
        for n in range(1, near):
            block += got_ref[n, at : at + part, :].astype(f32)
        agg += dot(block.astype(bf16), tiles_ref[k], ((1,), (1,)))
    rows = [got_ref[n, rows_each : rows_each + share, :] for n in range(near)]
    both = jnp.concatenate([agg.astype(bf16)] + rows, axis=0)
    for f in range(sent_ref.shape[0]):
        sent_ref[f] = both


def last_kernel(got_ref, hidden_ref, self_ref, other_ref, out_ref, first_ref, second_ref, *, part):
    feats = got_ref.shape[0]
    half = first_ref.shape[1] // 2
    agg = jnp.concatenate([got_ref[f, :part, :] for f in range(feats)], axis=0)
    out = dot(hidden_ref[...], self_ref[...], ((0,), (0,))) + dot(agg, other_ref[...], ((0,), (0,)))
    out_ref[...] = out.astype(bf16)
    for f in range(feats):
        at = f * part
        for n, ref in enumerate([first_ref, second_ref]):
            start = part * (1 + 2 * n)
            ref[at : at + part, :half] = got_ref[f, start : start + part, :].astype(f32)
            ref[at : at + part, half:] = got_ref[f, start + part : start + 2 * part, :].astype(f32)


def shards(
    features,
    self_one,
    neighbour_one,
    sample_ids,
    dest_slots,
    send_counts,
    self_ids,
    tile_blocks,
    tile_weights,
    self_two,
    neighbour_two,
    out_grad,
):
    feats = lax.axis_size("feat")
    nodes = lax.axis_size("node")
    nx, nb = 4, 2
    na = nodes // (nx * nb)
    near = nx * nb
    near_ids = [(x * na + a) * nb + b for a in range(na) for x in range(nx) for b in range(nb)]
    near_groups = [near_ids[a * near : (a + 1) * near] for a in range(na)]
    far_groups = [list(group) for group in zip(*near_groups)]
    feat = lax.axis_index("feat")
    capacity = sample_ids.shape[2]
    targets = self_ids.shape[1]
    width = features.shape[1]
    hidden = neighbour_one.shape[1]
    part = hidden // feats
    tiles = tile_weights[0]
    count = tiles.shape[0]

    sent = pack(
        sample_ids[0].T,
        dest_slots[0].T,
        send_counts,
        tile_blocks,
        features,
        tiles,
        out_grad,
        nx,
        na,
        nb,
        part,
        where_am_i,
    )
    got = exchange(sent, "node", near_groups)

    marks = got[:, na * capacity + count * part :]
    sent = in_vmem(
        functools.partial(gather_kernel, capacity=capacity, part=part, count=count),
        jax.ShapeDtypeStruct((na, targets + part + 8, width), bf16),
        got,
    )
    came = exchange(sent, "node", far_groups)

    self_rows = pick(features, self_ids[0])
    sent, mean_high = in_vmem(
        functools.partial(first_kernel, part=part),
        [
            jax.ShapeDtypeStruct((feats, 4 * part, targets), bf16),
            jax.ShapeDtypeStruct((targets, width), bf16),
        ],
        came,
        self_rows,
        self_one,
        neighbour_one,
    )
    back = exchange(sent, "feat")

    self_two_part = lax.dynamic_slice_in_dim(self_two, feat * part, part, 0)
    neighbour_two_part = lax.dynamic_slice_in_dim(neighbour_two, feat * part, part, 0)
    sent = in_vmem(
        functools.partial(hidden_kernel, part=part),
        jax.ShapeDtypeStruct((feats, 2 * part, targets), bf16),
        back,
        self_two_part,
        neighbour_two_part,
        out_grad,
    )
    hidden_part = sent
    full = exchange(sent, "feat")
    hidden_t = full[:, part:].reshape(hidden, targets)

    half = hidden // 2
    rows_each, share = 4 * width // near, 4 * part // near
    sent = in_vmem(
        functools.partial(grads_kernel, part=part),
        jax.ShapeDtypeStruct((near, rows_each + share, half), bf16),
        full,
        self_rows,
        mean_high,
        hidden_part,
        back,
        out_grad,
    )
    got = exchange(sent, "node", near_groups)
    sent = in_vmem(
        functools.partial(far_kernel, part=part),
        jax.ShapeDtypeStruct((na, rows_each + share + part, half), bf16),
        got,
        hidden_part,
    )
    got = exchange(sent, "node", far_groups)
    sums = rows_each + share
    sent = in_vmem(
        functools.partial(
            near_kernel,
            sums=sums,
            part=part,
            count=count,
            where=lambda: near_index(lax.axis_index("node"), na, nb),
        ),
        jax.ShapeDtypeStruct((near, sums + count * part, half), bf16),
        got,
        marks,
    )
    got = exchange(sent, "node", near_groups)
    lower = got[:, :rows_each].reshape(4, width, half).astype(f32)

    sent = in_vmem(
        functools.partial(second_kernel, rows_each=rows_each, share=share, part=part),
        jax.ShapeDtypeStruct((feats, part + near * share, targets), bf16),
        got,
        tiles,
    )
    got = exchange(sent, "feat")
    layer_output, upper_self, upper_others = in_vmem(
        functools.partial(last_kernel, part=part),
        [
            jax.ShapeDtypeStruct((targets, hidden), bf16),
            jax.ShapeDtypeStruct((hidden, hidden), f32),
            jax.ShapeDtypeStruct((hidden, hidden), f32),
        ],
        got,
        hidden_t,
        self_two,
        neighbour_two,
    )

    def halves(which):
        return jnp.concatenate([lower[2 * which], lower[2 * which + 1]], axis=1)

    return (layer_output, halves(0), halves(1), upper_self, upper_others)


def solution(mesh):
    placed = (
        P("node", "feat"),
        P("feat", None),
        P("feat", None),
        P("node", None, None),
        P("node", None, None),
        P(),
        P("node", None),
        P("node", None),
        P("node", None, None, None),
        P(),
        P(),
        P("node", None),
    )
    return jax.shard_map(
        shards,
        mesh=mesh,
        in_specs=placed,
        out_specs=(P("node", None), P("feat", None), P("feat", None), P(), P()),
        check_vma=False,
    )
```

```python
import functools

import jax
import jax.numpy as jnp
from jax import lax
from jax.experimental import pallas as pl
from jax.experimental.pallas import tpu as pltpu
from jax.sharding import PartitionSpec as P

bf16 = jnp.bfloat16
f32 = jnp.float32
VMEM_LIMIT = 16 * 1024 * 1024
PACK_LIMIT = 60 * 1024 * 1024


def dot(a, b, dims):
    return lax.dot_general(a, b, (dims, ((), ())), preferred_element_type=f32)


def exchange(values, axis, groups=None):
    return lax.all_to_all(
        values, axis, split_axis=0, concat_axis=0, tiled=True, axis_index_groups=groups
    )


def pick(table, row_ids):
    local_ids = jnp.arange(table.shape[0], dtype=jnp.int32)
    chosen = (row_ids[:, None] == local_ids[None, :]).astype(table.dtype)
    return dot(chosen, table, ((1,), (0,))).astype(table.dtype)


def quarters(first, second):
    half = first.shape[1] // 2
    parts = [first[:, :half], first[:, half:], second[:, :half], second[:, half:]]
    return jnp.concatenate(parts, axis=0).astype(bf16)


def near_index(device, na, nb):
    return device // (na * nb) * nb + device % nb


def where_am_i():
    return lax.axis_index("node"), lax.axis_index("feat")


def pack_kernel(
    ids_hbm,
    slots_hbm,
    counts_hbm,
    blocks_hbm,
    features_hbm,
    tiles_hbm,
    grad_hbm,
    sent_ref,
    ids_ref,
    slots_ref,
    counts_ref,
    blocks_ref,
    features_ref,
    tiles_ref,
    grad_ref,
    slots_scratch,
    grad_scratch,
    sems,
    *,
    nx,
    na,
    nb,
    place,
):
    copies = [
        pltpu.make_async_copy(source, target, sems.at[n])
        for n, (source, target) in enumerate(
            [
                (ids_hbm, ids_ref),
                (slots_hbm, slots_ref),
                (counts_hbm, counts_ref),
                (blocks_hbm, blocks_ref),
                (features_hbm, features_ref),
                (tiles_hbm, tiles_ref),
                (grad_hbm, grad_ref),
            ]
        )
    ]
    for copy in copies:
        copy.start()
    for copy in copies:
        copy.wait()
    device, feat = place()
    near = nx * nb
    capacity, nodes = ids_ref.shape
    locals_, width = features_ref.shape
    count, targets, _ = tiles_ref.shape
    part = sent_ref.shape[1] - na * capacity - na - 8
    part = part // count
    lanes = targets // capacity
    near_at = near_index(device, na, nb)

    used = lax.broadcasted_iota(jnp.int32, (capacity, nodes), 0) < counts_ref[pl.ds(device, 1), :]
    slots = jnp.where(used, slots_ref[...], targets).astype(f32)
    slots = jnp.concatenate([slots] * lanes, axis=0)
    slots = jnp.concatenate([slots, jnp.zeros((targets, targets - nodes), f32)], axis=1).T
    group = lax.broadcasted_iota(jnp.int32, (targets, targets), 1) // capacity
    slots_scratch[...] = jnp.where(group == near_at % lanes, slots, 0.0)
    grad_scratch[...] = grad_ref[...].astype(f32).T
    grad_t = grad_scratch[pl.ds(pl.multiple_of(feat * part, part), part), :].astype(bf16)
    terms = [dot(grad_t, tiles_ref[k], ((1,), (0,))) for k in range(count)]
    blocks = [blocks_ref[0, k] for k in range(count)]
    row = lax.broadcasted_iota(jnp.int32, (8, targets), 0)
    far_rows = jnp.zeros((8, targets), jnp.int32)
    for k in range(count):
        far_rows = jnp.where(row == k, blocks[k] % (na * nb) // nb, far_rows)
        far_rows = jnp.where(row == count + k, blocks[k] // (na * nb) * nb + blocks[k] % nb, far_rows)
    far_rows = far_rows.astype(f32)
    local_ids = lax.broadcasted_iota(jnp.int32, (capacity, locals_), 1)
    for x in range(nx):
        for b in range(nb):
            to = x * nb + b
            owners = [(x * na + a) * nb + b for a in range(na)]
            chosen = jnp.concatenate(
                [jnp.where(ids_ref[:, o : o + 1] == local_ids, 1.0, 0.0).astype(bf16) for o in owners],
                axis=0,
            )
            rows = dot(chosen, features_ref[...], ((1,), (0,)))
            sent_ref[to, : na * capacity, :] = rows.astype(bf16)
            at = na * capacity
            for k in range(count):
                there = blocks[k] // (na * nb) * nb + blocks[k] % nb == to
                term = jnp.where(there, terms[k], 0.0)
                sent_ref[to, at : at + part, :] = term.astype(bf16)
                at += part
            slot_rows = slots_scratch[pl.ds(owners[0], na, stride=nb), :]
            sent_ref[to, at : at + na + 8, :] = jnp.concatenate([slot_rows, far_rows], 0).astype(bf16)


def pack(sample_ids, dest_slots, counts, blocks, features, tiles, grad, nx, na, nb, part, place):
    count, targets, _ = tiles.shape
    capacity, nodes = sample_ids.shape
    total = na * capacity + count * part + na + 8
    kernel = functools.partial(pack_kernel, nx=nx, na=na, nb=nb, place=place)
    args = (sample_ids, dest_slots, counts, blocks, features, tiles, grad)
    held = [pltpu.VMEM(arg.shape, arg.dtype) for arg in args]
    held[3] = pltpu.SMEM(blocks.shape, blocks.dtype)
    return pl.pallas_call(
        kernel,
        out_shape=jax.ShapeDtypeStruct((nx * nb, total, features.shape[1]), bf16),
        in_specs=[pl.BlockSpec(memory_space=pltpu.HBM)] * len(args),
        out_specs=pl.BlockSpec(memory_space=pltpu.VMEM),
        scratch_shapes=held
        + [
            pltpu.VMEM((targets, targets), f32),
            pltpu.VMEM((grad.shape[1], targets), f32),
            pltpu.SemaphoreType.DMA((len(args),)),
        ],
        compiler_params=pltpu.CompilerParams(vmem_limit_bytes=PACK_LIMIT),
    )(*args)


def in_vmem(kernel, out_shape, *args, scratch_shapes=()):
    vmem = pl.BlockSpec(memory_space=pltpu.VMEM)
    many = isinstance(out_shape, (list, tuple))
    return pl.pallas_call(
        kernel,
        out_shape=out_shape,
        in_specs=[vmem] * len(args),
        out_specs=[vmem] * len(out_shape) if many else vmem,
        scratch_shapes=scratch_shapes,
        compiler_params=pltpu.CompilerParams(vmem_limit_bytes=VMEM_LIMIT),
    )(*args)


def halve(values):
    high = values.astype(bf16)
    return high, (values - high.astype(f32)).astype(bf16)


def gather_kernel(got_ref, sent_ref, marks_ref, *, capacity, part, count):
    near = got_ref.shape[0]
    far, _, targets = sent_ref.shape
    lanes = targets // capacity
    at = far * capacity + count * part
    marks = [got_ref[n, at : at + far + 8, :].astype(f32) for n in range(near)]
    for n in range(near):
        marks_ref[n] = got_ref[n, at : at + far + 8, :]
    slots = [sum(marks[h : h + lanes])[:far] for h in range(0, near, lanes)]
    nodes = lax.broadcasted_iota(jnp.int32, (targets, targets), 0).astype(f32)
    ones = jnp.ones((8, targets), bf16)
    back = [jnp.zeros((part, targets), f32) for _ in range(far)]
    for n in range(near):
        for k in range(count):
            start = far * capacity + k * part
            term = got_ref[n, start : start + part, :].astype(f32)
            mark = jnp.broadcast_to(marks[n][far + k : far + k + 1, :], (part, targets))
            back = [back[a] + jnp.where(mark == float(a), term, 0.0) for a in range(far)]
    for a in range(far):
        total = jnp.zeros((targets, targets), f32)
        degree = jnp.zeros((8, targets), f32)
        for h in range(near // lanes):
            chosen = jnp.where(slots[h][a : a + 1, :] == nodes, 1.0, 0.0).astype(bf16)
            rows = [
                got_ref[h * lanes + n, a * capacity : (a + 1) * capacity, :] for n in range(lanes)
            ]
            total += dot(chosen, jnp.concatenate(rows, axis=0), ((1,), (0,)))
            degree += dot(ones, chosen, ((1,), (1,)))
        sent_ref[a] = jnp.concatenate([total, back[a], degree], axis=0).astype(bf16)


def first_kernel(came_ref, rows_ref, self_ref, other_ref, sent_ref, mean_ref, *, part):
    targets = rows_ref.shape[0]
    came = came_ref[0].astype(f32)
    for a in range(1, came_ref.shape[0]):
        came += came_ref[a].astype(f32)
    degree = jnp.broadcast_to(came[targets + part : targets + part + 1, :], (targets, targets)).T
    high, low = halve(came[:targets] / (degree + 1.0))
    mean_ref[...] = high
    pre = dot(rows_ref[...], self_ref[...], ((1,), (0,)))
    pre += dot(high, other_ref[...], ((1,), (0,)))
    pre += dot(low, other_ref[...], ((1,), (0,)))
    back = halve(came[targets : targets + part])
    all_rows = jnp.concatenate([pre.T.astype(bf16), *back], axis=0)
    for f in range(sent_ref.shape[0]):
        sent_ref[f] = all_rows


def grads_kernel(
    got_ref,
    self_ref,
    other_ref,
    grad_ref,
    rows_ref,
    mean_ref,
    sent_ref,
    hidden_ref,
    mine_ref,
    scratch,
    *,
    part,
    slice_at,
):
    feats, near = got_ref.shape[0], sent_ref.shape[0]
    hidden = self_ref.shape[0]
    pre = got_ref[0, :hidden, :].astype(f32)
    for f in range(1, feats):
        pre += got_ref[f, :hidden, :].astype(f32)
    sigma = 1.0 / (1.0 + jnp.exp(-pre))
    slope = sigma * (1.0 + pre * (1.0 - sigma))
    scratch[...] = pre * sigma
    hidden_ref[...] = scratch[...].astype(bf16)
    mine = scratch[pl.ds(pl.multiple_of(slice_at() * part, part), part), :].astype(bf16)
    mine_ref[...] = mine
    back_high = [got_ref[f, hidden : hidden + part, :] for f in range(feats)]
    back_high = jnp.concatenate(back_high, axis=0)
    back_low = [got_ref[f, hidden + part :, :] for f in range(feats)]
    back_low = jnp.concatenate(back_low, axis=0)
    grad = dot(self_ref[...], grad_ref[...], ((1,), (1,)))
    grad += dot(other_ref[...], back_high, ((1,), (0,)))
    grad += dot(other_ref[...], back_low, ((1,), (0,)))
    grad = (grad * slope).astype(bf16)
    rows_t = rows_ref[...].astype(f32).T.astype(bf16)
    mean_t = mean_ref[...].astype(f32).T.astype(bf16)
    lower = quarters(dot(rows_t, grad, ((1,), (1,))), dot(mean_t, grad, ((1,), (1,))))
    upper = quarters(
        dot(mine, grad_ref[...], ((1,), (0,))),
        dot(mine, back_high, ((1,), (1,))) + dot(mine, back_low, ((1,), (1,))),
    )
    rows_each, share = lower.shape[0] // near, upper.shape[0] // near
    for n in range(near):
        sent_ref[n, :rows_each, :] = lower[n * rows_each : (n + 1) * rows_each]
        sent_ref[n, rows_each:, :] = upper[n * share : (n + 1) * share]


def far_kernel(got_ref, hidden_ref, sent_ref):
    total = got_ref[0].astype(f32)
    for n in range(1, got_ref.shape[0]):
        total += got_ref[n].astype(f32)
    total = total.astype(bf16)
    sums = total.shape[0]
    for a in range(sent_ref.shape[0]):
        sent_ref[a, :sums, :] = total
        sent_ref[a, sums:, :] = hidden_ref[...]


def near_kernel(got_ref, marks_ref, sent_ref, *, sums, part, count, where):
    far = got_ref.shape[0]
    total = got_ref[0, :sums, :].astype(f32)
    for a in range(1, far):
        total += got_ref[a, :sums, :].astype(f32)
    total = total.astype(bf16)
    here = where().astype(f32)
    blocks = [got_ref[a, sums:, :].astype(f32) for a in range(far)]
    for n in range(sent_ref.shape[0]):
        sent_ref[n, :sums, :] = total
        marks = marks_ref[n].astype(f32)
        for k in range(count):
            mark = jnp.where(marks[far + count + k :][:1] == here, marks[far + k :][:1], -1.0)
            mark = jnp.broadcast_to(mark, blocks[0].shape)
            block = jnp.zeros_like(blocks[0])
            for a in range(far):
                block = jnp.where(mark == float(a), blocks[a], block)
            at = sums + k * part
            sent_ref[n, at : at + part, :] = block.astype(bf16)


def second_kernel(got_ref, tiles_ref, sent_ref, *, rows_each, share, part):
    near = got_ref.shape[0]
    agg = jnp.zeros((part, tiles_ref.shape[1]), f32)
    for k in range(tiles_ref.shape[0]):
        at = rows_each + share + k * part
        block = got_ref[0, at : at + part, :].astype(f32)
        for n in range(1, near):
            block += got_ref[n, at : at + part, :].astype(f32)
        agg += dot(block.astype(bf16), tiles_ref[k], ((1,), (1,)))
    rows = [got_ref[n, rows_each : rows_each + share, :] for n in range(near)]
    both = jnp.concatenate([agg.astype(bf16)] + rows, axis=0)
    for f in range(sent_ref.shape[0]):
        sent_ref[f] = both


def last_kernel(got_ref, hidden_ref, self_ref, other_ref, out_ref, first_ref, second_ref, *, part):
    feats = got_ref.shape[0]
    half = first_ref.shape[1] // 2
    agg = jnp.concatenate([got_ref[f, :part, :] for f in range(feats)], axis=0)
    out = dot(hidden_ref[...], self_ref[...], ((0,), (0,))) + dot(agg, other_ref[...], ((0,), (0,)))
    out_ref[...] = out.astype(bf16)
    for f in range(feats):
        at = f * part
        for n, ref in enumerate([first_ref, second_ref]):
            start = part * (1 + 2 * n)
            ref[at : at + part, :half] = got_ref[f, start : start + part, :].astype(f32)
            ref[at : at + part, half:] = got_ref[f, start + part : start + 2 * part, :].astype(f32)


def shards(
    features,
    self_one,
    neighbour_one,
    sample_ids,
    dest_slots,
    send_counts,
    self_ids,
    tile_blocks,
    tile_weights,
    self_two,
    neighbour_two,
    out_grad,
):
    feats = lax.axis_size("feat")
    nodes = lax.axis_size("node")
    nx, nb = 4, 2
    na = nodes // (nx * nb)
    near = nx * nb
    near_ids = [(x * na + a) * nb + b for a in range(na) for x in range(nx) for b in range(nb)]
    near_groups = [near_ids[a * near : (a + 1) * near] for a in range(na)]
    far_groups = [list(group) for group in zip(*near_groups)]
    capacity = sample_ids.shape[2]
    targets = self_ids.shape[1]
    width = features.shape[1]
    hidden = neighbour_one.shape[1]
    part = hidden // feats
    tiles = tile_weights[0]
    count = tiles.shape[0]

    sent = pack(
        sample_ids[0].T,
        dest_slots[0].T,
        send_counts,
        tile_blocks,
        features,
        tiles,
        out_grad,
        nx,
        na,
        nb,
        part,
        where_am_i,
    )
    got = exchange(sent, "node", near_groups)

    sent, marks = in_vmem(
        functools.partial(gather_kernel, capacity=capacity, part=part, count=count),
        [
            jax.ShapeDtypeStruct((na, targets + part + 8, width), bf16),
            jax.ShapeDtypeStruct((near, na + 8, targets), bf16),
        ],
        got,
    )
    came = exchange(sent, "node", far_groups)

    self_rows = pick(features, self_ids[0])
    sent, mean_high = in_vmem(
        functools.partial(first_kernel, part=part),
        [
            jax.ShapeDtypeStruct((feats, hidden + 2 * part, targets), bf16),
            jax.ShapeDtypeStruct((targets, width), bf16),
        ],
        came,
        self_rows,
        self_one,
        neighbour_one,
    )
    got = exchange(sent, "feat")

    half = hidden // 2
    rows_each, share = 4 * width // near, 4 * part // near
    sent, hidden_t, hidden_part = in_vmem(
        functools.partial(grads_kernel, part=part, slice_at=lambda: lax.axis_index("feat")),
        [
            jax.ShapeDtypeStruct((near, rows_each + share, half), bf16),
            jax.ShapeDtypeStruct((hidden, targets), bf16),
            jax.ShapeDtypeStruct((part, targets), bf16),
        ],
        got,
        self_two,
        neighbour_two,
        out_grad,
        self_rows,
        mean_high,
        scratch_shapes=[pltpu.VMEM((hidden, targets), f32)],
    )
    got = exchange(sent, "node", near_groups)
    sent = in_vmem(
        far_kernel,
        jax.ShapeDtypeStruct((na, rows_each + share + part, half), bf16),
        got,
        hidden_part,
    )
    got = exchange(sent, "node", far_groups)
    sums = rows_each + share
    sent = in_vmem(
        functools.partial(
            near_kernel,
            sums=sums,
            part=part,
            count=count,
            where=lambda: near_index(lax.axis_index("node"), na, nb),
        ),
        jax.ShapeDtypeStruct((near, sums + count * part, half), bf16),
        got,
        marks,
    )
    got = exchange(sent, "node", near_groups)
    lower = got[:, :rows_each].reshape(4, width, half).astype(f32)

    sent = in_vmem(
        functools.partial(second_kernel, rows_each=rows_each, share=share, part=part),
        jax.ShapeDtypeStruct((feats, part + near * share, targets), bf16),
        got,
        tiles,
    )
    got = exchange(sent, "feat")
    layer_output, upper_self, upper_others = in_vmem(
        functools.partial(last_kernel, part=part),
        [
            jax.ShapeDtypeStruct((targets, hidden), bf16),
            jax.ShapeDtypeStruct((hidden, hidden), f32),
            jax.ShapeDtypeStruct((hidden, hidden), f32),
        ],
        got,
        hidden_t,
        self_two,
        neighbour_two,
    )

    def halves(which):
        return jnp.concatenate([lower[2 * which], lower[2 * which + 1]], axis=1)

    return (layer_output, halves(0), halves(1), upper_self, upper_others)


def solution(mesh):
    placed = (
        P("node", "feat"),
        P("feat", None),
        P("feat", None),
        P("node", None, None),
        P("node", None, None),
        P(),
        P("node", None),
        P("node", None),
        P("node", None, None, None),
        P(),
        P(),
        P("node", None),
    )
    return jax.shard_map(
        shards,
        mesh=mesh,
        in_specs=placed,
        out_specs=(P("node", None), P("feat", None), P("feat", None), P(), P()),
        check_vma=False,
    )
```

```python
import functools

import jax
import jax.numpy as jnp
from jax import lax
from jax.experimental import pallas as pl
from jax.experimental.pallas import tpu as pltpu
from jax.sharding import PartitionSpec as P

bf16 = jnp.bfloat16
f32 = jnp.float32
VMEM_LIMIT = 16 * 1024 * 1024
PACK_LIMIT = 60 * 1024 * 1024


def dot(a, b, dims):
    return lax.dot_general(a, b, (dims, ((), ())), preferred_element_type=f32)


def exchange(values, axis, groups=None):
    return lax.all_to_all(
        values, axis, split_axis=0, concat_axis=0, tiled=True, axis_index_groups=groups
    )


def quarters(first, second):
    half = first.shape[1] // 2
    parts = [first[:, :half], first[:, half:], second[:, :half], second[:, half:]]
    return jnp.concatenate(parts, axis=0).astype(bf16)


def near_index(device, na, nb):
    return device // (na * nb) * nb + device % nb


def where_am_i():
    return lax.axis_index("node"), lax.axis_index("feat")


def pack_kernel(
    ids_hbm,
    slots_hbm,
    counts_hbm,
    blocks_hbm,
    features_hbm,
    tiles_hbm,
    grad_hbm,
    own_hbm,
    sent_hbm,
    own_rows_ref,
    ids_ref,
    slots_ref,
    counts_ref,
    blocks_ref,
    features_ref,
    tiles_ref,
    grad_ref,
    own_ref,
    sent_ref,
    slots_scratch,
    grad_scratch,
    sems,
    out_sems,
    *,
    nx,
    na,
    nb,
    place,
):
    copies = [
        pltpu.make_async_copy(source, target, sems.at[n])
        for n, (source, target) in enumerate(
            [
                (ids_hbm, ids_ref),
                (slots_hbm, slots_ref),
                (counts_hbm, counts_ref),
                (blocks_hbm, blocks_ref),
                (features_hbm, features_ref),
                (tiles_hbm, tiles_ref),
                (grad_hbm, grad_ref),
                (own_hbm, own_ref),
            ]
        )
    ]
    for copy in copies:
        copy.start()
    for copy in copies:
        copy.wait()
    device, feat = place()
    near = nx * nb
    capacity, nodes = ids_ref.shape
    locals_, width = features_ref.shape
    count, targets, _ = tiles_ref.shape
    part = sent_ref.shape[1] - na * capacity - na - 8
    part = part // count
    lanes = targets // capacity
    near_at = near_index(device, na, nb)

    used = lax.broadcasted_iota(jnp.int32, (capacity, nodes), 0) < counts_ref[pl.ds(device, 1), :]
    slots = jnp.where(used, slots_ref[...], targets).astype(f32)
    slots = jnp.concatenate([slots] * lanes, axis=0)
    slots = jnp.concatenate([slots, jnp.zeros((targets, targets - nodes), f32)], axis=1).T
    group = lax.broadcasted_iota(jnp.int32, (targets, targets), 1) // capacity
    slots_scratch[...] = jnp.where(group == near_at % lanes, slots, 0.0)
    grad_scratch[...] = grad_ref[...].astype(f32).T
    grad_t = grad_scratch[pl.ds(pl.multiple_of(feat * part, part), part), :].astype(bf16)
    terms = [dot(grad_t, tiles_ref[k], ((1,), (0,))) for k in range(count)]
    blocks = [blocks_ref[0, k] for k in range(count)]
    row = lax.broadcasted_iota(jnp.int32, (8, targets), 0)
    far_rows = jnp.zeros((8, targets), jnp.int32)
    for k in range(count):
        far_rows = jnp.where(row == k, blocks[k] % (na * nb) // nb, far_rows)
        far_rows = jnp.where(row == count + k, blocks[k] // (na * nb) * nb + blocks[k] % nb, far_rows)
    far_rows = far_rows.astype(f32)
    local_ids = lax.broadcasted_iota(jnp.int32, (capacity, locals_), 1)
    outs = []
    for x in range(nx):
        for b in range(nb):
            to = x * nb + b
            owners = [(x * na + a) * nb + b for a in range(na)]
            chosen = jnp.concatenate(
                [jnp.where(ids_ref[:, o : o + 1] == local_ids, 1.0, 0.0).astype(bf16) for o in owners],
                axis=0,
            )
            rows = dot(chosen, features_ref[...], ((1,), (0,)))
            sent_ref[to, : na * capacity, :] = rows.astype(bf16)
            at = na * capacity
            for k in range(count):
                there = blocks[k] // (na * nb) * nb + blocks[k] % nb == to
                term = jnp.where(there, terms[k], 0.0)
                sent_ref[to, at : at + part, :] = term.astype(bf16)
                at += part
            slot_rows = slots_scratch[pl.ds(owners[0], na, stride=nb), :]
            sent_ref[to, at : at + na + 8, :] = jnp.concatenate([slot_rows, far_rows], 0).astype(bf16)
            out = pltpu.make_async_copy(sent_ref.at[to], sent_hbm.at[to], out_sems.at[to])
            out.start()
            outs.append(out)
    own = jnp.broadcast_to(own_ref[...], (targets, targets)).astype(f32).T.astype(jnp.int32)
    local_ids = lax.broadcasted_iota(jnp.int32, (targets, targets), 1)
    chosen = [
        jnp.where(own == local_ids + start, 1.0, 0.0).astype(bf16)
        for start in range(0, locals_, targets)
    ]
    own_rows = dot(jnp.concatenate(chosen, axis=1), features_ref[...], ((1,), (0,)))
    own_rows_ref[...] = own_rows.astype(bf16)
    for out in outs:
        out.wait()


def pack(sample_ids, dest_slots, counts, blocks, features, tiles, grad, own, nx, na, nb, part, place):
    count, targets, _ = tiles.shape
    capacity, nodes = sample_ids.shape
    total = na * capacity + count * part + na + 8
    kernel = functools.partial(pack_kernel, nx=nx, na=na, nb=nb, place=place)
    args = (sample_ids, dest_slots, counts, blocks, features, tiles, grad, own)
    held = [pltpu.VMEM(arg.shape, arg.dtype) for arg in args]
    held[3] = pltpu.SMEM(blocks.shape, blocks.dtype)
    return pl.pallas_call(
        kernel,
        out_shape=[
            jax.ShapeDtypeStruct((nx * nb, total, features.shape[1]), bf16),
            jax.ShapeDtypeStruct((targets, features.shape[1]), bf16),
        ],
        in_specs=[pl.BlockSpec(memory_space=pltpu.HBM)] * len(args),
        out_specs=[
            pl.BlockSpec(memory_space=pltpu.HBM),
            pl.BlockSpec(memory_space=pltpu.VMEM),
        ],
        scratch_shapes=held
        + [
            pltpu.VMEM((nx * nb, total, features.shape[1]), bf16),
            pltpu.VMEM((targets, targets), f32),
            pltpu.VMEM((grad.shape[1], targets), f32),
            pltpu.SemaphoreType.DMA((len(args),)),
            pltpu.SemaphoreType.DMA((nx * nb,)),
        ],
        compiler_params=pltpu.CompilerParams(vmem_limit_bytes=PACK_LIMIT),
    )(*args)


def in_vmem(kernel, out_shape, *args, scratch_shapes=()):
    vmem = pl.BlockSpec(memory_space=pltpu.VMEM)
    many = isinstance(out_shape, (list, tuple))
    return pl.pallas_call(
        kernel,
        out_shape=out_shape,
        in_specs=[vmem] * len(args),
        out_specs=[vmem] * len(out_shape) if many else vmem,
        scratch_shapes=scratch_shapes,
        compiler_params=pltpu.CompilerParams(vmem_limit_bytes=VMEM_LIMIT),
    )(*args)


def halve(values):
    high = values.astype(bf16)
    return high, (values - high.astype(f32)).astype(bf16)


def gather_kernel(got_ref, sent_ref, marks_ref, *, capacity, part, count):
    near = got_ref.shape[0]
    far, _, targets = sent_ref.shape
    lanes = targets // capacity
    at = far * capacity + count * part
    marks = [got_ref[n, at : at + far + 8, :].astype(f32) for n in range(near)]
    for n in range(near):
        marks_ref[n] = got_ref[n, at : at + far + 8, :]
    slots = [sum(marks[h : h + lanes])[:far] for h in range(0, near, lanes)]
    nodes = lax.broadcasted_iota(jnp.int32, (targets, targets), 0).astype(f32)
    ones = jnp.ones((8, targets), bf16)
    back = [jnp.zeros((part, targets), f32) for _ in range(far)]
    for n in range(near):
        for k in range(count):
            start = far * capacity + k * part
            term = got_ref[n, start : start + part, :].astype(f32)
            mark = jnp.broadcast_to(marks[n][far + k : far + k + 1, :], (part, targets))
            back = [back[a] + jnp.where(mark == float(a), term, 0.0) for a in range(far)]
    for a in range(far):
        total = jnp.zeros((targets, targets), f32)
        degree = jnp.zeros((8, targets), f32)
        for h in range(near // lanes):
            chosen = jnp.where(slots[h][a : a + 1, :] == nodes, 1.0, 0.0).astype(bf16)
            rows = [
                got_ref[h * lanes + n, a * capacity : (a + 1) * capacity, :] for n in range(lanes)
            ]
            total += dot(chosen, jnp.concatenate(rows, axis=0), ((1,), (0,)))
            degree += dot(ones, chosen, ((1,), (1,)))
        sent_ref[a] = jnp.concatenate([total, back[a], degree], axis=0).astype(bf16)


def first_kernel(came_ref, rows_ref, self_ref, other_ref, sent_ref, mean_ref, *, part):
    targets = rows_ref.shape[0]
    came = came_ref[0].astype(f32)
    for a in range(1, came_ref.shape[0]):
        came += came_ref[a].astype(f32)
    degree = jnp.broadcast_to(came[targets + part : targets + part + 1, :], (targets, targets)).T
    high, low = halve(came[:targets] / (degree + 1.0))
    mean_ref[...] = high
    pre = dot(rows_ref[...], self_ref[...], ((1,), (0,)))
    pre += dot(high, other_ref[...], ((1,), (0,)))
    pre += dot(low, other_ref[...], ((1,), (0,)))
    back = halve(came[targets : targets + part])
    all_rows = jnp.concatenate([pre.T.astype(bf16), *back], axis=0)
    for f in range(sent_ref.shape[0]):
        sent_ref[f] = all_rows


def grads_kernel(
    got_ref,
    self_ref,
    other_ref,
    grad_ref,
    rows_ref,
    mean_ref,
    sent_ref,
    hidden_ref,
    mine_ref,
    scratch,
    *,
    part,
    slice_at,
):
    feats, near = got_ref.shape[0], sent_ref.shape[0]
    hidden = self_ref.shape[0]
    pre = got_ref[0, :hidden, :].astype(f32)
    for f in range(1, feats):
        pre += got_ref[f, :hidden, :].astype(f32)
    sigma = 1.0 / (1.0 + jnp.exp(-pre))
    slope = sigma * (1.0 + pre * (1.0 - sigma))
    scratch[...] = pre * sigma
    hidden_ref[...] = scratch[...].astype(bf16)
    mine = scratch[pl.ds(pl.multiple_of(slice_at() * part, part), part), :].astype(bf16)
    mine_ref[...] = mine
    back_high = [got_ref[f, hidden : hidden + part, :] for f in range(feats)]
    back_high = jnp.concatenate(back_high, axis=0)
    back_low = [got_ref[f, hidden + part :, :] for f in range(feats)]
    back_low = jnp.concatenate(back_low, axis=0)
    grad = dot(self_ref[...], grad_ref[...], ((1,), (1,)))
    grad += dot(other_ref[...], back_high, ((1,), (0,)))
    grad += dot(other_ref[...], back_low, ((1,), (0,)))
    grad = (grad * slope).astype(bf16)
    rows_t = rows_ref[...].astype(f32).T.astype(bf16)
    mean_t = mean_ref[...].astype(f32).T.astype(bf16)
    lower = quarters(dot(rows_t, grad, ((1,), (1,))), dot(mean_t, grad, ((1,), (1,))))
    upper = quarters(
        dot(mine, grad_ref[...], ((1,), (0,))),
        dot(mine, back_high, ((1,), (1,))) + dot(mine, back_low, ((1,), (1,))),
    )
    rows_each, share = lower.shape[0] // near, upper.shape[0] // near
    for n in range(near):
        sent_ref[n, :rows_each, :] = lower[n * rows_each : (n + 1) * rows_each]
        sent_ref[n, rows_each:, :] = upper[n * share : (n + 1) * share]


def far_kernel(got_ref, hidden_ref, sent_ref):
    total = got_ref[0].astype(f32)
    for n in range(1, got_ref.shape[0]):
        total += got_ref[n].astype(f32)
    total = total.astype(bf16)
    sums = total.shape[0]
    for a in range(sent_ref.shape[0]):
        sent_ref[a, :sums, :] = total
        sent_ref[a, sums:, :] = hidden_ref[...]


def near_kernel(got_ref, marks_ref, sent_ref, *, sums, part, count, where):
    far = got_ref.shape[0]
    total = got_ref[0, :sums, :].astype(f32)
    for a in range(1, far):
        total += got_ref[a, :sums, :].astype(f32)
    total = total.astype(bf16)
    here = where().astype(f32)
    blocks = [got_ref[a, sums:, :].astype(f32) for a in range(far)]
    for n in range(sent_ref.shape[0]):
        sent_ref[n, :sums, :] = total
        marks = marks_ref[n].astype(f32)
        for k in range(count):
            mark = jnp.where(marks[far + count + k :][:1] == here, marks[far + k :][:1], -1.0)
            mark = jnp.broadcast_to(mark, blocks[0].shape)
            block = jnp.zeros_like(blocks[0])
            for a in range(far):
                block = jnp.where(mark == float(a), blocks[a], block)
            at = sums + k * part
            sent_ref[n, at : at + part, :] = block.astype(bf16)


def second_kernel(got_ref, tiles_ref, sent_ref, *, rows_each, share, part):
    near = got_ref.shape[0]
    agg = jnp.zeros((part, tiles_ref.shape[1]), f32)
    for k in range(tiles_ref.shape[0]):
        at = rows_each + share + k * part
        block = got_ref[0, at : at + part, :].astype(f32)
        for n in range(1, near):
            block += got_ref[n, at : at + part, :].astype(f32)
        agg += dot(block.astype(bf16), tiles_ref[k], ((1,), (1,)))
    rows = [got_ref[n, rows_each : rows_each + share, :] for n in range(near)]
    both = jnp.concatenate([agg.astype(bf16)] + rows, axis=0)
    for f in range(sent_ref.shape[0]):
        sent_ref[f] = both


def last_kernel(
    got_ref,
    hidden_ref,
    self_ref,
    other_ref,
    lower_ref,
    out_ref,
    low_first_ref,
    low_second_ref,
    first_ref,
    second_ref,
    *,
    part,
    rows_each,
):
    feats = got_ref.shape[0]
    half = first_ref.shape[1] // 2
    agg = jnp.concatenate([got_ref[f, :part, :] for f in range(feats)], axis=0)
    out = dot(hidden_ref[...], self_ref[...], ((0,), (0,))) + dot(agg, other_ref[...], ((0,), (0,)))
    out_ref[...] = out.astype(bf16)
    for f in range(feats):
        at = f * part
        for n, ref in enumerate([first_ref, second_ref]):
            start = part * (1 + 2 * n)
            ref[at : at + part, :half] = got_ref[f, start : start + part, :].astype(f32)
            ref[at : at + part, half:] = got_ref[f, start + part : start + 2 * part, :].astype(f32)
    width = low_first_ref.shape[0]
    for n in range(lower_ref.shape[0]):
        quarter, at = divmod(n * rows_each, width)
        ref = (low_first_ref, low_second_ref)[quarter // 2]
        left = quarter % 2 * half
        rows = lower_ref[n, :rows_each, :].astype(f32)
        ref[at : at + rows_each, left : left + half] = rows


def shards(
    features,
    self_one,
    neighbour_one,
    sample_ids,
    dest_slots,
    send_counts,
    self_ids,
    tile_blocks,
    tile_weights,
    self_two,
    neighbour_two,
    out_grad,
):
    feats = lax.axis_size("feat")
    nodes = lax.axis_size("node")
    nx, nb = 4, 2
    na = nodes // (nx * nb)
    near = nx * nb
    near_ids = [(x * na + a) * nb + b for a in range(na) for x in range(nx) for b in range(nb)]
    near_groups = [near_ids[a * near : (a + 1) * near] for a in range(na)]
    far_groups = [list(group) for group in zip(*near_groups)]
    capacity = sample_ids.shape[2]
    targets = self_ids.shape[1]
    width = features.shape[1]
    hidden = neighbour_one.shape[1]
    part = hidden // feats
    tiles = tile_weights[0]
    count = tiles.shape[0]

    sent, self_rows = pack(
        sample_ids[0].T,
        dest_slots[0].T,
        send_counts,
        tile_blocks,
        features,
        tiles,
        out_grad,
        self_ids,
        nx,
        na,
        nb,
        part,
        where_am_i,
    )
    got = exchange(sent, "node", near_groups)

    sent, marks = in_vmem(
        functools.partial(gather_kernel, capacity=capacity, part=part, count=count),
        [
            jax.ShapeDtypeStruct((na, targets + part + 8, width), bf16),
            jax.ShapeDtypeStruct((near, na + 8, targets), bf16),
        ],
        got,
    )
    came = exchange(sent, "node", far_groups)

    sent, mean_high = in_vmem(
        functools.partial(first_kernel, part=part),
        [
            jax.ShapeDtypeStruct((feats, hidden + 2 * part, targets), bf16),
            jax.ShapeDtypeStruct((targets, width), bf16),
        ],
        came,
        self_rows,
        self_one,
        neighbour_one,
    )
    got = exchange(sent, "feat")

    half = hidden // 2
    rows_each, share = 4 * width // near, 4 * part // near
    sent, hidden_t, hidden_part = in_vmem(
        functools.partial(grads_kernel, part=part, slice_at=lambda: lax.axis_index("feat")),
        [
            jax.ShapeDtypeStruct((near, rows_each + share, half), bf16),
            jax.ShapeDtypeStruct((hidden, targets), bf16),
            jax.ShapeDtypeStruct((part, targets), bf16),
        ],
        got,
        self_two,
        neighbour_two,
        out_grad,
        self_rows,
        mean_high,
        scratch_shapes=[pltpu.VMEM((hidden, targets), f32)],
    )
    got = exchange(sent, "node", near_groups)
    sent = in_vmem(
        far_kernel,
        jax.ShapeDtypeStruct((na, rows_each + share + part, half), bf16),
        got,
        hidden_part,
    )
    got = exchange(sent, "node", far_groups)
    sums = rows_each + share
    sent = in_vmem(
        functools.partial(
            near_kernel,
            sums=sums,
            part=part,
            count=count,
            where=lambda: near_index(lax.axis_index("node"), na, nb),
        ),
        jax.ShapeDtypeStruct((near, sums + count * part, half), bf16),
        got,
        marks,
    )
    got = exchange(sent, "node", near_groups)
    lower = got

    sent = in_vmem(
        functools.partial(second_kernel, rows_each=rows_each, share=share, part=part),
        jax.ShapeDtypeStruct((feats, part + near * share, targets), bf16),
        got,
        tiles,
    )
    got = exchange(sent, "feat")
    return in_vmem(
        functools.partial(last_kernel, part=part, rows_each=rows_each),
        [
            jax.ShapeDtypeStruct((targets, hidden), bf16),
            jax.ShapeDtypeStruct((width, hidden), f32),
            jax.ShapeDtypeStruct((width, hidden), f32),
            jax.ShapeDtypeStruct((hidden, hidden), f32),
            jax.ShapeDtypeStruct((hidden, hidden), f32),
        ],
        got,
        hidden_t,
        self_two,
        neighbour_two,
        lower,
    )


def solution(mesh):
    placed = (
        P("node", "feat"),
        P("feat", None),
        P("feat", None),
        P("node", None, None),
        P("node", None, None),
        P(),
        P("node", None),
        P("node", None),
        P("node", None, None, None),
        P(),
        P(),
        P("node", None),
    )
    return jax.shard_map(
        shards,
        mesh=mesh,
        in_specs=placed,
        out_specs=(P("node", None), P("feat", None), P("feat", None), P(), P()),
        check_vma=False,
    )
```

```python
import functools

import jax
import jax.numpy as jnp
from jax import lax
from jax.experimental import pallas as pl
from jax.experimental.pallas import tpu as pltpu
from jax.sharding import PartitionSpec as P

bf16 = jnp.bfloat16
f32 = jnp.float32
VMEM_LIMIT = 16 * 1024 * 1024
PACK_LIMIT = 60 * 1024 * 1024


def dot(a, b, dims):
    return lax.dot_general(a, b, (dims, ((), ())), preferred_element_type=f32)


def exchange(values, axis, groups=None):
    return lax.all_to_all(
        values, axis, split_axis=0, concat_axis=0, tiled=True, axis_index_groups=groups
    )


def pick(table, row_ids):
    local_ids = jnp.arange(table.shape[0], dtype=jnp.int32)
    chosen = (row_ids[:, None] == local_ids[None, :]).astype(table.dtype)
    return dot(chosen, table, ((1,), (0,))).astype(table.dtype)


def quarters(first, second):
    half = first.shape[1] // 2
    parts = [first[:, :half], first[:, half:], second[:, :half], second[:, half:]]
    return jnp.concatenate(parts, axis=0).astype(bf16)


def near_index(device, na, nb):
    return device // (na * nb) * nb + device % nb


def where_am_i():
    return lax.axis_index("node"), lax.axis_index("feat")


def pack_kernel(
    ids_hbm,
    slots_hbm,
    counts_hbm,
    blocks_hbm,
    features_hbm,
    tiles_hbm,
    grad_hbm,
    sent_hbm,
    ids_ref,
    slots_ref,
    counts_ref,
    blocks_ref,
    features_ref,
    tiles_ref,
    grad_ref,
    sent_ref,
    slots_scratch,
    grad_scratch,
    sems,
    out_sems,
    *,
    nx,
    na,
    nb,
    place,
):
    copies = [
        pltpu.make_async_copy(source, target, sems.at[n])
        for n, (source, target) in enumerate(
            [
                (ids_hbm, ids_ref),
                (slots_hbm, slots_ref),
                (counts_hbm, counts_ref),
                (blocks_hbm, blocks_ref),
                (features_hbm, features_ref),
                (tiles_hbm, tiles_ref),
                (grad_hbm, grad_ref),
            ]
        )
    ]
    for copy in copies:
        copy.start()
    for copy in copies:
        copy.wait()
    device, feat = place()
    near = nx * nb
    capacity, nodes = ids_ref.shape
    locals_, width = features_ref.shape
    count, targets, _ = tiles_ref.shape
    part = sent_ref.shape[1] - na * capacity - na - 8
    part = part // count
    lanes = targets // capacity
    near_at = near_index(device, na, nb)

    used = lax.broadcasted_iota(jnp.int32, (capacity, nodes), 0) < counts_ref[pl.ds(device, 1), :]
    slots = jnp.where(used, slots_ref[...], targets).astype(f32)
    slots = jnp.concatenate([slots] * lanes, axis=0)
    slots = jnp.concatenate([slots, jnp.zeros((targets, targets - nodes), f32)], axis=1).T
    group = lax.broadcasted_iota(jnp.int32, (targets, targets), 1) // capacity
    slots_scratch[...] = jnp.where(group == near_at % lanes, slots, 0.0)
    grad_scratch[...] = grad_ref[...].astype(f32).T
    grad_t = grad_scratch[pl.ds(pl.multiple_of(feat * part, part), part), :].astype(bf16)
    terms = [dot(grad_t, tiles_ref[k], ((1,), (0,))) for k in range(count)]
    blocks = [blocks_ref[0, k] for k in range(count)]
    row = lax.broadcasted_iota(jnp.int32, (8, targets), 0)
    far_rows = jnp.zeros((8, targets), jnp.int32)
    for k in range(count):
        far_rows = jnp.where(row == k, blocks[k] % (na * nb) // nb, far_rows)
        far_rows = jnp.where(row == count + k, blocks[k] // (na * nb) * nb + blocks[k] % nb, far_rows)
    far_rows = far_rows.astype(f32)
    local_ids = lax.broadcasted_iota(jnp.int32, (capacity, locals_), 1)
    outs = []
    for x in range(nx):
        for b in range(nb):
            to = x * nb + b
            owners = [(x * na + a) * nb + b for a in range(na)]
            chosen = jnp.concatenate(
                [jnp.where(ids_ref[:, o : o + 1] == local_ids, 1.0, 0.0).astype(bf16) for o in owners],
                axis=0,
            )
            rows = dot(chosen, features_ref[...], ((1,), (0,)))
            sent_ref[to, : na * capacity, :] = rows.astype(bf16)
            at = na * capacity
            for k in range(count):
                there = blocks[k] // (na * nb) * nb + blocks[k] % nb == to
                term = jnp.where(there, terms[k], 0.0)
                sent_ref[to, at : at + part, :] = term.astype(bf16)
                at += part
            slot_rows = slots_scratch[pl.ds(owners[0], na, stride=nb), :]
            sent_ref[to, at : at + na + 8, :] = jnp.concatenate([slot_rows, far_rows], 0).astype(bf16)
            out = pltpu.make_async_copy(sent_ref.at[to], sent_hbm.at[to], out_sems.at[to])
            out.start()
            outs.append(out)
    for out in outs:
        out.wait()


def pack(sample_ids, dest_slots, counts, blocks, features, tiles, grad, nx, na, nb, part, place):
    count, targets, _ = tiles.shape
    capacity, nodes = sample_ids.shape
    total = na * capacity + count * part + na + 8
    kernel = functools.partial(pack_kernel, nx=nx, na=na, nb=nb, place=place)
    args = (sample_ids, dest_slots, counts, blocks, features, tiles, grad)
    held = [pltpu.VMEM(arg.shape, arg.dtype) for arg in args]
    held[3] = pltpu.SMEM(blocks.shape, blocks.dtype)
    return pl.pallas_call(
        kernel,
        out_shape=jax.ShapeDtypeStruct((nx * nb, total, features.shape[1]), bf16),
        in_specs=[pl.BlockSpec(memory_space=pltpu.HBM)] * len(args),
        out_specs=pl.BlockSpec(memory_space=pltpu.HBM),
        scratch_shapes=held
        + [
            pltpu.VMEM((nx * nb, total, features.shape[1]), bf16),
            pltpu.VMEM((targets, targets), f32),
            pltpu.VMEM((grad.shape[1], targets), f32),
            pltpu.SemaphoreType.DMA((len(args),)),
            pltpu.SemaphoreType.DMA((nx * nb,)),
        ],
        compiler_params=pltpu.CompilerParams(vmem_limit_bytes=PACK_LIMIT),
    )(*args)


def in_vmem(kernel, out_shape, *args, scratch_shapes=()):
    vmem = pl.BlockSpec(memory_space=pltpu.VMEM)
    many = isinstance(out_shape, (list, tuple))
    return pl.pallas_call(
        kernel,
        out_shape=out_shape,
        in_specs=[vmem] * len(args),
        out_specs=[vmem] * len(out_shape) if many else vmem,
        scratch_shapes=scratch_shapes,
        compiler_params=pltpu.CompilerParams(vmem_limit_bytes=VMEM_LIMIT),
    )(*args)


def halve(values):
    high = values.astype(bf16)
    return high, (values - high.astype(f32)).astype(bf16)


def gather_kernel(got_ref, sent_ref, marks_ref, *, capacity, part, count):
    near = got_ref.shape[0]
    far, _, targets = sent_ref.shape
    lanes = targets // capacity
    at = far * capacity + count * part
    marks = [got_ref[n, at : at + far + 8, :].astype(f32) for n in range(near)]
    for n in range(near):
        marks_ref[n] = got_ref[n, at : at + far + 8, :]
    slots = [sum(marks[h : h + lanes])[:far] for h in range(0, near, lanes)]
    nodes = lax.broadcasted_iota(jnp.int32, (targets, targets), 0).astype(f32)
    ones = jnp.ones((8, targets), bf16)
    back = [jnp.zeros((part, targets), f32) for _ in range(far)]
    for n in range(near):
        for k in range(count):
            start = far * capacity + k * part
            term = got_ref[n, start : start + part, :].astype(f32)
            mark = jnp.broadcast_to(marks[n][far + k : far + k + 1, :], (part, targets))
            back = [back[a] + jnp.where(mark == float(a), term, 0.0) for a in range(far)]
    for a in range(far):
        total = jnp.zeros((targets, targets), f32)
        degree = jnp.zeros((8, targets), f32)
        for h in range(near // lanes):
            chosen = jnp.where(slots[h][a : a + 1, :] == nodes, 1.0, 0.0).astype(bf16)
            rows = [
                got_ref[h * lanes + n, a * capacity : (a + 1) * capacity, :] for n in range(lanes)
            ]
            total += dot(chosen, jnp.concatenate(rows, axis=0), ((1,), (0,)))
            degree += dot(ones, chosen, ((1,), (1,)))
        sent_ref[a] = jnp.concatenate([total, back[a], degree], axis=0).astype(bf16)


def first_kernel(came_ref, rows_ref, self_ref, other_ref, sent_ref, mean_ref, *, part):
    targets = rows_ref.shape[0]
    came = came_ref[0].astype(f32)
    for a in range(1, came_ref.shape[0]):
        came += came_ref[a].astype(f32)
    degree = jnp.broadcast_to(came[targets + part : targets + part + 1, :], (targets, targets)).T
    high, low = halve(came[:targets] / (degree + 1.0))
    mean_ref[...] = high
    pre = dot(rows_ref[...], self_ref[...], ((1,), (0,)))
    pre += dot(high, other_ref[...], ((1,), (0,)))
    pre += dot(low, other_ref[...], ((1,), (0,)))
    back = halve(came[targets : targets + part])
    all_rows = jnp.concatenate([pre.T.astype(bf16), *back], axis=0)
    for f in range(sent_ref.shape[0]):
        sent_ref[f] = all_rows


def grads_kernel(
    got_ref,
    self_grad_ref,
    other_ref,
    grad_ref,
    rows_ref,
    mean_ref,
    sent_ref,
    hidden_ref,
    mine_ref,
    scratch,
    *,
    part,
    slice_at,
):
    feats, near = got_ref.shape[0], sent_ref.shape[0]
    hidden = self_grad_ref.shape[0]
    pre = got_ref[0, :hidden, :].astype(f32)
    for f in range(1, feats):
        pre += got_ref[f, :hidden, :].astype(f32)
    sigma = 1.0 / (1.0 + jnp.exp(-pre))
    slope = sigma * (1.0 + pre * (1.0 - sigma))
    scratch[...] = pre * sigma
    hidden_ref[...] = scratch[...].astype(bf16)
    mine = scratch[pl.ds(pl.multiple_of(slice_at() * part, part), part), :].astype(bf16)
    mine_ref[...] = mine
    back_high = [got_ref[f, hidden : hidden + part, :] for f in range(feats)]
    back_high = jnp.concatenate(back_high, axis=0)
    back_low = [got_ref[f, hidden + part :, :] for f in range(feats)]
    back_low = jnp.concatenate(back_low, axis=0)
    grad = self_grad_ref[...] + dot(other_ref[...], back_high, ((1,), (0,)))
    grad += dot(other_ref[...], back_low, ((1,), (0,)))
    grad = (grad * slope).astype(bf16)
    rows_t = rows_ref[...].astype(f32).T.astype(bf16)
    mean_t = mean_ref[...].astype(f32).T.astype(bf16)
    lower = quarters(dot(rows_t, grad, ((1,), (1,))), dot(mean_t, grad, ((1,), (1,))))
    upper = quarters(
        dot(mine, grad_ref[...], ((1,), (0,))),
        dot(mine, back_high, ((1,), (1,))) + dot(mine, back_low, ((1,), (1,))),
    )
    rows_each, share = lower.shape[0] // near, upper.shape[0] // near
    for n in range(near):
        sent_ref[n, :rows_each, :] = lower[n * rows_each : (n + 1) * rows_each]
        sent_ref[n, rows_each:, :] = upper[n * share : (n + 1) * share]


def far_kernel(got_ref, hidden_ref, sent_ref):
    total = got_ref[0].astype(f32)
    for n in range(1, got_ref.shape[0]):
        total += got_ref[n].astype(f32)
    total = total.astype(bf16)
    sums = total.shape[0]
    for a in range(sent_ref.shape[0]):
        sent_ref[a, :sums, :] = total
        sent_ref[a, sums:, :] = hidden_ref[...]


def near_kernel(got_ref, marks_ref, sent_ref, *, sums, part, count, where):
    far = got_ref.shape[0]
    total = got_ref[0, :sums, :].astype(f32)
    for a in range(1, far):
        total += got_ref[a, :sums, :].astype(f32)
    total = total.astype(bf16)
    here = where().astype(f32)
    blocks = [got_ref[a, sums:, :].astype(f32) for a in range(far)]
    for n in range(sent_ref.shape[0]):
        sent_ref[n, :sums, :] = total
        marks = marks_ref[n].astype(f32)
        for k in range(count):
            mark = jnp.where(marks[far + count + k :][:1] == here, marks[far + k :][:1], -1.0)
            mark = jnp.broadcast_to(mark, blocks[0].shape)
            block = jnp.zeros_like(blocks[0])
            for a in range(far):
                block = jnp.where(mark == float(a), blocks[a], block)
            at = sums + k * part
            sent_ref[n, at : at + part, :] = block.astype(bf16)


def second_kernel(got_ref, tiles_ref, sent_ref, *, rows_each, share, part):
    near = got_ref.shape[0]
    agg = jnp.zeros((part, tiles_ref.shape[1]), f32)
    for k in range(tiles_ref.shape[0]):
        at = rows_each + share + k * part
        block = got_ref[0, at : at + part, :].astype(f32)
        for n in range(1, near):
            block += got_ref[n, at : at + part, :].astype(f32)
        agg += dot(block.astype(bf16), tiles_ref[k], ((1,), (1,)))
    rows = [got_ref[n, rows_each : rows_each + share, :] for n in range(near)]
    both = jnp.concatenate([agg.astype(bf16)] + rows, axis=0)
    for f in range(sent_ref.shape[0]):
        sent_ref[f] = both


def last_kernel(
    got_ref,
    hidden_ref,
    self_ref,
    other_ref,
    lower_ref,
    out_ref,
    low_first_ref,
    low_second_ref,
    first_ref,
    second_ref,
    *,
    part,
    rows_each,
):
    feats = got_ref.shape[0]
    half = first_ref.shape[1] // 2
    agg = jnp.concatenate([got_ref[f, :part, :] for f in range(feats)], axis=0)
    out = dot(hidden_ref[...], self_ref[...], ((0,), (0,))) + dot(agg, other_ref[...], ((0,), (0,)))
    out_ref[...] = out.astype(bf16)
    for f in range(feats):
        at = f * part
        for n, ref in enumerate([first_ref, second_ref]):
            start = part * (1 + 2 * n)
            ref[at : at + part, :half] = got_ref[f, start : start + part, :].astype(f32)
            ref[at : at + part, half:] = got_ref[f, start + part : start + 2 * part, :].astype(f32)
    width = low_first_ref.shape[0]
    for n in range(lower_ref.shape[0]):
        quarter, at = divmod(n * rows_each, width)
        ref = (low_first_ref, low_second_ref)[quarter // 2]
        left = quarter % 2 * half
        rows = lower_ref[n, :rows_each, :].astype(f32)
        ref[at : at + rows_each, left : left + half] = rows


def shards(
    features,
    self_one,
    neighbour_one,
    sample_ids,
    dest_slots,
    send_counts,
    self_ids,
    tile_blocks,
    tile_weights,
    self_two,
    neighbour_two,
    out_grad,
):
    feats = lax.axis_size("feat")
    nodes = lax.axis_size("node")
    nx, nb = 4, 2
    na = nodes // (nx * nb)
    near = nx * nb
    near_ids = [(x * na + a) * nb + b for a in range(na) for x in range(nx) for b in range(nb)]
    near_groups = [near_ids[a * near : (a + 1) * near] for a in range(na)]
    far_groups = [list(group) for group in zip(*near_groups)]
    capacity = sample_ids.shape[2]
    targets = self_ids.shape[1]
    width = features.shape[1]
    hidden = neighbour_one.shape[1]
    part = hidden // feats
    tiles = tile_weights[0]
    count = tiles.shape[0]

    sent = pack(
        sample_ids[0].T,
        dest_slots[0].T,
        send_counts,
        tile_blocks,
        features,
        tiles,
        out_grad,
        nx,
        na,
        nb,
        part,
        where_am_i,
    )
    got = exchange(sent, "node", near_groups)

    sent, marks = in_vmem(
        functools.partial(gather_kernel, capacity=capacity, part=part, count=count),
        [
            jax.ShapeDtypeStruct((na, targets + part + 8, width), bf16),
            jax.ShapeDtypeStruct((near, na + 8, targets), bf16),
        ],
        got,
    )
    came = exchange(sent, "node", far_groups)

    self_rows = pick(features, self_ids[0])
    sent, mean_high = in_vmem(
        functools.partial(first_kernel, part=part),
        [
            jax.ShapeDtypeStruct((feats, hidden + 2 * part, targets), bf16),
            jax.ShapeDtypeStruct((targets, width), bf16),
        ],
        came,
        self_rows,
        self_one,
        neighbour_one,
    )
    got = exchange(sent, "feat")

    half = hidden // 2
    rows_each, share = 4 * width // near, 4 * part // near
    sent, hidden_t, hidden_part = in_vmem(
        functools.partial(grads_kernel, part=part, slice_at=lambda: lax.axis_index("feat")),
        [
            jax.ShapeDtypeStruct((near, rows_each + share, half), bf16),
            jax.ShapeDtypeStruct((hidden, targets), bf16),
            jax.ShapeDtypeStruct((part, targets), bf16),
        ],
        got,
        dot(self_two, out_grad, ((1,), (1,))),
        neighbour_two,
        out_grad,
        self_rows,
        mean_high,
        scratch_shapes=[pltpu.VMEM((hidden, targets), f32)],
    )
    got = exchange(sent, "node", near_groups)
    sent = in_vmem(
        far_kernel,
        jax.ShapeDtypeStruct((na, rows_each + share + part, half), bf16),
        got,
        hidden_part,
    )
    got = exchange(sent, "node", far_groups)
    sums = rows_each + share
    sent = in_vmem(
        functools.partial(
            near_kernel,
            sums=sums,
            part=part,
            count=count,
            where=lambda: near_index(lax.axis_index("node"), na, nb),
        ),
        jax.ShapeDtypeStruct((near, sums + count * part, half), bf16),
        got,
        marks,
    )
    got = exchange(sent, "node", near_groups)
    lower = got

    sent = in_vmem(
        functools.partial(second_kernel, rows_each=rows_each, share=share, part=part),
        jax.ShapeDtypeStruct((feats, part + near * share, targets), bf16),
        got,
        tiles,
    )
    got = exchange(sent, "feat")
    return in_vmem(
        functools.partial(last_kernel, part=part, rows_each=rows_each),
        [
            jax.ShapeDtypeStruct((targets, hidden), bf16),
            jax.ShapeDtypeStruct((width, hidden), f32),
            jax.ShapeDtypeStruct((width, hidden), f32),
            jax.ShapeDtypeStruct((hidden, hidden), f32),
            jax.ShapeDtypeStruct((hidden, hidden), f32),
        ],
        got,
        hidden_t,
        self_two,
        neighbour_two,
        lower,
    )


def solution(mesh):
    placed = (
        P("node", "feat"),
        P("feat", None),
        P("feat", None),
        P("node", None, None),
        P("node", None, None),
        P(),
        P("node", None),
        P("node", None),
        P("node", None, None, None),
        P(),
        P(),
        P("node", None),
    )
    return jax.shard_map(
        shards,
        mesh=mesh,
        in_specs=placed,
        out_specs=(P("node", None), P("feat", None), P("feat", None), P(), P()),
        check_vma=False,
    )
```

```python
import functools

import jax
import jax.numpy as jnp
from jax import lax
from jax.experimental import pallas as pl
from jax.experimental.pallas import tpu as pltpu
from jax.sharding import PartitionSpec as P

bf16 = jnp.bfloat16
f32 = jnp.float32
VMEM_LIMIT = 16 * 1024 * 1024
PACK_LIMIT = 60 * 1024 * 1024


def dot(a, b, dims):
    return lax.dot_general(a, b, (dims, ((), ())), preferred_element_type=f32)


def exchange(values, axis, groups=None):
    return lax.all_to_all(
        values, axis, split_axis=0, concat_axis=0, tiled=True, axis_index_groups=groups
    )


def pick(table, row_ids):
    local_ids = jnp.arange(table.shape[0], dtype=jnp.int32)
    chosen = (row_ids[:, None] == local_ids[None, :]).astype(table.dtype)
    return dot(chosen, table, ((1,), (0,))).astype(table.dtype)


def quarters(first, second):
    half = first.shape[1] // 2
    parts = [first[:, :half], first[:, half:], second[:, :half], second[:, half:]]
    return jnp.concatenate(parts, axis=0).astype(bf16)


def near_index(device, na, nb):
    return device // (na * nb) * nb + device % nb


def where_am_i():
    return lax.axis_index("node"), lax.axis_index("feat")


def pack_kernel(
    ids_hbm,
    slots_hbm,
    counts_hbm,
    blocks_hbm,
    features_hbm,
    tiles_hbm,
    grad_hbm,
    sent_hbm,
    ids_ref,
    slots_ref,
    counts_ref,
    blocks_ref,
    features_ref,
    tiles_ref,
    grad_ref,
    sent_ref,
    slots_scratch,
    grad_scratch,
    sems,
    out_sems,
    *,
    nx,
    na,
    nb,
    place,
):
    copies = [
        pltpu.make_async_copy(source, target, sems.at[n])
        for n, (source, target) in enumerate(
            [
                (ids_hbm, ids_ref),
                (slots_hbm, slots_ref),
                (counts_hbm, counts_ref),
                (blocks_hbm, blocks_ref),
                (features_hbm, features_ref),
                (tiles_hbm, tiles_ref),
                (grad_hbm, grad_ref),
            ]
        )
    ]
    for copy in copies:
        copy.start()
    for copy in copies:
        copy.wait()
    device, feat = place()
    near = nx * nb
    capacity, nodes = ids_ref.shape
    locals_, width = features_ref.shape
    count, targets, _ = tiles_ref.shape
    part = sent_ref.shape[1] - na * capacity - na - 8
    part = part // count
    lanes = targets // capacity
    near_at = near_index(device, na, nb)

    used = lax.broadcasted_iota(jnp.int32, (capacity, nodes), 0) < counts_ref[pl.ds(device, 1), :]
    slots = jnp.where(used, slots_ref[...], targets).astype(f32)
    slots = jnp.concatenate([slots] * lanes, axis=0)
    slots = jnp.concatenate([slots, jnp.zeros((targets, targets - nodes), f32)], axis=1).T
    group = lax.broadcasted_iota(jnp.int32, (targets, targets), 1) // capacity
    slots_scratch[...] = jnp.where(group == near_at % lanes, slots, 0.0)
    grad_scratch[...] = grad_ref[...].astype(f32).T
    grad_t = grad_scratch[pl.ds(pl.multiple_of(feat * part, part), part), :].astype(bf16)
    terms = [dot(grad_t, tiles_ref[k], ((1,), (0,))) for k in range(count)]
    blocks = [blocks_ref[0, k] for k in range(count)]
    row = lax.broadcasted_iota(jnp.int32, (8, targets), 0)
    far_rows = jnp.zeros((8, targets), jnp.int32)
    for k in range(count):
        far_rows = jnp.where(row == k, blocks[k] % (na * nb) // nb, far_rows)
        far_rows = jnp.where(row == count + k, blocks[k] // (na * nb) * nb + blocks[k] % nb, far_rows)
    far_rows = far_rows.astype(f32)
    local_ids = lax.broadcasted_iota(jnp.int32, (capacity, locals_), 1)
    outs = []
    for x in range(nx):
        for b in range(nb):
            to = x * nb + b
            owners = [(x * na + a) * nb + b for a in range(na)]
            chosen = jnp.concatenate(
                [jnp.where(ids_ref[:, o : o + 1] == local_ids, 1.0, 0.0).astype(bf16) for o in owners],
                axis=0,
            )
            rows = dot(chosen, features_ref[...], ((1,), (0,)))
            sent_ref[to, : na * capacity, :] = rows.astype(bf16)
            at = na * capacity
            for k in range(count):
                there = blocks[k] // (na * nb) * nb + blocks[k] % nb == to
                term = jnp.where(there, terms[k], 0.0)
                sent_ref[to, at : at + part, :] = term.astype(bf16)
                at += part
            slot_rows = slots_scratch[pl.ds(owners[0], na, stride=nb), :]
            sent_ref[to, at : at + na + 8, :] = jnp.concatenate([slot_rows, far_rows], 0).astype(bf16)
            out = pltpu.make_async_copy(sent_ref.at[to], sent_hbm.at[to], out_sems.at[to])
            out.start()
            outs.append(out)
    for out in outs:
        out.wait()


def pack(sample_ids, dest_slots, counts, blocks, features, tiles, grad, nx, na, nb, part, place):
    count, targets, _ = tiles.shape
    capacity, nodes = sample_ids.shape
    total = na * capacity + count * part + na + 8
    kernel = functools.partial(pack_kernel, nx=nx, na=na, nb=nb, place=place)
    args = (sample_ids, dest_slots, counts, blocks, features, tiles, grad)
    held = [pltpu.VMEM(arg.shape, arg.dtype) for arg in args]
    held[3] = pltpu.SMEM(blocks.shape, blocks.dtype)
    return pl.pallas_call(
        kernel,
        out_shape=jax.ShapeDtypeStruct((nx * nb, total, features.shape[1]), bf16),
        in_specs=[pl.BlockSpec(memory_space=pltpu.HBM)] * len(args),
        out_specs=pl.BlockSpec(memory_space=pltpu.HBM),
        scratch_shapes=held
        + [
            pltpu.VMEM((nx * nb, total, features.shape[1]), bf16),
            pltpu.VMEM((targets, targets), f32),
            pltpu.VMEM((grad.shape[1], targets), f32),
            pltpu.SemaphoreType.DMA((len(args),)),
            pltpu.SemaphoreType.DMA((nx * nb,)),
        ],
        compiler_params=pltpu.CompilerParams(vmem_limit_bytes=PACK_LIMIT),
    )(*args)


def in_vmem(kernel, out_shape, *args, scratch_shapes=()):
    vmem = pl.BlockSpec(memory_space=pltpu.VMEM)
    many = isinstance(out_shape, (list, tuple))
    return pl.pallas_call(
        kernel,
        out_shape=out_shape,
        in_specs=[vmem] * len(args),
        out_specs=[vmem] * len(out_shape) if many else vmem,
        scratch_shapes=scratch_shapes,
        compiler_params=pltpu.CompilerParams(vmem_limit_bytes=VMEM_LIMIT),
    )(*args)


def halve(values):
    high = values.astype(bf16)
    return high, (values - high.astype(f32)).astype(bf16)


def gather_kernel(
    got_ref, rows_ref, sent_ref, marks_ref, rows_t_ref, *, capacity, part, count
):
    rows_t_ref[...] = rows_ref[...].astype(f32).T.astype(bf16)
    near = got_ref.shape[0]
    far, _, targets = sent_ref.shape
    lanes = targets // capacity
    at = far * capacity + count * part
    marks = [got_ref[n, at : at + far + 8, :].astype(f32) for n in range(near)]
    for n in range(near):
        marks_ref[n] = got_ref[n, at : at + far + 8, :]
    slots = [sum(marks[h : h + lanes])[:far] for h in range(0, near, lanes)]
    nodes = lax.broadcasted_iota(jnp.int32, (targets, targets), 0).astype(f32)
    ones = jnp.ones((8, targets), bf16)
    back = [jnp.zeros((part, targets), f32) for _ in range(far)]
    for n in range(near):
        for k in range(count):
            start = far * capacity + k * part
            term = got_ref[n, start : start + part, :].astype(f32)
            mark = jnp.broadcast_to(marks[n][far + k : far + k + 1, :], (part, targets))
            back = [back[a] + jnp.where(mark == float(a), term, 0.0) for a in range(far)]
    for a in range(far):
        total = jnp.zeros((targets, targets), f32)
        degree = jnp.zeros((8, targets), f32)
        for h in range(near // lanes):
            chosen = jnp.where(slots[h][a : a + 1, :] == nodes, 1.0, 0.0).astype(bf16)
            rows = [
                got_ref[h * lanes + n, a * capacity : (a + 1) * capacity, :] for n in range(lanes)
            ]
            total += dot(chosen, jnp.concatenate(rows, axis=0), ((1,), (0,)))
            degree += dot(ones, chosen, ((1,), (1,)))
        sent_ref[a] = jnp.concatenate([total, back[a], degree], axis=0).astype(bf16)


def first_kernel(came_ref, rows_ref, self_ref, other_ref, sent_ref, mean_ref, *, part):
    targets = rows_ref.shape[0]
    came = came_ref[0].astype(f32)
    for a in range(1, came_ref.shape[0]):
        came += came_ref[a].astype(f32)
    degree = jnp.broadcast_to(came[targets + part : targets + part + 1, :], (targets, targets)).T
    high, low = halve(came[:targets] / (degree + 1.0))
    mean_ref[...] = high
    pre = dot(rows_ref[...], self_ref[...], ((1,), (0,)))
    pre += dot(high, other_ref[...], ((1,), (0,)))
    pre += dot(low, other_ref[...], ((1,), (0,)))
    back = halve(came[targets : targets + part])
    sent_ref[...] = jnp.concatenate([pre.T.astype(bf16), *back], axis=0)


def grads_kernel(
    got_ref,
    self_ref,
    other_ref,
    grad_ref,
    rows_t_ref,
    mean_ref,
    sent_ref,
    hidden_ref,
    mine_ref,
    scratch,
    *,
    part,
    slice_at,
):
    feats, near = got_ref.shape[0], sent_ref.shape[0]
    hidden = self_ref.shape[0]
    pre = got_ref[0, :hidden, :].astype(f32)
    for f in range(1, feats):
        pre += got_ref[f, :hidden, :].astype(f32)
    sigma = 1.0 / (1.0 + jnp.exp(-pre))
    slope = sigma * (1.0 + pre * (1.0 - sigma))
    scratch[...] = pre * sigma
    hidden_ref[...] = scratch[...].astype(bf16)
    mine = scratch[pl.ds(pl.multiple_of(slice_at() * part, part), part), :].astype(bf16)
    mine_ref[...] = mine
    back_high = [got_ref[f, hidden : hidden + part, :] for f in range(feats)]
    back_high = jnp.concatenate(back_high, axis=0)
    back_low = [got_ref[f, hidden + part :, :] for f in range(feats)]
    back_low = jnp.concatenate(back_low, axis=0)
    grad = dot(self_ref[...], grad_ref[...], ((1,), (1,)))
    grad += dot(other_ref[...], back_high, ((1,), (0,)))
    grad += dot(other_ref[...], back_low, ((1,), (0,)))
    grad = (grad * slope).astype(bf16)
    mean_t = mean_ref[...].astype(f32).T.astype(bf16)
    lower = quarters(dot(rows_t_ref[...], grad, ((1,), (1,))), dot(mean_t, grad, ((1,), (1,))))
    upper = quarters(
        dot(mine, grad_ref[...], ((1,), (0,))),
        dot(mine, back_high, ((1,), (1,))) + dot(mine, back_low, ((1,), (1,))),
    )
    rows_each, share = lower.shape[0] // near, upper.shape[0] // near
    for n in range(near):
        sent_ref[n, :rows_each, :] = lower[n * rows_each : (n + 1) * rows_each]
        sent_ref[n, rows_each:, :] = upper[n * share : (n + 1) * share]


def far_kernel(got_ref, hidden_ref, sent_ref):
    total = got_ref[0].astype(f32)
    for n in range(1, got_ref.shape[0]):
        total += got_ref[n].astype(f32)
    total = total.astype(bf16)
    sums = total.shape[0]
    for a in range(sent_ref.shape[0]):
        sent_ref[a, :sums, :] = total
        sent_ref[a, sums:, :] = hidden_ref[...]


def near_kernel(got_ref, marks_ref, sent_ref, *, sums, part, count, where):
    far = got_ref.shape[0]
    total = got_ref[0, :sums, :].astype(f32)
    for a in range(1, far):
        total += got_ref[a, :sums, :].astype(f32)
    total = total.astype(bf16)
    here = where().astype(f32)
    blocks = [got_ref[a, sums:, :].astype(f32) for a in range(far)]
    for n in range(sent_ref.shape[0]):
        sent_ref[n, :sums, :] = total
        marks = marks_ref[n].astype(f32)
        for k in range(count):
            mark = jnp.where(marks[far + count + k :][:1] == here, marks[far + k :][:1], -1.0)
            mark = jnp.broadcast_to(mark, blocks[0].shape)
            block = jnp.zeros_like(blocks[0])
            for a in range(far):
                block = jnp.where(mark == float(a), blocks[a], block)
            at = sums + k * part
            sent_ref[n, at : at + part, :] = block.astype(bf16)


def second_kernel(got_ref, tiles_ref, sent_ref, *, rows_each, share, part):
    near = got_ref.shape[0]
    agg = jnp.zeros((part, tiles_ref.shape[1]), f32)
    for k in range(tiles_ref.shape[0]):
        at = rows_each + share + k * part
        block = got_ref[0, at : at + part, :].astype(f32)
        for n in range(1, near):
            block += got_ref[n, at : at + part, :].astype(f32)
        agg += dot(block.astype(bf16), tiles_ref[k], ((1,), (1,)))
    rows = [got_ref[n, rows_each : rows_each + share, :] for n in range(near)]
    both = jnp.concatenate([agg.astype(bf16)] + rows, axis=0)
    for f in range(sent_ref.shape[0]):
        sent_ref[f] = both


def last_kernel(
    got_ref,
    hidden_ref,
    self_ref,
    other_ref,
    lower_ref,
    out_ref,
    low_first_ref,
    low_second_ref,
    first_ref,
    second_ref,
    *,
    part,
    rows_each,
):
    feats = got_ref.shape[0]
    half = first_ref.shape[1] // 2
    agg = jnp.concatenate([got_ref[f, :part, :] for f in range(feats)], axis=0)
    out = dot(hidden_ref[...], self_ref[...], ((0,), (0,))) + dot(agg, other_ref[...], ((0,), (0,)))
    out_ref[...] = out.astype(bf16)
    for f in range(feats):
        at = f * part
        for n, ref in enumerate([first_ref, second_ref]):
            start = part * (1 + 2 * n)
            ref[at : at + part, :half] = got_ref[f, start : start + part, :].astype(f32)
            ref[at : at + part, half:] = got_ref[f, start + part : start + 2 * part, :].astype(f32)
    width = low_first_ref.shape[0]
    for n in range(lower_ref.shape[0]):
        quarter, at = divmod(n * rows_each, width)
        ref = (low_first_ref, low_second_ref)[quarter // 2]
        left = quarter % 2 * half
        rows = lower_ref[n, :rows_each, :].astype(f32)
        ref[at : at + rows_each, left : left + half] = rows


def shards(
    features,
    self_one,
    neighbour_one,
    sample_ids,
    dest_slots,
    send_counts,
    self_ids,
    tile_blocks,
    tile_weights,
    self_two,
    neighbour_two,
    out_grad,
):
    feats = lax.axis_size("feat")
    nodes = lax.axis_size("node")
    nx, nb = 4, 2
    na = nodes // (nx * nb)
    near = nx * nb
    near_ids = [(x * na + a) * nb + b for a in range(na) for x in range(nx) for b in range(nb)]
    near_groups = [near_ids[a * near : (a + 1) * near] for a in range(na)]
    far_groups = [list(group) for group in zip(*near_groups)]
    capacity = sample_ids.shape[2]
    targets = self_ids.shape[1]
    width = features.shape[1]
    hidden = neighbour_one.shape[1]
    part = hidden // feats
    tiles = tile_weights[0]
    count = tiles.shape[0]

    sent = pack(
        sample_ids[0].T,
        dest_slots[0].T,
        send_counts,
        tile_blocks,
        features,
        tiles,
        out_grad,
        nx,
        na,
        nb,
        part,
        where_am_i,
    )
    got = exchange(sent, "node", near_groups)
    self_rows = pick(features, self_ids[0])

    sent, marks, self_rows_t = in_vmem(
        functools.partial(gather_kernel, capacity=capacity, part=part, count=count),
        [
            jax.ShapeDtypeStruct((na, targets + part + 8, width), bf16),
            jax.ShapeDtypeStruct((near, na + 8, targets), bf16),
            jax.ShapeDtypeStruct((width, targets), bf16),
        ],
        got,
        self_rows,
    )
    came = exchange(sent, "node", far_groups)

    sent, mean_high = in_vmem(
        functools.partial(first_kernel, part=part),
        [
            jax.ShapeDtypeStruct((hidden + 2 * part, targets), bf16),
            jax.ShapeDtypeStruct((targets, width), bf16),
        ],
        came,
        self_rows,
        self_one,
        neighbour_one,
    )
    got = lax.all_gather(sent, "feat")

    half = hidden // 2
    rows_each, share = 4 * width // near, 4 * part // near
    sent, hidden_t, hidden_part = in_vmem(
        functools.partial(grads_kernel, part=part, slice_at=lambda: lax.axis_index("feat")),
        [
            jax.ShapeDtypeStruct((near, rows_each + share, half), bf16),
            jax.ShapeDtypeStruct((hidden, targets), bf16),
            jax.ShapeDtypeStruct((part, targets), bf16),
        ],
        got,
        self_two,
        neighbour_two,
        out_grad,
        self_rows_t,
        mean_high,
        scratch_shapes=[pltpu.VMEM((hidden, targets), f32)],
    )
    got = exchange(sent, "node", near_groups)
    sent = in_vmem(
        far_kernel,
        jax.ShapeDtypeStruct((na, rows_each + share + part, half), bf16),
        got,
        hidden_part,
    )
    got = exchange(sent, "node", far_groups)
    sums = rows_each + share
    sent = in_vmem(
        functools.partial(
            near_kernel,
            sums=sums,
            part=part,
            count=count,
            where=lambda: near_index(lax.axis_index("node"), na, nb),
        ),
        jax.ShapeDtypeStruct((near, sums + count * part, half), bf16),
        got,
        marks,
    )
    got = exchange(sent, "node", near_groups)
    lower = got

    sent = in_vmem(
        functools.partial(second_kernel, rows_each=rows_each, share=share, part=part),
        jax.ShapeDtypeStruct((feats, part + near * share, targets), bf16),
        got,
        tiles,
    )
    got = exchange(sent, "feat")
    return in_vmem(
        functools.partial(last_kernel, part=part, rows_each=rows_each),
        [
            jax.ShapeDtypeStruct((targets, hidden), bf16),
            jax.ShapeDtypeStruct((width, hidden), f32),
            jax.ShapeDtypeStruct((width, hidden), f32),
            jax.ShapeDtypeStruct((hidden, hidden), f32),
            jax.ShapeDtypeStruct((hidden, hidden), f32),
        ],
        got,
        hidden_t,
        self_two,
        neighbour_two,
        lower,
    )


def solution(mesh):
    placed = (
        P("node", "feat"),
        P("feat", None),
        P("feat", None),
        P("node", None, None),
        P("node", None, None),
        P(),
        P("node", None),
        P("node", None),
        P("node", None, None, None),
        P(),
        P(),
        P("node", None),
    )
    return jax.shard_map(
        shards,
        mesh=mesh,
        in_specs=placed,
        out_specs=(P("node", None), P("feat", None), P("feat", None), P(), P()),
        check_vma=False,
    )
```

```python
import functools

import jax
import jax.numpy as jnp
from jax import lax
from jax.experimental import pallas as pl
from jax.experimental.pallas import tpu as pltpu
from jax.sharding import PartitionSpec as P

bf16 = jnp.bfloat16
f32 = jnp.float32
VMEM_LIMIT = 16 * 1024 * 1024
PACK_LIMIT = 60 * 1024 * 1024


def dot(a, b, dims):
    return lax.dot_general(a, b, (dims, ((), ())), preferred_element_type=f32)


def exchange(values, axis, groups=None):
    return lax.all_to_all(
        values, axis, split_axis=0, concat_axis=0, tiled=True, axis_index_groups=groups
    )


def pick(table, row_ids):
    local_ids = jnp.arange(table.shape[0], dtype=jnp.int32)
    chosen = (row_ids[:, None] == local_ids[None, :]).astype(table.dtype)
    return dot(chosen, table, ((1,), (0,))).astype(table.dtype)


def quarters(first, second):
    half = first.shape[1] // 2
    parts = [first[:, :half], first[:, half:], second[:, :half], second[:, half:]]
    return jnp.concatenate(parts, axis=0).astype(bf16)


def near_index(device, na, nb):
    return device // (na * nb) * nb + device % nb


def where_am_i():
    return lax.axis_index("node"), lax.axis_index("feat")


def pack_kernel(
    ids_hbm,
    slots_hbm,
    counts_hbm,
    blocks_hbm,
    features_hbm,
    tiles_hbm,
    grad_hbm,
    sent_hbm,
    ids_ref,
    slots_ref,
    counts_ref,
    blocks_ref,
    features_ref,
    tiles_ref,
    grad_ref,
    sent_ref,
    slots_scratch,
    grad_scratch,
    sems,
    out_sems,
    *,
    nx,
    na,
    nb,
    place,
):
    copies = [
        pltpu.make_async_copy(source, target, sems.at[n])
        for n, (source, target) in enumerate(
            [
                (ids_hbm, ids_ref),
                (slots_hbm, slots_ref),
                (counts_hbm, counts_ref),
                (blocks_hbm, blocks_ref),
                (features_hbm, features_ref),
                (tiles_hbm, tiles_ref),
                (grad_hbm, grad_ref),
            ]
        )
    ]
    for copy in copies:
        copy.start()
    device, feat = place()
    near = nx * nb
    capacity, nodes = ids_ref.shape
    locals_, width = features_ref.shape
    count, targets, _ = tiles_ref.shape
    part = sent_ref.shape[1] - na * capacity - na - 8
    part = part // count
    lanes = targets // capacity
    near_at = near_index(device, na, nb)

    near_owners = [
        [(x * na + a) * nb + b for a in range(na)] for x in range(nx) for b in range(nb)
    ]
    local_ids = lax.broadcasted_iota(jnp.int32, (capacity, locals_), 1)
    copies[0].wait()
    copies[4].wait()
    for to, owners in enumerate(near_owners):
        chosen = jnp.concatenate(
            [jnp.where(ids_ref[:, o : o + 1] == local_ids, 1.0, 0.0).astype(bf16) for o in owners],
            axis=0,
        )
        rows = dot(chosen, features_ref[...], ((1,), (0,)))
        sent_ref[to, : na * capacity, :] = rows.astype(bf16)

    for n in (1, 2, 3, 5, 6):
        copies[n].wait()
    used = lax.broadcasted_iota(jnp.int32, (capacity, nodes), 0) < counts_ref[pl.ds(device, 1), :]
    slots = jnp.where(used, slots_ref[...], targets).astype(f32)
    slots = jnp.concatenate([slots] * lanes, axis=0)
    slots = jnp.concatenate([slots, jnp.zeros((targets, targets - nodes), f32)], axis=1).T
    group = lax.broadcasted_iota(jnp.int32, (targets, targets), 1) // capacity
    slots_scratch[...] = jnp.where(group == near_at % lanes, slots, 0.0)
    grad_scratch[...] = grad_ref[...].astype(f32).T
    grad_t = grad_scratch[pl.ds(pl.multiple_of(feat * part, part), part), :].astype(bf16)
    terms = [dot(grad_t, tiles_ref[k], ((1,), (0,))) for k in range(count)]
    blocks = [blocks_ref[0, k] for k in range(count)]
    row = lax.broadcasted_iota(jnp.int32, (8, targets), 0)
    marks = jnp.zeros((8, targets), jnp.int32)
    for k in range(count):
        marks = jnp.where(row == k, blocks[k] % (na * nb) // nb, marks)
        marks = jnp.where(row == count + k, near_index(blocks[k], na, nb), marks)
    marks = marks.astype(f32)
    outs = []
    for to, owners in enumerate(near_owners):
        at = na * capacity
        for k in range(count):
            term = jnp.where(near_index(blocks[k], na, nb) == to, terms[k], 0.0)
            sent_ref[to, at : at + part, :] = term.astype(bf16)
            at += part
        slot_rows = slots_scratch[pl.ds(owners[0], na, stride=nb), :]
        sent_ref[to, at : at + na + 8, :] = jnp.concatenate([slot_rows, marks], 0).astype(bf16)
        out = pltpu.make_async_copy(sent_ref.at[to], sent_hbm.at[to], out_sems.at[to])
        out.start()
        outs.append(out)
    for out in outs:
        out.wait()


def pack(sample_ids, dest_slots, counts, blocks, features, tiles, grad, nx, na, nb, part, place):
    count, targets, _ = tiles.shape
    capacity, nodes = sample_ids.shape
    total = na * capacity + count * part + na + 8
    kernel = functools.partial(pack_kernel, nx=nx, na=na, nb=nb, place=place)
    args = (sample_ids, dest_slots, counts, blocks, features, tiles, grad)
    held = [pltpu.VMEM(arg.shape, arg.dtype) for arg in args]
    held[3] = pltpu.SMEM(blocks.shape, blocks.dtype)
    return pl.pallas_call(
        kernel,
        out_shape=jax.ShapeDtypeStruct((nx * nb, total, features.shape[1]), bf16),
        in_specs=[pl.BlockSpec(memory_space=pltpu.HBM)] * len(args),
        out_specs=pl.BlockSpec(memory_space=pltpu.HBM),
        scratch_shapes=held
        + [
            pltpu.VMEM((nx * nb, total, features.shape[1]), bf16),
            pltpu.VMEM((targets, targets), f32),
            pltpu.VMEM((grad.shape[1], targets), f32),
            pltpu.SemaphoreType.DMA((len(args),)),
            pltpu.SemaphoreType.DMA((nx * nb,)),
        ],
        compiler_params=pltpu.CompilerParams(vmem_limit_bytes=PACK_LIMIT),
    )(*args)


def in_vmem(kernel, out_shape, *args, scratch_shapes=()):
    vmem = pl.BlockSpec(memory_space=pltpu.VMEM)
    many = isinstance(out_shape, (list, tuple))
    return pl.pallas_call(
        kernel,
        out_shape=out_shape,
        in_specs=[vmem] * len(args),
        out_specs=[vmem] * len(out_shape) if many else vmem,
        scratch_shapes=scratch_shapes,
        compiler_params=pltpu.CompilerParams(vmem_limit_bytes=VMEM_LIMIT),
    )(*args)


def halve(values):
    high = values.astype(bf16)
    return high, (values - high.astype(f32)).astype(bf16)


def gather_kernel(
    got_ref, rows_ref, sent_ref, marks_ref, rows_t_ref, *, capacity, part, count
):
    rows_t_ref[...] = rows_ref[...].astype(f32).T.astype(bf16)
    near = got_ref.shape[0]
    far, _, targets = sent_ref.shape
    lanes = targets // capacity
    at = far * capacity + count * part
    marks = [got_ref[n, at : at + far + 8, :].astype(f32) for n in range(near)]
    for n in range(near):
        marks_ref[n] = got_ref[n, at : at + far + 8, :]
    slots = [sum(marks[h : h + lanes])[:far] for h in range(0, near, lanes)]
    nodes = lax.broadcasted_iota(jnp.int32, (targets, targets), 0).astype(f32)
    extra = sent_ref.shape[1] - targets - part
    ones = jnp.ones((extra, targets), bf16)
    back = [jnp.zeros((part, targets), f32) for _ in range(far)]
    for n in range(near):
        for k in range(count):
            start = far * capacity + k * part
            term = got_ref[n, start : start + part, :].astype(f32)
            mark = jnp.broadcast_to(marks[n][far + k : far + k + 1, :], (part, targets))
            back = [back[a] + jnp.where(mark == float(a), term, 0.0) for a in range(far)]
    for a in range(far):
        total = jnp.zeros((targets, targets), f32)
        degree = jnp.zeros((extra, targets), f32)
        for h in range(near // lanes):
            chosen = jnp.where(slots[h][a : a + 1, :] == nodes, 1.0, 0.0).astype(bf16)
            rows = [
                got_ref[h * lanes + n, a * capacity : (a + 1) * capacity, :] for n in range(lanes)
            ]
            total += dot(chosen, jnp.concatenate(rows, axis=0), ((1,), (0,)))
            degree += dot(ones, chosen, ((1,), (1,)))
        sent_ref[a] = jnp.concatenate([total, back[a], degree], axis=0).astype(bf16)


def first_kernel(came_ref, rows_ref, self_ref, other_ref, sent_ref, mean_ref, *, part):
    targets = rows_ref.shape[0]
    came = came_ref[0].astype(f32)
    for a in range(1, came_ref.shape[0]):
        came += came_ref[a].astype(f32)
    degree = jnp.broadcast_to(came[targets + part : targets + part + 1, :], (targets, targets)).T
    high, low = halve(came[:targets] / (degree + 1.0))
    mean_ref[...] = high
    pre = dot(rows_ref[...], self_ref[...], ((1,), (0,)))
    pre += dot(high, other_ref[...], ((1,), (0,)))
    pre += dot(low, other_ref[...], ((1,), (0,)))
    back = halve(came[targets : targets + part])
    sent_ref[...] = jnp.concatenate([pre.T.astype(bf16), *back], axis=0)


def grads_kernel(
    got_ref,
    self_ref,
    other_ref,
    grad_ref,
    rows_t_ref,
    mean_ref,
    sent_ref,
    hidden_ref,
    mine_ref,
    scratch,
    *,
    part,
    slice_at,
):
    feats, near = got_ref.shape[0], sent_ref.shape[0]
    hidden = self_ref.shape[0]
    pre = got_ref[0, :hidden, :].astype(f32)
    for f in range(1, feats):
        pre += got_ref[f, :hidden, :].astype(f32)
    sigma = 1.0 / (1.0 + jnp.exp(-pre))
    slope = sigma * (1.0 + pre * (1.0 - sigma))
    scratch[...] = pre * sigma
    hidden_ref[...] = scratch[...].astype(bf16)
    mine = scratch[pl.ds(pl.multiple_of(slice_at() * part, part), part), :].astype(bf16)
    mine_ref[...] = mine
    back_high = [got_ref[f, hidden : hidden + part, :] for f in range(feats)]
    back_high = jnp.concatenate(back_high, axis=0)
    back_low = [got_ref[f, hidden + part :, :] for f in range(feats)]
    back_low = jnp.concatenate(back_low, axis=0)
    grad = dot(self_ref[...], grad_ref[...], ((1,), (1,)))
    grad += dot(other_ref[...], back_high, ((1,), (0,)))
    grad += dot(other_ref[...], back_low, ((1,), (0,)))
    grad = (grad * slope).astype(bf16)
    mean_t = mean_ref[...].astype(f32).T.astype(bf16)
    lower = quarters(dot(rows_t_ref[...], grad, ((1,), (1,))), dot(mean_t, grad, ((1,), (1,))))
    upper = quarters(
        dot(mine, grad_ref[...], ((1,), (0,))),
        dot(mine, back_high, ((1,), (1,))) + dot(mine, back_low, ((1,), (1,))),
    )
    rows_each, share = lower.shape[0] // near, upper.shape[0] // near
    for n in range(near):
        sent_ref[n, :rows_each, :] = lower[n * rows_each : (n + 1) * rows_each]
        sent_ref[n, rows_each:, :] = upper[n * share : (n + 1) * share]


def far_kernel(got_ref, hidden_ref, sent_ref):
    total = got_ref[0].astype(f32)
    for n in range(1, got_ref.shape[0]):
        total += got_ref[n].astype(f32)
    total = total.astype(bf16)
    sums = total.shape[0]
    for a in range(sent_ref.shape[0]):
        sent_ref[a, :sums, :] = total
        sent_ref[a, sums:, :] = hidden_ref[...]


def near_kernel(got_ref, marks_ref, sent_ref, *, sums, part, count, where):
    far = got_ref.shape[0]
    total = got_ref[0, :sums, :].astype(f32)
    for a in range(1, far):
        total += got_ref[a, :sums, :].astype(f32)
    total = total.astype(bf16)
    here = where().astype(f32)
    blocks = [got_ref[a, sums:, :].astype(f32) for a in range(far)]
    for n in range(sent_ref.shape[0]):
        sent_ref[n, :sums, :] = total
        marks = marks_ref[n].astype(f32)
        for k in range(count):
            mark = jnp.where(marks[far + count + k :][:1] == here, marks[far + k :][:1], -1.0)
            mark = jnp.broadcast_to(mark, blocks[0].shape)
            block = jnp.zeros_like(blocks[0])
            for a in range(far):
                block = jnp.where(mark == float(a), blocks[a], block)
            at = sums + k * part
            sent_ref[n, at : at + part, :] = block.astype(bf16)


def second_kernel(got_ref, tiles_ref, sent_ref, *, rows_each, share, part):
    near = got_ref.shape[0]
    agg = jnp.zeros((part, tiles_ref.shape[1]), f32)
    for k in range(tiles_ref.shape[0]):
        at = rows_each + share + k * part
        block = got_ref[0, at : at + part, :].astype(f32)
        for n in range(1, near):
            block += got_ref[n, at : at + part, :].astype(f32)
        agg += dot(block.astype(bf16), tiles_ref[k], ((1,), (1,)))
    rows = [got_ref[n, rows_each : rows_each + share, :] for n in range(near)]
    both = jnp.concatenate([agg.astype(bf16)] + rows, axis=0)
    for f in range(sent_ref.shape[0]):
        sent_ref[f] = both


def last_kernel(
    got_ref,
    hidden_ref,
    self_ref,
    other_ref,
    lower_ref,
    out_ref,
    low_first_ref,
    low_second_ref,
    first_ref,
    second_ref,
    *,
    part,
    rows_each,
):
    feats = got_ref.shape[0]
    half = first_ref.shape[1] // 2
    agg = jnp.concatenate([got_ref[f, :part, :] for f in range(feats)], axis=0)
    out = dot(hidden_ref[...], self_ref[...], ((0,), (0,))) + dot(agg, other_ref[...], ((0,), (0,)))
    out_ref[...] = out.astype(bf16)
    for f in range(feats):
        at = f * part
        for n, ref in enumerate([first_ref, second_ref]):
            start = part * (1 + 2 * n)
            ref[at : at + part, :half] = got_ref[f, start : start + part, :].astype(f32)
            ref[at : at + part, half:] = got_ref[f, start + part : start + 2 * part, :].astype(f32)
    width = low_first_ref.shape[0]
    for n in range(lower_ref.shape[0]):
        quarter, at = divmod(n * rows_each, width)
        ref = (low_first_ref, low_second_ref)[quarter // 2]
        left = quarter % 2 * half
        rows = lower_ref[n, :rows_each, :].astype(f32)
        ref[at : at + rows_each, left : left + half] = rows


def shards(
    features,
    self_one,
    neighbour_one,
    sample_ids,
    dest_slots,
    send_counts,
    self_ids,
    tile_blocks,
    tile_weights,
    self_two,
    neighbour_two,
    out_grad,
):
    feats = lax.axis_size("feat")
    nodes = lax.axis_size("node")
    nx, nb = 4, 2
    na = nodes // (nx * nb)
    near = nx * nb
    near_ids = [(x * na + a) * nb + b for a in range(na) for x in range(nx) for b in range(nb)]
    near_groups = [near_ids[a * near : (a + 1) * near] for a in range(na)]
    far_groups = [list(group) for group in zip(*near_groups)]
    capacity = sample_ids.shape[2]
    targets = self_ids.shape[1]
    width = features.shape[1]
    hidden = neighbour_one.shape[1]
    part = hidden // feats
    tiles = tile_weights[0]
    count = tiles.shape[0]

    sent = pack(
        sample_ids[0].T,
        dest_slots[0].T,
        send_counts,
        tile_blocks,
        features,
        tiles,
        out_grad,
        nx,
        na,
        nb,
        part,
        where_am_i,
    )
    got = exchange(sent, "node", near_groups)
    self_rows = pick(features, self_ids[0])

    sent, marks, self_rows_t = in_vmem(
        functools.partial(gather_kernel, capacity=capacity, part=part, count=count),
        [
            jax.ShapeDtypeStruct((na, targets + part + 16, width), bf16),
            jax.ShapeDtypeStruct((near, na + 8, targets), bf16),
            jax.ShapeDtypeStruct((width, targets), bf16),
        ],
        got,
        self_rows,
    )
    came = exchange(sent, "node", far_groups)

    sent, mean_high = in_vmem(
        functools.partial(first_kernel, part=part),
        [
            jax.ShapeDtypeStruct((hidden + 2 * part, targets), bf16),
            jax.ShapeDtypeStruct((targets, width), bf16),
        ],
        came,
        self_rows,
        self_one,
        neighbour_one,
    )
    got = lax.all_gather(sent, "feat")

    half = hidden // 2
    rows_each, share = 4 * width // near, 4 * part // near
    sent, hidden_t, hidden_part = in_vmem(
        functools.partial(grads_kernel, part=part, slice_at=lambda: lax.axis_index("feat")),
        [
            jax.ShapeDtypeStruct((near, rows_each + share, half), bf16),
            jax.ShapeDtypeStruct((hidden, targets), bf16),
            jax.ShapeDtypeStruct((part, targets), bf16),
        ],
        got,
        self_two,
        neighbour_two,
        out_grad,
        self_rows_t,
        mean_high,
        scratch_shapes=[pltpu.VMEM((hidden, targets), f32)],
    )
    got = exchange(sent, "node", near_groups)
    sent = in_vmem(
        far_kernel,
        jax.ShapeDtypeStruct((na, rows_each + share + part, half), bf16),
        got,
        hidden_part,
    )
    got = exchange(sent, "node", far_groups)
    sums = rows_each + share
    sent = in_vmem(
        functools.partial(
            near_kernel,
            sums=sums,
            part=part,
            count=count,
            where=lambda: near_index(lax.axis_index("node"), na, nb),
        ),
        jax.ShapeDtypeStruct((near, sums + count * part, half), bf16),
        got,
        marks,
    )
    got = exchange(sent, "node", near_groups)
    lower = got

    sent = in_vmem(
        functools.partial(second_kernel, rows_each=rows_each, share=share, part=part),
        jax.ShapeDtypeStruct((feats, part + near * share, targets), bf16),
        got,
        tiles,
    )
    got = exchange(sent, "feat")
    return in_vmem(
        functools.partial(last_kernel, part=part, rows_each=rows_each),
        [
            jax.ShapeDtypeStruct((targets, hidden), bf16),
            jax.ShapeDtypeStruct((width, hidden), f32),
            jax.ShapeDtypeStruct((width, hidden), f32),
            jax.ShapeDtypeStruct((hidden, hidden), f32),
            jax.ShapeDtypeStruct((hidden, hidden), f32),
        ],
        got,
        hidden_t,
        self_two,
        neighbour_two,
        lower,
    )


def solution(mesh):
    placed = (
        P("node", "feat"),
        P("feat", None),
        P("feat", None),
        P("node", None, None),
        P("node", None, None),
        P(),
        P("node", None),
        P("node", None),
        P("node", None, None, None),
        P(),
        P(),
        P("node", None),
    )
    return jax.shard_map(
        shards,
        mesh=mesh,
        in_specs=placed,
        out_specs=(P("node", None), P("feat", None), P("feat", None), P(), P()),
        check_vma=False,
    )
```

```python
import functools

import jax
import jax.numpy as jnp
from jax import lax
from jax.experimental import pallas as pl
from jax.experimental.pallas import tpu as pltpu
from jax.sharding import PartitionSpec as P

bf16 = jnp.bfloat16
f32 = jnp.float32
VMEM_LIMIT = 16 * 1024 * 1024
PACK_LIMIT = 60 * 1024 * 1024


def dot(a, b, dims):
    return lax.dot_general(a, b, (dims, ((), ())), preferred_element_type=f32)


def exchange(values, axis, groups=None):
    return lax.all_to_all(
        values, axis, split_axis=0, concat_axis=0, tiled=True, axis_index_groups=groups
    )


def pick(table, row_ids):
    local_ids = jnp.arange(table.shape[0], dtype=jnp.int32)
    chosen = (row_ids[:, None] == local_ids[None, :]).astype(table.dtype)
    return dot(chosen, table, ((1,), (0,))).astype(table.dtype)


def quarters(first, second):
    half = first.shape[1] // 2
    parts = [first[:, :half], first[:, half:], second[:, :half], second[:, half:]]
    return jnp.concatenate(parts, axis=0).astype(bf16)


def near_index(device, na, nb):
    return device // (na * nb) * nb + device % nb


def where_am_i():
    return lax.axis_index("node"), lax.axis_index("feat")


def pack_kernel(
    ids_hbm,
    slots_hbm,
    counts_hbm,
    blocks_hbm,
    features_hbm,
    tiles_hbm,
    grad_hbm,
    sent_hbm,
    ids_ref,
    slots_ref,
    counts_ref,
    blocks_ref,
    features_ref,
    tiles_ref,
    grad_ref,
    sent_ref,
    slots_scratch,
    grad_scratch,
    sems,
    out_sems,
    *,
    nx,
    na,
    nb,
    place,
):
    copies = [
        pltpu.make_async_copy(source, target, sems.at[n])
        for n, (source, target) in enumerate(
            [
                (ids_hbm, ids_ref),
                (slots_hbm, slots_ref),
                (counts_hbm, counts_ref),
                (blocks_hbm, blocks_ref),
                (features_hbm, features_ref),
                (tiles_hbm, tiles_ref),
                (grad_hbm, grad_ref),
            ]
        )
    ]
    for copy in copies:
        copy.start()
    for copy in copies:
        copy.wait()
    device, feat = place()
    near = nx * nb
    capacity, nodes = ids_ref.shape
    locals_, width = features_ref.shape
    count, targets, _ = tiles_ref.shape
    part = sent_ref.shape[1] - na * capacity - na - 8
    part = part // count
    lanes = targets // capacity
    near_at = near_index(device, na, nb)

    used = lax.broadcasted_iota(jnp.int32, (capacity, nodes), 0) < counts_ref[pl.ds(device, 1), :]
    slots = jnp.where(used, slots_ref[...], targets).astype(f32)
    slots = jnp.concatenate([slots] * lanes, axis=0)
    slots = jnp.concatenate([slots, jnp.zeros((targets, targets - nodes), f32)], axis=1).T
    group = lax.broadcasted_iota(jnp.int32, (targets, targets), 1) // capacity
    slots_scratch[...] = jnp.where(group == near_at % lanes, slots, 0.0)
    grad_scratch[...] = grad_ref[...].astype(f32).T
    grad_t = grad_scratch[pl.ds(pl.multiple_of(feat * part, part), part), :].astype(bf16)
    terms = [dot(grad_t, tiles_ref[k], ((1,), (0,))) for k in range(count)]
    blocks = [blocks_ref[0, k] for k in range(count)]
    row = lax.broadcasted_iota(jnp.int32, (8, targets), 0)
    far_rows = jnp.zeros((8, targets), jnp.int32)
    for k in range(count):
        far_rows = jnp.where(row == k, blocks[k] % (na * nb) // nb, far_rows)
        far_rows = jnp.where(row == count + k, blocks[k] // (na * nb) * nb + blocks[k] % nb, far_rows)
    far_rows = far_rows.astype(f32)
    local_ids = lax.broadcasted_iota(jnp.int32, (capacity, locals_), 1)
    outs = []
    for x in range(nx):
        for b in range(nb):
            to = x * nb + b
            owners = [(x * na + a) * nb + b for a in range(na)]
            chosen = jnp.concatenate(
                [jnp.where(ids_ref[:, o : o + 1] == local_ids, 1.0, 0.0).astype(bf16) for o in owners],
                axis=0,
            )
            rows = dot(chosen, features_ref[...], ((1,), (0,)))
            sent_ref[to, : na * capacity, :] = rows.astype(bf16)
            at = na * capacity
            for k in range(count):
                there = blocks[k] // (na * nb) * nb + blocks[k] % nb == to
                term = jnp.where(there, terms[k], 0.0)
                sent_ref[to, at : at + part, :] = term.astype(bf16)
                at += part
            slot_rows = slots_scratch[pl.ds(owners[0], na, stride=nb), :]
            sent_ref[to, at : at + na + 8, :] = jnp.concatenate([slot_rows, far_rows], 0).astype(bf16)
            out = pltpu.make_async_copy(sent_ref.at[to], sent_hbm.at[to], out_sems.at[to])
            out.start()
            outs.append(out)
    for out in outs:
        out.wait()


def pack(sample_ids, dest_slots, counts, blocks, features, tiles, grad, nx, na, nb, part, place):
    count, targets, _ = tiles.shape
    capacity, nodes = sample_ids.shape
    total = na * capacity + count * part + na + 8
    kernel = functools.partial(pack_kernel, nx=nx, na=na, nb=nb, place=place)
    args = (sample_ids, dest_slots, counts, blocks, features, tiles, grad)
    held = [pltpu.VMEM(arg.shape, arg.dtype) for arg in args]
    held[3] = pltpu.SMEM(blocks.shape, blocks.dtype)
    return pl.pallas_call(
        kernel,
        out_shape=jax.ShapeDtypeStruct((nx * nb, total, features.shape[1]), bf16),
        in_specs=[pl.BlockSpec(memory_space=pltpu.HBM)] * len(args),
        out_specs=pl.BlockSpec(memory_space=pltpu.HBM),
        scratch_shapes=held
        + [
            pltpu.VMEM((nx * nb, total, features.shape[1]), bf16),
            pltpu.VMEM((targets, targets), f32),
            pltpu.VMEM((grad.shape[1], targets), f32),
            pltpu.SemaphoreType.DMA((len(args),)),
            pltpu.SemaphoreType.DMA((nx * nb,)),
        ],
        compiler_params=pltpu.CompilerParams(vmem_limit_bytes=PACK_LIMIT),
    )(*args)


def in_vmem(kernel, out_shape, *args, scratch_shapes=()):
    vmem = pl.BlockSpec(memory_space=pltpu.VMEM)
    many = isinstance(out_shape, (list, tuple))
    return pl.pallas_call(
        kernel,
        out_shape=out_shape,
        in_specs=[vmem] * len(args),
        out_specs=[vmem] * len(out_shape) if many else vmem,
        scratch_shapes=scratch_shapes,
        compiler_params=pltpu.CompilerParams(vmem_limit_bytes=VMEM_LIMIT),
    )(*args)


def halve(values):
    high = values.astype(bf16)
    return high, (values - high.astype(f32)).astype(bf16)


def gather_kernel(
    got_ref, rows_ref, sent_ref, marks_ref, rows_t_ref, *, capacity, part, count
):
    rows_t_ref[...] = rows_ref[...].astype(f32).T.astype(bf16)
    near = got_ref.shape[0]
    far, _, targets = sent_ref.shape
    lanes = targets // capacity
    at = far * capacity + count * part
    marks = [got_ref[n, at : at + far + 8, :].astype(f32) for n in range(near)]
    for n in range(near):
        marks_ref[n] = got_ref[n, at : at + far + 8, :]
    slots = [sum(marks[h : h + lanes])[:far] for h in range(0, near, lanes)]
    nodes = lax.broadcasted_iota(jnp.int32, (targets, targets), 0).astype(f32)
    ones = jnp.ones((8, targets), bf16)
    back = [jnp.zeros((part, targets), f32) for _ in range(far)]
    for n in range(near):
        for k in range(count):
            start = far * capacity + k * part
            term = got_ref[n, start : start + part, :].astype(f32)
            mark = jnp.broadcast_to(marks[n][far + k : far + k + 1, :], (part, targets))
            back = [back[a] + jnp.where(mark == float(a), term, 0.0) for a in range(far)]
    for a in range(far):
        total = jnp.zeros((targets, targets), f32)
        degree = jnp.zeros((8, targets), f32)
        for h in range(near // lanes):
            chosen = jnp.where(slots[h][a : a + 1, :] == nodes, 1.0, 0.0).astype(bf16)
            rows = [
                got_ref[h * lanes + n, a * capacity : (a + 1) * capacity, :] for n in range(lanes)
            ]
            total += dot(chosen, jnp.concatenate(rows, axis=0), ((1,), (0,)))
            degree += dot(ones, chosen, ((1,), (1,)))
        sent_ref[a] = jnp.concatenate([total, back[a], degree], axis=0).astype(bf16)


def first_kernel(came_ref, rows_ref, self_ref, other_ref, sent_ref, mean_ref, *, part):
    targets = rows_ref.shape[0]
    came = came_ref[0].astype(f32)
    for a in range(1, came_ref.shape[0]):
        came += came_ref[a].astype(f32)
    degree = jnp.broadcast_to(came[targets + part : targets + part + 1, :], (targets, targets)).T
    high, low = halve(came[:targets] / (degree + 1.0))
    mean_ref[...] = high
    pre = dot(rows_ref[...], self_ref[...], ((1,), (0,)))
    pre += dot(high, other_ref[...], ((1,), (0,)))
    pre += dot(low, other_ref[...], ((1,), (0,)))
    back = halve(came[targets : targets + part])
    all_rows = jnp.concatenate([pre.T.astype(bf16), *back], axis=0)
    for y in range(sent_ref.shape[0]):
        sent_ref[y] = all_rows


def pair_kernel(got_ref, sent_ref, *, hidden):
    pre = got_ref[0, :hidden, :].astype(f32)
    for y in range(1, got_ref.shape[0]):
        pre += got_ref[y, :hidden, :].astype(f32)
    back = [got_ref[y, hidden:, :] for y in range(got_ref.shape[0])]
    sent_ref[...] = jnp.concatenate([*halve(pre), *back], axis=0)


def grads_kernel(
    got_ref,
    self_ref,
    other_ref,
    grad_ref,
    rows_t_ref,
    mean_ref,
    sent_ref,
    hidden_ref,
    mine_ref,
    scratch,
    *,
    part,
    slice_at,
):
    cores, near = got_ref.shape[0], sent_ref.shape[0]
    hidden = self_ref.shape[0]
    pre = got_ref[0, :hidden, :].astype(f32) + got_ref[0, hidden : 2 * hidden, :].astype(f32)
    for c in range(1, cores):
        pre += got_ref[c, :hidden, :].astype(f32)
        pre += got_ref[c, hidden : 2 * hidden, :].astype(f32)
    sigma = 1.0 / (1.0 + jnp.exp(-pre))
    slope = sigma * (1.0 + pre * (1.0 - sigma))
    scratch[...] = pre * sigma
    hidden_ref[...] = scratch[...].astype(bf16)
    mine = scratch[pl.ds(pl.multiple_of(slice_at() * part, part), part), :].astype(bf16)
    mine_ref[...] = mine
    back_high, back_low = [], []
    for y in range(hidden // part // cores):
        at = 2 * (hidden + y * part)
        for c in range(cores):
            back_high.append(got_ref[c, at : at + part, :])
            back_low.append(got_ref[c, at + part : at + 2 * part, :])
    back_high = jnp.concatenate(back_high, axis=0)
    back_low = jnp.concatenate(back_low, axis=0)
    grad = dot(self_ref[...], grad_ref[...], ((1,), (1,)))
    grad += dot(other_ref[...], back_high, ((1,), (0,)))
    grad += dot(other_ref[...], back_low, ((1,), (0,)))
    grad = (grad * slope).astype(bf16)
    mean_t = mean_ref[...].astype(f32).T.astype(bf16)
    lower = quarters(dot(rows_t_ref[...], grad, ((1,), (1,))), dot(mean_t, grad, ((1,), (1,))))
    upper = quarters(
        dot(mine, grad_ref[...], ((1,), (0,))),
        dot(mine, back_high, ((1,), (1,))) + dot(mine, back_low, ((1,), (1,))),
    )
    rows_each, share = lower.shape[0] // near, upper.shape[0] // near
    for n in range(near):
        sent_ref[n, :rows_each, :] = lower[n * rows_each : (n + 1) * rows_each]
        sent_ref[n, rows_each:, :] = upper[n * share : (n + 1) * share]


def far_kernel(got_ref, hidden_ref, sent_ref):
    total = got_ref[0].astype(f32)
    for n in range(1, got_ref.shape[0]):
        total += got_ref[n].astype(f32)
    total = total.astype(bf16)
    sums = total.shape[0]
    for a in range(sent_ref.shape[0]):
        sent_ref[a, :sums, :] = total
        sent_ref[a, sums:, :] = hidden_ref[...]


def near_kernel(got_ref, marks_ref, sent_ref, *, sums, part, count, where):
    far = got_ref.shape[0]
    total = got_ref[0, :sums, :].astype(f32)
    for a in range(1, far):
        total += got_ref[a, :sums, :].astype(f32)
    total = total.astype(bf16)
    here = where().astype(f32)
    blocks = [got_ref[a, sums:, :].astype(f32) for a in range(far)]
    for n in range(sent_ref.shape[0]):
        sent_ref[n, :sums, :] = total
        marks = marks_ref[n].astype(f32)
        for k in range(count):
            mark = jnp.where(marks[far + count + k :][:1] == here, marks[far + k :][:1], -1.0)
            mark = jnp.broadcast_to(mark, blocks[0].shape)
            block = jnp.zeros_like(blocks[0])
            for a in range(far):
                block = jnp.where(mark == float(a), blocks[a], block)
            at = sums + k * part
            sent_ref[n, at : at + part, :] = block.astype(bf16)


def second_kernel(got_ref, tiles_ref, sent_ref, *, rows_each, share, part):
    near = got_ref.shape[0]
    agg = jnp.zeros((part, tiles_ref.shape[1]), f32)
    for k in range(tiles_ref.shape[0]):
        at = rows_each + share + k * part
        block = got_ref[0, at : at + part, :].astype(f32)
        for n in range(1, near):
            block += got_ref[n, at : at + part, :].astype(f32)
        agg += dot(block.astype(bf16), tiles_ref[k], ((1,), (1,)))
    rows = [got_ref[n, rows_each : rows_each + share, :] for n in range(near)]
    both = jnp.concatenate([agg.astype(bf16)] + rows, axis=0)
    for f in range(sent_ref.shape[0]):
        sent_ref[f] = both


def last_kernel(
    got_ref,
    hidden_ref,
    self_ref,
    other_ref,
    lower_ref,
    out_ref,
    low_first_ref,
    low_second_ref,
    first_ref,
    second_ref,
    *,
    part,
    rows_each,
):
    feats = got_ref.shape[0]
    half = first_ref.shape[1] // 2
    agg = jnp.concatenate([got_ref[f, :part, :] for f in range(feats)], axis=0)
    out = dot(hidden_ref[...], self_ref[...], ((0,), (0,))) + dot(agg, other_ref[...], ((0,), (0,)))
    out_ref[...] = out.astype(bf16)
    for f in range(feats):
        at = f * part
        for n, ref in enumerate([first_ref, second_ref]):
            start = part * (1 + 2 * n)
            ref[at : at + part, :half] = got_ref[f, start : start + part, :].astype(f32)
            ref[at : at + part, half:] = got_ref[f, start + part : start + 2 * part, :].astype(f32)
    width = low_first_ref.shape[0]
    for n in range(lower_ref.shape[0]):
        quarter, at = divmod(n * rows_each, width)
        ref = (low_first_ref, low_second_ref)[quarter // 2]
        left = quarter % 2 * half
        rows = lower_ref[n, :rows_each, :].astype(f32)
        ref[at : at + rows_each, left : left + half] = rows


def shards(
    features,
    self_one,
    neighbour_one,
    sample_ids,
    dest_slots,
    send_counts,
    self_ids,
    tile_blocks,
    tile_weights,
    self_two,
    neighbour_two,
    out_grad,
):
    feats = lax.axis_size("feat")
    nodes = lax.axis_size("node")
    nx, nb = 4, 2
    na = nodes // (nx * nb)
    near = nx * nb
    near_ids = [(x * na + a) * nb + b for a in range(na) for x in range(nx) for b in range(nb)]
    near_groups = [near_ids[a * near : (a + 1) * near] for a in range(na)]
    far_groups = [list(group) for group in zip(*near_groups)]
    cores = 2
    core_groups = [[y * cores + c for c in range(cores)] for y in range(feats // cores)]
    y_groups = [list(group) for group in zip(*core_groups)]
    capacity = sample_ids.shape[2]
    targets = self_ids.shape[1]
    width = features.shape[1]
    hidden = neighbour_one.shape[1]
    part = hidden // feats
    tiles = tile_weights[0]
    count = tiles.shape[0]

    sent = pack(
        sample_ids[0].T,
        dest_slots[0].T,
        send_counts,
        tile_blocks,
        features,
        tiles,
        out_grad,
        nx,
        na,
        nb,
        part,
        where_am_i,
    )
    got = exchange(sent, "node", near_groups)
    self_rows = pick(features, self_ids[0])

    sent, marks, self_rows_t = in_vmem(
        functools.partial(gather_kernel, capacity=capacity, part=part, count=count),
        [
            jax.ShapeDtypeStruct((na, targets + part + 8, width), bf16),
            jax.ShapeDtypeStruct((near, na + 8, targets), bf16),
            jax.ShapeDtypeStruct((width, targets), bf16),
        ],
        got,
        self_rows,
    )
    came = exchange(sent, "node", far_groups)

    sent, mean_high = in_vmem(
        functools.partial(first_kernel, part=part),
        [
            jax.ShapeDtypeStruct((feats // cores, hidden + 2 * part, targets), bf16),
            jax.ShapeDtypeStruct((targets, width), bf16),
        ],
        came,
        self_rows,
        self_one,
        neighbour_one,
    )
    got = exchange(sent, "feat", y_groups)
    sent = in_vmem(
        functools.partial(pair_kernel, hidden=hidden),
        jax.ShapeDtypeStruct((2 * hidden + 2 * part * feats // cores, targets), bf16),
        got,
    )
    got = lax.all_gather(sent, "feat", axis_index_groups=core_groups)

    half = hidden // 2
    rows_each, share = 4 * width // near, 4 * part // near
    sent, hidden_t, hidden_part = in_vmem(
        functools.partial(grads_kernel, part=part, slice_at=lambda: lax.axis_index("feat")),
        [
            jax.ShapeDtypeStruct((near, rows_each + share, half), bf16),
            jax.ShapeDtypeStruct((hidden, targets), bf16),
            jax.ShapeDtypeStruct((part, targets), bf16),
        ],
        got,
        self_two,
        neighbour_two,
        out_grad,
        self_rows_t,
        mean_high,
        scratch_shapes=[pltpu.VMEM((hidden, targets), f32)],
    )
    got = exchange(sent, "node", near_groups)
    sent = in_vmem(
        far_kernel,
        jax.ShapeDtypeStruct((na, rows_each + share + part, half), bf16),
        got,
        hidden_part,
    )
    got = exchange(sent, "node", far_groups)
    sums = rows_each + share
    sent = in_vmem(
        functools.partial(
            near_kernel,
            sums=sums,
            part=part,
            count=count,
            where=lambda: near_index(lax.axis_index("node"), na, nb),
        ),
        jax.ShapeDtypeStruct((near, sums + count * part, half), bf16),
        got,
        marks,
    )
    got = exchange(sent, "node", near_groups)
    lower = got

    sent = in_vmem(
        functools.partial(second_kernel, rows_each=rows_each, share=share, part=part),
        jax.ShapeDtypeStruct((feats, part + near * share, targets), bf16),
        got,
        tiles,
    )
    got = exchange(sent, "feat")
    return in_vmem(
        functools.partial(last_kernel, part=part, rows_each=rows_each),
        [
            jax.ShapeDtypeStruct((targets, hidden), bf16),
            jax.ShapeDtypeStruct((width, hidden), f32),
            jax.ShapeDtypeStruct((width, hidden), f32),
            jax.ShapeDtypeStruct((hidden, hidden), f32),
            jax.ShapeDtypeStruct((hidden, hidden), f32),
        ],
        got,
        hidden_t,
        self_two,
        neighbour_two,
        lower,
    )


def solution(mesh):
    placed = (
        P("node", "feat"),
        P("feat", None),
        P("feat", None),
        P("node", None, None),
        P("node", None, None),
        P(),
        P("node", None),
        P("node", None),
        P("node", None, None, None),
        P(),
        P(),
        P("node", None),
    )
    return jax.shard_map(
        shards,
        mesh=mesh,
        in_specs=placed,
        out_specs=(P("node", None), P("feat", None), P("feat", None), P(), P()),
        check_vma=False,
    )
```

```python
import functools

import jax
import jax.numpy as jnp
from jax import lax
from jax.experimental import pallas as pl
from jax.experimental.pallas import tpu as pltpu
from jax.sharding import PartitionSpec as P

bf16 = jnp.bfloat16
f32 = jnp.float32
VMEM_LIMIT = 16 * 1024 * 1024
PACK_LIMIT = 60 * 1024 * 1024


def dot(a, b, dims):
    return lax.dot_general(a, b, (dims, ((), ())), preferred_element_type=f32)


def exchange(values, axis, groups=None):
    return lax.all_to_all(
        values, axis, split_axis=0, concat_axis=0, tiled=True, axis_index_groups=groups
    )


def pick(table, row_ids):
    local_ids = jnp.arange(table.shape[0], dtype=jnp.int32)
    chosen = (row_ids[:, None] == local_ids[None, :]).astype(table.dtype)
    return dot(chosen, table, ((1,), (0,))).astype(table.dtype)


def quarters(first, second):
    half = first.shape[1] // 2
    parts = [first[:, :half], first[:, half:], second[:, :half], second[:, half:]]
    return jnp.concatenate(parts, axis=0).astype(bf16)


def near_index(device, na, nb):
    return device // (na * nb) * nb + device % nb


def where_am_i():
    return lax.axis_index("node"), lax.axis_index("feat")


def pack_kernel(
    ids_hbm,
    slots_hbm,
    counts_hbm,
    blocks_hbm,
    features_hbm,
    tiles_hbm,
    grad_hbm,
    sent_hbm,
    ids_ref,
    slots_ref,
    counts_ref,
    blocks_ref,
    features_ref,
    tiles_ref,
    grad_ref,
    sent_ref,
    slots_scratch,
    grad_scratch,
    sems,
    out_sems,
    *,
    nx,
    na,
    nb,
    place,
):
    copies = [
        pltpu.make_async_copy(source, target, sems.at[n])
        for n, (source, target) in enumerate(
            [
                (ids_hbm, ids_ref),
                (slots_hbm, slots_ref),
                (counts_hbm, counts_ref),
                (blocks_hbm, blocks_ref),
                (features_hbm, features_ref),
                (tiles_hbm, tiles_ref),
                (grad_hbm, grad_ref),
            ]
        )
    ]
    for copy in copies:
        copy.start()
    device, feat = place()
    near = nx * nb
    capacity, nodes = ids_ref.shape
    locals_, width = features_ref.shape
    count, targets, _ = tiles_ref.shape
    part = sent_ref.shape[1] - na * capacity - na - 8
    part = part // count
    lanes = targets // capacity
    near_at = near_index(device, na, nb)

    near_owners = [
        [(x * na + a) * nb + b for a in range(na)] for x in range(nx) for b in range(nb)
    ]
    cut = na * capacity
    outs = []

    def copy_out(to, start, stop):
        rows = pl.ds(start, stop - start)
        out = pltpu.make_async_copy(
            sent_ref.at[to, rows], sent_hbm.at[to, rows], out_sems.at[len(outs)]
        )
        out.start()
        outs.append(out)

    local_ids = lax.broadcasted_iota(jnp.int32, (capacity, locals_), 1)
    copies[0].wait()
    copies[4].wait()
    for to, owners in enumerate(near_owners):
        chosen = jnp.concatenate(
            [jnp.where(ids_ref[:, o : o + 1] == local_ids, 1.0, 0.0).astype(bf16) for o in owners],
            axis=0,
        )
        sent_ref[to, :cut, :] = dot(chosen, features_ref[...], ((1,), (0,))).astype(bf16)
        copy_out(to, 0, cut)

    for n in (1, 2, 3, 5, 6):
        copies[n].wait()
    used = lax.broadcasted_iota(jnp.int32, (capacity, nodes), 0) < counts_ref[pl.ds(device, 1), :]
    slots = jnp.where(used, slots_ref[...], targets).astype(f32)
    slots = jnp.concatenate([slots] * lanes, axis=0)
    slots = jnp.concatenate([slots, jnp.zeros((targets, targets - nodes), f32)], axis=1).T
    group = lax.broadcasted_iota(jnp.int32, (targets, targets), 1) // capacity
    slots_scratch[...] = jnp.where(group == near_at % lanes, slots, 0.0)
    grad_scratch[...] = grad_ref[...].astype(f32).T
    grad_t = grad_scratch[pl.ds(pl.multiple_of(feat * part, part), part), :].astype(bf16)
    terms = [dot(grad_t, tiles_ref[k], ((1,), (0,))) for k in range(count)]
    blocks = [blocks_ref[0, k] for k in range(count)]
    row = lax.broadcasted_iota(jnp.int32, (8, targets), 0)
    marks = jnp.zeros((8, targets), jnp.int32)
    for k in range(count):
        marks = jnp.where(row == k, blocks[k] % (na * nb) // nb, marks)
        marks = jnp.where(row == count + k, near_index(blocks[k], na, nb), marks)
    marks = marks.astype(f32)
    for to, owners in enumerate(near_owners):
        at = cut
        for k in range(count):
            term = jnp.where(near_index(blocks[k], na, nb) == to, terms[k], 0.0)
            sent_ref[to, at : at + part, :] = term.astype(bf16)
            at += part
        slot_rows = slots_scratch[pl.ds(owners[0], na, stride=nb), :]
        sent_ref[to, at : at + na + 8, :] = jnp.concatenate([slot_rows, marks], 0).astype(bf16)
        copy_out(to, cut, at + na + 8)
    for out in outs:
        out.wait()


def pack(sample_ids, dest_slots, counts, blocks, features, tiles, grad, nx, na, nb, part, place):
    count, targets, _ = tiles.shape
    capacity, nodes = sample_ids.shape
    total = na * capacity + count * part + na + 8
    kernel = functools.partial(pack_kernel, nx=nx, na=na, nb=nb, place=place)
    args = (sample_ids, dest_slots, counts, blocks, features, tiles, grad)
    held = [pltpu.VMEM(arg.shape, arg.dtype) for arg in args]
    held[3] = pltpu.SMEM(blocks.shape, blocks.dtype)
    return pl.pallas_call(
        kernel,
        out_shape=jax.ShapeDtypeStruct((nx * nb, total, features.shape[1]), bf16),
        in_specs=[pl.BlockSpec(memory_space=pltpu.HBM)] * len(args),
        out_specs=pl.BlockSpec(memory_space=pltpu.HBM),
        scratch_shapes=held
        + [
            pltpu.VMEM((nx * nb, total, features.shape[1]), bf16),
            pltpu.VMEM((targets, targets), f32),
            pltpu.VMEM((grad.shape[1], targets), f32),
            pltpu.SemaphoreType.DMA((len(args),)),
            pltpu.SemaphoreType.DMA((2 * nx * nb,)),
        ],
        compiler_params=pltpu.CompilerParams(vmem_limit_bytes=PACK_LIMIT),
    )(*args)


def in_vmem(kernel, out_shape, *args, scratch_shapes=(), out_space=pltpu.VMEM):
    vmem = pl.BlockSpec(memory_space=pltpu.VMEM)
    out = pl.BlockSpec(memory_space=out_space)
    many = isinstance(out_shape, (list, tuple))
    return pl.pallas_call(
        kernel,
        out_shape=out_shape,
        in_specs=[vmem] * len(args),
        out_specs=[out] * len(out_shape) if many else out,
        scratch_shapes=scratch_shapes,
        compiler_params=pltpu.CompilerParams(vmem_limit_bytes=VMEM_LIMIT),
    )(*args)


def halve(values):
    high = values.astype(bf16)
    return high, (values - high.astype(f32)).astype(bf16)


def gather_kernel(
    got_ref, rows_ref, sent_ref, marks_ref, rows_t_ref, *, capacity, part, count
):
    rows_t_ref[...] = rows_ref[...].astype(f32).T.astype(bf16)
    near = got_ref.shape[0]
    far, _, targets = sent_ref.shape
    lanes = targets // capacity
    at = far * capacity + count * part
    marks = [got_ref[n, at : at + far + 8, :].astype(f32) for n in range(near)]
    for n in range(near):
        marks_ref[n] = got_ref[n, at : at + far + 8, :]
    slots = [sum(marks[h : h + lanes])[:far] for h in range(0, near, lanes)]
    nodes = lax.broadcasted_iota(jnp.int32, (targets, targets), 0).astype(f32)
    ones = jnp.ones((8, targets), bf16)
    back = [jnp.zeros((part, targets), f32) for _ in range(far)]
    for n in range(near):
        for k in range(count):
            start = far * capacity + k * part
            term = got_ref[n, start : start + part, :].astype(f32)
            mark = jnp.broadcast_to(marks[n][far + k : far + k + 1, :], (part, targets))
            back = [back[a] + jnp.where(mark == float(a), term, 0.0) for a in range(far)]
    for a in range(far):
        total = jnp.zeros((targets, targets), f32)
        degree = jnp.zeros((8, targets), f32)
        for h in range(near // lanes):
            chosen = jnp.where(slots[h][a : a + 1, :] == nodes, 1.0, 0.0).astype(bf16)
            rows = [
                got_ref[h * lanes + n, a * capacity : (a + 1) * capacity, :] for n in range(lanes)
            ]
            total += dot(chosen, jnp.concatenate(rows, axis=0), ((1,), (0,)))
            degree += dot(ones, chosen, ((1,), (1,)))
        sent_ref[a] = jnp.concatenate([total, back[a], degree], axis=0).astype(bf16)


def first_kernel(came_ref, rows_ref, self_ref, other_ref, sent_ref, mean_ref, *, part):
    targets = rows_ref.shape[0]
    came = came_ref[0].astype(f32)
    for a in range(1, came_ref.shape[0]):
        came += came_ref[a].astype(f32)
    degree = jnp.broadcast_to(came[targets + part : targets + part + 1, :], (targets, targets)).T
    high, low = halve(came[:targets] / (degree + 1.0))
    mean_ref[...] = high
    pre = dot(rows_ref[...], self_ref[...], ((1,), (0,)))
    pre += dot(high, other_ref[...], ((1,), (0,)))
    pre += dot(low, other_ref[...], ((1,), (0,)))
    back = halve(came[targets : targets + part])
    all_rows = jnp.concatenate([pre.T.astype(bf16), *back], axis=0)
    for y in range(sent_ref.shape[0]):
        sent_ref[y] = all_rows


def pair_kernel(got_ref, sent_ref, *, hidden):
    pre = got_ref[0, :hidden, :].astype(f32)
    for y in range(1, got_ref.shape[0]):
        pre += got_ref[y, :hidden, :].astype(f32)
    back = [got_ref[y, hidden:, :] for y in range(got_ref.shape[0])]
    sent_ref[...] = jnp.concatenate([*halve(pre), *back], axis=0)


def grads_kernel(
    got_ref,
    self_ref,
    other_ref,
    grad_ref,
    rows_t_ref,
    mean_ref,
    sent_ref,
    hidden_ref,
    mine_ref,
    scratch,
    *,
    part,
    slice_at,
):
    cores, near = got_ref.shape[0], sent_ref.shape[0]
    hidden = self_ref.shape[0]
    pre = got_ref[0, :hidden, :].astype(f32) + got_ref[0, hidden : 2 * hidden, :].astype(f32)
    for c in range(1, cores):
        pre += got_ref[c, :hidden, :].astype(f32)
        pre += got_ref[c, hidden : 2 * hidden, :].astype(f32)
    sigma = 1.0 / (1.0 + jnp.exp(-pre))
    slope = sigma * (1.0 + pre * (1.0 - sigma))
    scratch[...] = pre * sigma
    hidden_ref[...] = scratch[...].astype(bf16)
    mine = scratch[pl.ds(pl.multiple_of(slice_at() * part, part), part), :].astype(bf16)
    mine_ref[...] = mine
    back_high, back_low = [], []
    for y in range(hidden // part // cores):
        at = 2 * (hidden + y * part)
        for c in range(cores):
            back_high.append(got_ref[c, at : at + part, :])
            back_low.append(got_ref[c, at + part : at + 2 * part, :])
    back_high = jnp.concatenate(back_high, axis=0)
    back_low = jnp.concatenate(back_low, axis=0)
    grad = dot(self_ref[...], grad_ref[...], ((1,), (1,)))
    grad += dot(other_ref[...], back_high, ((1,), (0,)))
    grad += dot(other_ref[...], back_low, ((1,), (0,)))
    grad = (grad * slope).astype(bf16)
    mean_t = mean_ref[...].astype(f32).T.astype(bf16)
    lower = quarters(dot(rows_t_ref[...], grad, ((1,), (1,))), dot(mean_t, grad, ((1,), (1,))))
    upper = quarters(
        dot(mine, grad_ref[...], ((1,), (0,))),
        dot(mine, back_high, ((1,), (1,))) + dot(mine, back_low, ((1,), (1,))),
    )
    rows_each, share = lower.shape[0] // near, upper.shape[0] // near
    for n in range(near):
        sent_ref[n, :rows_each, :] = lower[n * rows_each : (n + 1) * rows_each]
        sent_ref[n, rows_each:, :] = upper[n * share : (n + 1) * share]


def far_kernel(got_ref, hidden_ref, sent_ref):
    total = got_ref[0].astype(f32)
    for n in range(1, got_ref.shape[0]):
        total += got_ref[n].astype(f32)
    total = total.astype(bf16)
    sums = total.shape[0]
    for a in range(sent_ref.shape[0]):
        sent_ref[a, :sums, :] = total
        sent_ref[a, sums:, :] = hidden_ref[...]


def near_kernel(got_ref, marks_ref, sent_ref, *, sums, part, count, where):
    far = got_ref.shape[0]
    total = got_ref[0, :sums, :].astype(f32)
    for a in range(1, far):
        total += got_ref[a, :sums, :].astype(f32)
    total = total.astype(bf16)
    here = where().astype(f32)
    blocks = [got_ref[a, sums:, :].astype(f32) for a in range(far)]
    for n in range(sent_ref.shape[0]):
        sent_ref[n, :sums, :] = total
        marks = marks_ref[n].astype(f32)
        for k in range(count):
            mark = jnp.where(marks[far + count + k :][:1] == here, marks[far + k :][:1], -1.0)
            mark = jnp.broadcast_to(mark, blocks[0].shape)
            block = jnp.zeros_like(blocks[0])
            for a in range(far):
                block = jnp.where(mark == float(a), blocks[a], block)
            at = sums + k * part
            sent_ref[n, at : at + part, :] = block.astype(bf16)


def second_kernel(got_ref, tiles_ref, sent_ref, *, rows_each, share, part):
    near = got_ref.shape[0]
    agg = jnp.zeros((part, tiles_ref.shape[1]), f32)
    for k in range(tiles_ref.shape[0]):
        at = rows_each + share + k * part
        block = got_ref[0, at : at + part, :].astype(f32)
        for n in range(1, near):
            block += got_ref[n, at : at + part, :].astype(f32)
        agg += dot(block.astype(bf16), tiles_ref[k], ((1,), (1,)))
    rows = [got_ref[n, rows_each : rows_each + share, :] for n in range(near)]
    both = jnp.concatenate([agg.astype(bf16)] + rows, axis=0)
    for f in range(sent_ref.shape[0]):
        sent_ref[f] = both


def last_kernel(
    got_ref, hidden_ref, self_ref, other_ref, lower_ref, *refs, part, rows_each
):
    outs, held, sems = refs[:5], refs[5:10], refs[10]
    out_ref, low_first_ref, low_second_ref, first_ref, second_ref = held
    feats = got_ref.shape[0]
    half = first_ref.shape[1] // 2
    width = low_first_ref.shape[0]
    copies = [pltpu.make_async_copy(held[n], outs[n], sems.at[n]) for n in range(5)]
    for n in range(lower_ref.shape[0]):
        quarter, at = divmod(n * rows_each, width)
        ref = (low_first_ref, low_second_ref)[quarter // 2]
        left = quarter % 2 * half
        rows = lower_ref[n, :rows_each, :].astype(f32)
        ref[at : at + rows_each, left : left + half] = rows
    copies[1].start()
    copies[2].start()
    for n, ref in enumerate([first_ref, second_ref]):
        start = part * (1 + 2 * n)
        for f in range(feats):
            at = f * part
            ref[at : at + part, :half] = got_ref[f, start : start + part, :].astype(f32)
            ref[at : at + part, half:] = got_ref[f, start + part : start + 2 * part, :].astype(f32)
        copies[3 + n].start()
    agg = jnp.concatenate([got_ref[f, :part, :] for f in range(feats)], axis=0)
    out = dot(hidden_ref[...], self_ref[...], ((0,), (0,))) + dot(agg, other_ref[...], ((0,), (0,)))
    out_ref[...] = out.astype(bf16)
    copies[0].start()
    for copy in copies:
        copy.wait()


def shards(
    features,
    self_one,
    neighbour_one,
    sample_ids,
    dest_slots,
    send_counts,
    self_ids,
    tile_blocks,
    tile_weights,
    self_two,
    neighbour_two,
    out_grad,
):
    feats = lax.axis_size("feat")
    nodes = lax.axis_size("node")
    nx, nb = 4, 2
    na = nodes // (nx * nb)
    near = nx * nb
    near_ids = [(x * na + a) * nb + b for a in range(na) for x in range(nx) for b in range(nb)]
    near_groups = [near_ids[a * near : (a + 1) * near] for a in range(na)]
    far_groups = [list(group) for group in zip(*near_groups)]
    cores = 2
    core_groups = [[y * cores + c for c in range(cores)] for y in range(feats // cores)]
    y_groups = [list(group) for group in zip(*core_groups)]
    capacity = sample_ids.shape[2]
    targets = self_ids.shape[1]
    width = features.shape[1]
    hidden = neighbour_one.shape[1]
    part = hidden // feats
    tiles = tile_weights[0]
    count = tiles.shape[0]

    sent = pack(
        sample_ids[0].T,
        dest_slots[0].T,
        send_counts,
        tile_blocks,
        features,
        tiles,
        out_grad,
        nx,
        na,
        nb,
        part,
        where_am_i,
    )
    got = exchange(sent, "node", near_groups)
    self_rows = pick(features, self_ids[0])

    sent, marks, self_rows_t = in_vmem(
        functools.partial(gather_kernel, capacity=capacity, part=part, count=count),
        [
            jax.ShapeDtypeStruct((na, targets + part + 8, width), bf16),
            jax.ShapeDtypeStruct((near, na + 8, targets), bf16),
            jax.ShapeDtypeStruct((width, targets), bf16),
        ],
        got,
        self_rows,
    )
    came = exchange(sent, "node", far_groups)

    sent, mean_high = in_vmem(
        functools.partial(first_kernel, part=part),
        [
            jax.ShapeDtypeStruct((feats // cores, hidden + 2 * part, targets), bf16),
            jax.ShapeDtypeStruct((targets, width), bf16),
        ],
        came,
        self_rows,
        self_one,
        neighbour_one,
    )
    got = exchange(sent, "feat", y_groups)
    sent = in_vmem(
        functools.partial(pair_kernel, hidden=hidden),
        jax.ShapeDtypeStruct((2 * hidden + 2 * part * feats // cores, targets), bf16),
        got,
    )
    got = lax.all_gather(sent, "feat", axis_index_groups=core_groups)

    half = hidden // 2
    rows_each, share = 4 * width // near, 4 * part // near
    sent, hidden_t, hidden_part = in_vmem(
        functools.partial(grads_kernel, part=part, slice_at=lambda: lax.axis_index("feat")),
        [
            jax.ShapeDtypeStruct((near, rows_each + share, half), bf16),
            jax.ShapeDtypeStruct((hidden, targets), bf16),
            jax.ShapeDtypeStruct((part, targets), bf16),
        ],
        got,
        self_two,
        neighbour_two,
        out_grad,
        self_rows_t,
        mean_high,
        scratch_shapes=[pltpu.VMEM((hidden, targets), f32)],
    )
    got = exchange(sent, "node", near_groups)
    sent = in_vmem(
        far_kernel,
        jax.ShapeDtypeStruct((na, rows_each + share + part, half), bf16),
        got,
        hidden_part,
    )
    got = exchange(sent, "node", far_groups)
    sums = rows_each + share
    sent = in_vmem(
        functools.partial(
            near_kernel,
            sums=sums,
            part=part,
            count=count,
            where=lambda: near_index(lax.axis_index("node"), na, nb),
        ),
        jax.ShapeDtypeStruct((near, sums + count * part, half), bf16),
        got,
        marks,
    )
    got = exchange(sent, "node", near_groups)
    lower = got

    sent = in_vmem(
        functools.partial(second_kernel, rows_each=rows_each, share=share, part=part),
        jax.ShapeDtypeStruct((feats, part + near * share, targets), bf16),
        got,
        tiles,
    )
    got = exchange(sent, "feat")
    shapes = [
        jax.ShapeDtypeStruct((targets, hidden), bf16),
        jax.ShapeDtypeStruct((width, hidden), f32),
        jax.ShapeDtypeStruct((width, hidden), f32),
        jax.ShapeDtypeStruct((hidden, hidden), f32),
        jax.ShapeDtypeStruct((hidden, hidden), f32),
    ]
    return in_vmem(
        functools.partial(last_kernel, part=part, rows_each=rows_each),
        shapes,
        got,
        hidden_t,
        self_two,
        neighbour_two,
        lower,
        out_space=pltpu.HBM,
        scratch_shapes=[pltpu.VMEM(shape.shape, shape.dtype) for shape in shapes]
        + [pltpu.SemaphoreType.DMA((len(shapes),))],
    )


def solution(mesh):
    placed = (
        P("node", "feat"),
        P("feat", None),
        P("feat", None),
        P("node", None, None),
        P("node", None, None),
        P(),
        P("node", None),
        P("node", None),
        P("node", None, None, None),
        P(),
        P(),
        P("node", None),
    )
    return jax.shard_map(
        shards,
        mesh=mesh,
        in_specs=placed,
        out_specs=(P("node", None), P("feat", None), P("feat", None), P(), P()),
        check_vma=False,
    )
```

```python
import functools

import jax
import jax.numpy as jnp
from jax import lax
from jax.experimental import pallas as pl
from jax.experimental.pallas import tpu as pltpu
from jax.sharding import PartitionSpec as P

bf16 = jnp.bfloat16
f32 = jnp.float32
VMEM_LIMIT = 16 * 1024 * 1024
PACK_LIMIT = 60 * 1024 * 1024


def dot(a, b, dims):
    return lax.dot_general(a, b, (dims, ((), ())), preferred_element_type=f32)


def exchange(values, axis, groups=None):
    return lax.all_to_all(
        values, axis, split_axis=0, concat_axis=0, tiled=True, axis_index_groups=groups
    )


def pick(table, row_ids):
    local_ids = jnp.arange(table.shape[0], dtype=jnp.int32)
    chosen = (row_ids[:, None] == local_ids[None, :]).astype(table.dtype)
    return dot(chosen, table, ((1,), (0,))).astype(table.dtype)


def quarters(first, second):
    half = first.shape[1] // 2
    parts = [first[:, :half], first[:, half:], second[:, :half], second[:, half:]]
    return jnp.concatenate(parts, axis=0).astype(bf16)


def near_index(device, na, nb):
    return device // (na * nb) * nb + device % nb


def where_am_i():
    return lax.axis_index("node"), lax.axis_index("feat")


def pack_kernel(
    ids_hbm,
    slots_hbm,
    counts_hbm,
    blocks_hbm,
    features_hbm,
    tiles_hbm,
    grad_hbm,
    sent_hbm,
    ids_ref,
    slots_ref,
    counts_ref,
    blocks_ref,
    features_ref,
    tiles_ref,
    grad_ref,
    sent_ref,
    slots_scratch,
    grad_scratch,
    sems,
    out_sems,
    *,
    nx,
    na,
    nb,
    place,
):
    copies = [
        pltpu.make_async_copy(source, target, sems.at[n])
        for n, (source, target) in enumerate(
            [
                (ids_hbm, ids_ref),
                (slots_hbm, slots_ref),
                (counts_hbm, counts_ref),
                (blocks_hbm, blocks_ref),
                (features_hbm, features_ref),
                (tiles_hbm, tiles_ref),
                (grad_hbm, grad_ref),
            ]
        )
    ]
    for copy in copies:
        copy.start()
    for copy in copies:
        copy.wait()
    device, feat = place()
    near = nx * nb
    capacity, nodes = ids_ref.shape
    locals_, width = features_ref.shape
    count, targets, _ = tiles_ref.shape
    part = sent_ref.shape[1] - na * capacity - na - 8
    part = part // count
    lanes = targets // capacity
    near_at = near_index(device, na, nb)

    used = lax.broadcasted_iota(jnp.int32, (capacity, nodes), 0) < counts_ref[pl.ds(device, 1), :]
    slots = jnp.where(used, slots_ref[...], targets).astype(f32)
    slots = jnp.concatenate([slots] * lanes, axis=0)
    slots = jnp.concatenate([slots, jnp.zeros((targets, targets - nodes), f32)], axis=1).T
    group = lax.broadcasted_iota(jnp.int32, (targets, targets), 1) // capacity
    slots_scratch[...] = jnp.where(group == near_at % lanes, slots, 0.0)
    grad_scratch[...] = grad_ref[...].astype(f32).T
    grad_t = grad_scratch[pl.ds(pl.multiple_of(feat * part, part), part), :].astype(bf16)
    terms = [dot(grad_t, tiles_ref[k], ((1,), (0,))) for k in range(count)]
    blocks = [blocks_ref[0, k] for k in range(count)]
    row = lax.broadcasted_iota(jnp.int32, (8, targets), 0)
    far_rows = jnp.zeros((8, targets), jnp.int32)
    for k in range(count):
        far_rows = jnp.where(row == k, blocks[k] % (na * nb) // nb, far_rows)
        far_rows = jnp.where(row == count + k, blocks[k] // (na * nb) * nb + blocks[k] % nb, far_rows)
    far_rows = far_rows.astype(f32)
    local_ids = lax.broadcasted_iota(jnp.int32, (capacity, locals_), 1)
    outs = []
    for x in range(nx):
        for b in range(nb):
            to = x * nb + b
            owners = [(x * na + a) * nb + b for a in range(na)]
            chosen = jnp.concatenate(
                [jnp.where(ids_ref[:, o : o + 1] == local_ids, 1.0, 0.0).astype(bf16) for o in owners],
                axis=0,
            )
            rows = dot(chosen, features_ref[...], ((1,), (0,)))
            sent_ref[to, : na * capacity, :] = rows.astype(bf16)
            at = na * capacity
            for k in range(count):
                there = blocks[k] // (na * nb) * nb + blocks[k] % nb == to
                term = jnp.where(there, terms[k], 0.0)
                sent_ref[to, at : at + part, :] = term.astype(bf16)
                at += part
            slot_rows = slots_scratch[pl.ds(owners[0], na, stride=nb), :]
            sent_ref[to, at : at + na + 8, :] = jnp.concatenate([slot_rows, far_rows], 0).astype(bf16)
            out = pltpu.make_async_copy(sent_ref.at[to], sent_hbm.at[to], out_sems.at[to])
            out.start()
            outs.append(out)
    for out in outs:
        out.wait()


def pack(sample_ids, dest_slots, counts, blocks, features, tiles, grad, nx, na, nb, part, place):
    count, targets, _ = tiles.shape
    capacity, nodes = sample_ids.shape
    total = na * capacity + count * part + na + 8
    kernel = functools.partial(pack_kernel, nx=nx, na=na, nb=nb, place=place)
    args = (sample_ids, dest_slots, counts, blocks, features, tiles, grad)
    held = [pltpu.VMEM(arg.shape, arg.dtype) for arg in args]
    held[3] = pltpu.SMEM(blocks.shape, blocks.dtype)
    return pl.pallas_call(
        kernel,
        out_shape=jax.ShapeDtypeStruct((nx * nb, total, features.shape[1]), bf16),
        in_specs=[pl.BlockSpec(memory_space=pltpu.HBM)] * len(args),
        out_specs=pl.BlockSpec(memory_space=pltpu.HBM),
        scratch_shapes=held
        + [
            pltpu.VMEM((nx * nb, total, features.shape[1]), bf16),
            pltpu.VMEM((targets, targets), f32),
            pltpu.VMEM((grad.shape[1], targets), f32),
            pltpu.SemaphoreType.DMA((len(args),)),
            pltpu.SemaphoreType.DMA((nx * nb,)),
        ],
        compiler_params=pltpu.CompilerParams(vmem_limit_bytes=PACK_LIMIT),
    )(*args)


def in_vmem(kernel, out_shape, *args, scratch_shapes=()):
    vmem = pl.BlockSpec(memory_space=pltpu.VMEM)
    many = isinstance(out_shape, (list, tuple))
    return pl.pallas_call(
        kernel,
        out_shape=out_shape,
        in_specs=[vmem] * len(args),
        out_specs=[vmem] * len(out_shape) if many else vmem,
        scratch_shapes=scratch_shapes,
        compiler_params=pltpu.CompilerParams(vmem_limit_bytes=VMEM_LIMIT),
    )(*args)


def halve(values):
    high = values.astype(bf16)
    return high, (values - high.astype(f32)).astype(bf16)


def gather_kernel(
    got_ref, rows_ref, sent_ref, marks_ref, rows_t_ref, *, capacity, part, count
):
    rows_t_ref[...] = rows_ref[...].astype(f32).T.astype(bf16)
    near = got_ref.shape[0]
    far, _, targets = sent_ref.shape
    lanes = targets // capacity
    at = far * capacity + count * part
    marks = [got_ref[n, at : at + far + 8, :].astype(f32) for n in range(near)]
    for n in range(near):
        marks_ref[n] = got_ref[n, at : at + far + 8, :]
    slots = [sum(marks[h : h + lanes])[:far] for h in range(0, near, lanes)]
    nodes = lax.broadcasted_iota(jnp.int32, (targets, targets), 0).astype(f32)
    ones = jnp.ones((8, targets), bf16)
    back = [jnp.zeros((part, targets), f32) for _ in range(far)]
    for n in range(near):
        for k in range(count):
            start = far * capacity + k * part
            term = got_ref[n, start : start + part, :].astype(f32)
            mark = jnp.broadcast_to(marks[n][far + k : far + k + 1, :], (part, targets))
            back = [back[a] + jnp.where(mark == float(a), term, 0.0) for a in range(far)]
    for a in range(far):
        total = jnp.zeros((targets, targets), f32)
        degree = jnp.zeros((8, targets), f32)
        for h in range(near // lanes):
            chosen = jnp.where(slots[h][a : a + 1, :] == nodes, 1.0, 0.0).astype(bf16)
            rows = [
                got_ref[h * lanes + n, a * capacity : (a + 1) * capacity, :] for n in range(lanes)
            ]
            total += dot(chosen, jnp.concatenate(rows, axis=0), ((1,), (0,)))
            degree += dot(ones, chosen, ((1,), (1,)))
        sent_ref[a] = jnp.concatenate([total, back[a], degree], axis=0).astype(bf16)


def first_kernel(came_ref, rows_ref, self_ref, other_ref, sent_ref, mean_ref, *, part):
    targets = rows_ref.shape[0]
    came = came_ref[0].astype(f32)
    for a in range(1, came_ref.shape[0]):
        came += came_ref[a].astype(f32)
    degree = jnp.broadcast_to(came[targets + part : targets + part + 1, :], (targets, targets)).T
    high, low = halve(came[:targets] / (degree + 1.0))
    mean_ref[...] = high
    pre = dot(rows_ref[...], self_ref[...], ((1,), (0,)))
    pre += dot(high, other_ref[...], ((1,), (0,)))
    pre += dot(low, other_ref[...], ((1,), (0,)))
    back = halve(came[targets : targets + part])
    all_rows = jnp.concatenate([pre.T.astype(bf16), *back], axis=0)
    for y in range(sent_ref.shape[0]):
        sent_ref[y] = all_rows


def pair_kernel(got_ref, sent_ref, *, hidden):
    pre = got_ref[0, :hidden, :].astype(f32)
    for y in range(1, got_ref.shape[0]):
        pre += got_ref[y, :hidden, :].astype(f32)
    back = [got_ref[y, hidden:, :] for y in range(got_ref.shape[0])]
    sent_ref[...] = jnp.concatenate([*halve(pre), *back], axis=0)


def grads_kernel(
    got_ref,
    self_ref,
    other_ref,
    grad_ref,
    rows_t_ref,
    mean_ref,
    sent_ref,
    hidden_ref,
    mine_ref,
    scratch,
    *,
    part,
    slice_at,
):
    cores, near = got_ref.shape[0], sent_ref.shape[0]
    hidden = self_ref.shape[0]
    pre = got_ref[0, :hidden, :].astype(f32) + got_ref[0, hidden : 2 * hidden, :].astype(f32)
    for c in range(1, cores):
        pre += got_ref[c, :hidden, :].astype(f32)
        pre += got_ref[c, hidden : 2 * hidden, :].astype(f32)
    sigma = 1.0 / (1.0 + jnp.exp(-pre))
    slope = sigma * (1.0 + pre * (1.0 - sigma))
    scratch[...] = pre * sigma
    hidden_ref[...] = scratch[...].astype(bf16)
    mine = scratch[pl.ds(pl.multiple_of(slice_at() * part, part), part), :].astype(bf16)
    mine_ref[...] = mine
    back_high, back_low = [], []
    for y in range(hidden // part // cores):
        at = 2 * (hidden + y * part)
        for c in range(cores):
            back_high.append(got_ref[c, at : at + part, :])
            back_low.append(got_ref[c, at + part : at + 2 * part, :])
    back_high = jnp.concatenate(back_high, axis=0)
    back_low = jnp.concatenate(back_low, axis=0)
    grad = dot(self_ref[...], grad_ref[...], ((1,), (1,)))
    grad += dot(other_ref[...], back_high, ((1,), (0,)))
    grad += dot(other_ref[...], back_low, ((1,), (0,)))
    grad = (grad * slope).astype(bf16)
    mean_t = mean_ref[...].astype(f32).T.astype(bf16)
    lower = quarters(dot(rows_t_ref[...], grad, ((1,), (1,))), dot(mean_t, grad, ((1,), (1,))))
    upper = quarters(
        dot(mine, grad_ref[...], ((1,), (0,))),
        dot(mine, back_high, ((1,), (1,))) + dot(mine, back_low, ((1,), (1,))),
    )
    rows_each, share = lower.shape[0] // near, upper.shape[0] // near
    for n in range(near):
        sent_ref[n, :rows_each, :] = lower[n * rows_each : (n + 1) * rows_each]
        sent_ref[n, rows_each:, :] = upper[n * share : (n + 1) * share]


def far_kernel(got_ref, hidden_ref, sent_ref):
    total = got_ref[0].astype(f32)
    for n in range(1, got_ref.shape[0]):
        total += got_ref[n].astype(f32)
    total = total.astype(bf16)
    sums = total.shape[0]
    for a in range(sent_ref.shape[0]):
        sent_ref[a, :sums, :] = total
        sent_ref[a, sums:, :] = hidden_ref[...]


def near_kernel(got_ref, marks_ref, sent_ref, *, sums, part, count, where):
    far = got_ref.shape[0]
    total = got_ref[0, :sums, :].astype(f32)
    for a in range(1, far):
        total += got_ref[a, :sums, :].astype(f32)
    total = total.astype(bf16)
    here = where().astype(f32)
    blocks = [got_ref[a, sums:, :].astype(f32) for a in range(far)]
    for n in range(sent_ref.shape[0]):
        sent_ref[n, :sums, :] = total
        marks = marks_ref[n].astype(f32)
        for k in range(count):
            mark = jnp.where(marks[far + count + k :][:1] == here, marks[far + k :][:1], -1.0)
            mark = jnp.broadcast_to(mark, blocks[0].shape)
            block = jnp.zeros_like(blocks[0])
            for a in range(far):
                block = jnp.where(mark == float(a), blocks[a], block)
            at = sums + k * part
            sent_ref[n, at : at + part, :] = block.astype(bf16)


def second_kernel(got_ref, tiles_ref, sent_ref, *, rows_each, share, part):
    near = got_ref.shape[0]
    agg = jnp.zeros((part, tiles_ref.shape[1]), f32)
    for k in range(tiles_ref.shape[0]):
        at = rows_each + share + k * part
        block = got_ref[0, at : at + part, :].astype(f32)
        for n in range(1, near):
            block += got_ref[n, at : at + part, :].astype(f32)
        agg += dot(block.astype(bf16), tiles_ref[k], ((1,), (1,)))
    rows = [got_ref[n, rows_each : rows_each + share, :] for n in range(near)]
    both = jnp.concatenate([agg.astype(bf16)] + rows, axis=0)
    for f in range(sent_ref.shape[0]):
        sent_ref[f] = both


def last_kernel(
    got_ref,
    hidden_ref,
    self_ref,
    other_ref,
    lower_ref,
    out_ref,
    low_first_ref,
    low_second_ref,
    first_ref,
    second_ref,
    *,
    part,
    rows_each,
):
    cores = got_ref.shape[0]
    feats = first_ref.shape[0] // part
    rows = got_ref.shape[1] // (feats // cores)

    def slice_rows(f, start):
        at = f // cores * rows + start
        return got_ref[f % cores, at : at + part, :]

    half = first_ref.shape[1] // 2
    agg = jnp.concatenate([slice_rows(f, 0) for f in range(feats)], axis=0)
    out = dot(hidden_ref[...], self_ref[...], ((0,), (0,))) + dot(agg, other_ref[...], ((0,), (0,)))
    out_ref[...] = out.astype(bf16)
    for f in range(feats):
        at = f * part
        for n, ref in enumerate([first_ref, second_ref]):
            start = part * (1 + 2 * n)
            ref[at : at + part, :half] = slice_rows(f, start).astype(f32)
            ref[at : at + part, half:] = slice_rows(f, start + part).astype(f32)
    width = low_first_ref.shape[0]
    for n in range(lower_ref.shape[0]):
        quarter, at = divmod(n * rows_each, width)
        ref = (low_first_ref, low_second_ref)[quarter // 2]
        left = quarter % 2 * half
        part_rows = lower_ref[n, :rows_each, :].astype(f32)
        ref[at : at + rows_each, left : left + half] = part_rows


def shards(
    features,
    self_one,
    neighbour_one,
    sample_ids,
    dest_slots,
    send_counts,
    self_ids,
    tile_blocks,
    tile_weights,
    self_two,
    neighbour_two,
    out_grad,
):
    feats = lax.axis_size("feat")
    nodes = lax.axis_size("node")
    nx, nb = 4, 2
    na = nodes // (nx * nb)
    near = nx * nb
    near_ids = [(x * na + a) * nb + b for a in range(na) for x in range(nx) for b in range(nb)]
    near_groups = [near_ids[a * near : (a + 1) * near] for a in range(na)]
    far_groups = [list(group) for group in zip(*near_groups)]
    cores = 2
    core_groups = [[y * cores + c for c in range(cores)] for y in range(feats // cores)]
    y_groups = [list(group) for group in zip(*core_groups)]
    capacity = sample_ids.shape[2]
    targets = self_ids.shape[1]
    width = features.shape[1]
    hidden = neighbour_one.shape[1]
    part = hidden // feats
    tiles = tile_weights[0]
    count = tiles.shape[0]

    sent = pack(
        sample_ids[0].T,
        dest_slots[0].T,
        send_counts,
        tile_blocks,
        features,
        tiles,
        out_grad,
        nx,
        na,
        nb,
        part,
        where_am_i,
    )
    got = exchange(sent, "node", near_groups)
    self_rows = pick(features, self_ids[0])

    sent, marks, self_rows_t = in_vmem(
        functools.partial(gather_kernel, capacity=capacity, part=part, count=count),
        [
            jax.ShapeDtypeStruct((na, targets + part + 8, width), bf16),
            jax.ShapeDtypeStruct((near, na + 8, targets), bf16),
            jax.ShapeDtypeStruct((width, targets), bf16),
        ],
        got,
        self_rows,
    )
    came = exchange(sent, "node", far_groups)

    sent, mean_high = in_vmem(
        functools.partial(first_kernel, part=part),
        [
            jax.ShapeDtypeStruct((feats // cores, hidden + 2 * part, targets), bf16),
            jax.ShapeDtypeStruct((targets, width), bf16),
        ],
        came,
        self_rows,
        self_one,
        neighbour_one,
    )
    got = exchange(sent, "feat", y_groups)
    sent = in_vmem(
        functools.partial(pair_kernel, hidden=hidden),
        jax.ShapeDtypeStruct((2 * hidden + 2 * part * feats // cores, targets), bf16),
        got,
    )
    got = lax.all_gather(sent, "feat", axis_index_groups=core_groups)

    half = hidden // 2
    rows_each, share = 4 * width // near, 4 * part // near
    sent, hidden_t, hidden_part = in_vmem(
        functools.partial(grads_kernel, part=part, slice_at=lambda: lax.axis_index("feat")),
        [
            jax.ShapeDtypeStruct((near, rows_each + share, half), bf16),
            jax.ShapeDtypeStruct((hidden, targets), bf16),
            jax.ShapeDtypeStruct((part, targets), bf16),
        ],
        got,
        self_two,
        neighbour_two,
        out_grad,
        self_rows_t,
        mean_high,
        scratch_shapes=[pltpu.VMEM((hidden, targets), f32)],
    )
    got = exchange(sent, "node", near_groups)
    sent = in_vmem(
        far_kernel,
        jax.ShapeDtypeStruct((na, rows_each + share + part, half), bf16),
        got,
        hidden_part,
    )
    got = exchange(sent, "node", far_groups)
    sums = rows_each + share
    sent = in_vmem(
        functools.partial(
            near_kernel,
            sums=sums,
            part=part,
            count=count,
            where=lambda: near_index(lax.axis_index("node"), na, nb),
        ),
        jax.ShapeDtypeStruct((near, sums + count * part, half), bf16),
        got,
        marks,
    )
    got = exchange(sent, "node", near_groups)
    lower = got

    sent = in_vmem(
        functools.partial(second_kernel, rows_each=rows_each, share=share, part=part),
        jax.ShapeDtypeStruct((feats // cores, part + near * share, targets), bf16),
        got,
        tiles,
    )
    got = exchange(sent, "feat", y_groups).reshape(-1, targets)
    got = lax.all_gather(got, "feat", axis_index_groups=core_groups)
    return in_vmem(
        functools.partial(last_kernel, part=part, rows_each=rows_each),
        [
            jax.ShapeDtypeStruct((targets, hidden), bf16),
            jax.ShapeDtypeStruct((width, hidden), f32),
            jax.ShapeDtypeStruct((width, hidden), f32),
            jax.ShapeDtypeStruct((hidden, hidden), f32),
            jax.ShapeDtypeStruct((hidden, hidden), f32),
        ],
        got,
        hidden_t,
        self_two,
        neighbour_two,
        lower,
    )


def solution(mesh):
    placed = (
        P("node", "feat"),
        P("feat", None),
        P("feat", None),
        P("node", None, None),
        P("node", None, None),
        P(),
        P("node", None),
        P("node", None),
        P("node", None, None, None),
        P(),
        P(),
        P("node", None),
    )
    return jax.shard_map(
        shards,
        mesh=mesh,
        in_specs=placed,
        out_specs=(P("node", None), P("feat", None), P("feat", None), P(), P()),
        check_vma=False,
    )
```

```python
import functools

import jax
import jax.numpy as jnp
from jax import lax
from jax.experimental import pallas as pl
from jax.experimental.pallas import tpu as pltpu
from jax.sharding import PartitionSpec as P

bf16 = jnp.bfloat16
f32 = jnp.float32
VMEM_LIMIT = 16 * 1024 * 1024
PACK_LIMIT = 60 * 1024 * 1024


def dot(a, b, dims):
    return lax.dot_general(a, b, (dims, ((), ())), preferred_element_type=f32)


def exchange(values, axis, groups=None):
    return lax.all_to_all(
        values, axis, split_axis=0, concat_axis=0, tiled=True, axis_index_groups=groups
    )


def pick(table, row_ids):
    local_ids = jnp.arange(table.shape[0], dtype=jnp.int32)
    chosen = (row_ids[:, None] == local_ids[None, :]).astype(table.dtype)
    return dot(chosen, table, ((1,), (0,))).astype(table.dtype)


def quarters(first, second):
    half = first.shape[1] // 2
    parts = [first[:, :half], first[:, half:], second[:, :half], second[:, half:]]
    return jnp.concatenate(parts, axis=0).astype(bf16)


def near_index(device, na, nb):
    return device // (na * nb) * nb + device % nb


def where_am_i():
    return lax.axis_index("node"), lax.axis_index("feat")


def pack_kernel(
    ids_hbm,
    slots_hbm,
    counts_hbm,
    blocks_hbm,
    features_hbm,
    tiles_hbm,
    grad_hbm,
    sent_hbm,
    ids_ref,
    slots_ref,
    counts_ref,
    blocks_ref,
    features_ref,
    tiles_ref,
    grad_ref,
    sent_ref,
    slots_scratch,
    sems,
    out_sems,
    *,
    nx,
    na,
    nb,
    place,
):
    copies = [
        pltpu.make_async_copy(source, target, sems.at[n])
        for n, (source, target) in enumerate(
            [
                (ids_hbm, ids_ref),
                (slots_hbm, slots_ref),
                (counts_hbm, counts_ref),
                (blocks_hbm, blocks_ref),
                (features_hbm, features_ref),
                (tiles_hbm, tiles_ref),
                (grad_hbm, grad_ref),
            ]
        )
    ]
    for n in (4, 5, 6, 0, 1, 2, 3):
        copies[n].start()
    for copy in copies:
        copy.wait()
    device, feat = place()
    near = nx * nb
    capacity, nodes = ids_ref.shape
    locals_, width = features_ref.shape
    count, targets, _ = tiles_ref.shape
    part = sent_ref.shape[1] - na * capacity - na - 8
    part = part // count
    lanes = targets // capacity
    near_at = near_index(device, na, nb)

    used = lax.broadcasted_iota(jnp.int32, (capacity, nodes), 0) < counts_ref[pl.ds(device, 1), :]
    slots = jnp.where(used, slots_ref[...], targets).astype(f32)
    slots = jnp.concatenate([slots] * lanes, axis=0)
    slots = jnp.concatenate([slots, jnp.zeros((targets, targets - nodes), f32)], axis=1).T
    group = lax.broadcasted_iota(jnp.int32, (targets, targets), 1) // capacity
    slots_scratch[...] = jnp.where(group == near_at % lanes, slots, 0.0)
    shape = (part, grad_ref.shape[1])
    column = lax.broadcasted_iota(jnp.int32, shape, 0) + feat * part
    mine = jnp.where(column == lax.broadcasted_iota(jnp.int32, shape, 1), 1.0, 0.0).astype(bf16)
    grad_t = dot(mine, grad_ref[...], ((1,), (1,))).astype(bf16)
    terms = [dot(grad_t, tiles_ref[k], ((1,), (0,))) for k in range(count)]
    blocks = [blocks_ref[0, k] for k in range(count)]
    row = lax.broadcasted_iota(jnp.int32, (8, targets), 0)
    far_rows = jnp.zeros((8, targets), jnp.int32)
    for k in range(count):
        far_rows = jnp.where(row == k, blocks[k] % (na * nb) // nb, far_rows)
        far_rows = jnp.where(row == count + k, blocks[k] // (na * nb) * nb + blocks[k] % nb, far_rows)
    far_rows = far_rows.astype(f32)
    local_ids = lax.broadcasted_iota(jnp.int32, (capacity, locals_), 1)
    outs = []
    for x in range(nx):
        for b in range(nb):
            to = x * nb + b
            owners = [(x * na + a) * nb + b for a in range(na)]
            chosen = jnp.concatenate(
                [jnp.where(ids_ref[:, o : o + 1] == local_ids, 1.0, 0.0).astype(bf16) for o in owners],
                axis=0,
            )
            rows = dot(chosen, features_ref[...], ((1,), (0,)))
            sent_ref[to, : na * capacity, :] = rows.astype(bf16)
            at = na * capacity
            for k in range(count):
                there = blocks[k] // (na * nb) * nb + blocks[k] % nb == to
                term = jnp.where(there, terms[k], 0.0)
                sent_ref[to, at : at + part, :] = term.astype(bf16)
                at += part
            slot_rows = slots_scratch[pl.ds(owners[0], na, stride=nb), :]
            sent_ref[to, at : at + na + 8, :] = jnp.concatenate([slot_rows, far_rows], 0).astype(bf16)
            out = pltpu.make_async_copy(sent_ref.at[to], sent_hbm.at[to], out_sems.at[to])
            out.start()
            outs.append(out)
    for out in outs:
        out.wait()


def pack(sample_ids, dest_slots, counts, blocks, features, tiles, grad, nx, na, nb, part, place):
    count, targets, _ = tiles.shape
    capacity, nodes = sample_ids.shape
    total = na * capacity + count * part + na + 8
    kernel = functools.partial(pack_kernel, nx=nx, na=na, nb=nb, place=place)
    args = (sample_ids, dest_slots, counts, blocks, features, tiles, grad)
    held = [pltpu.VMEM(arg.shape, arg.dtype) for arg in args]
    held[3] = pltpu.SMEM(blocks.shape, blocks.dtype)
    return pl.pallas_call(
        kernel,
        out_shape=jax.ShapeDtypeStruct((nx * nb, total, features.shape[1]), bf16),
        in_specs=[pl.BlockSpec(memory_space=pltpu.HBM)] * len(args),
        out_specs=pl.BlockSpec(memory_space=pltpu.HBM),
        scratch_shapes=held
        + [
            pltpu.VMEM((nx * nb, total, features.shape[1]), bf16),
            pltpu.VMEM((targets, targets), f32),
            pltpu.SemaphoreType.DMA((len(args),)),
            pltpu.SemaphoreType.DMA((nx * nb,)),
        ],
        compiler_params=pltpu.CompilerParams(vmem_limit_bytes=PACK_LIMIT),
    )(*args)


def in_vmem(kernel, out_shape, *args, scratch_shapes=()):
    vmem = pl.BlockSpec(memory_space=pltpu.VMEM)
    many = isinstance(out_shape, (list, tuple))
    return pl.pallas_call(
        kernel,
        out_shape=out_shape,
        in_specs=[vmem] * len(args),
        out_specs=[vmem] * len(out_shape) if many else vmem,
        scratch_shapes=scratch_shapes,
        compiler_params=pltpu.CompilerParams(vmem_limit_bytes=VMEM_LIMIT),
    )(*args)


def halve(values):
    high = values.astype(bf16)
    return high, (values - high.astype(f32)).astype(bf16)


def gather_kernel(
    got_ref, rows_ref, sent_ref, marks_ref, rows_t_ref, *, capacity, part, count
):
    rows_t_ref[...] = rows_ref[...].astype(f32).T.astype(bf16)
    near = got_ref.shape[0]
    far, _, targets = sent_ref.shape
    lanes = targets // capacity
    at = far * capacity + count * part
    marks = [got_ref[n, at : at + far + 8, :].astype(f32) for n in range(near)]
    for n in range(near):
        marks_ref[n] = got_ref[n, at : at + far + 8, :]
    slots = [sum(marks[h : h + lanes])[:far] for h in range(0, near, lanes)]
    nodes = lax.broadcasted_iota(jnp.int32, (targets, targets), 0).astype(f32)
    ones = jnp.ones((8, targets), bf16)
    back = [jnp.zeros((part, targets), f32) for _ in range(far)]
    for n in range(near):
        for k in range(count):
            start = far * capacity + k * part
            term = got_ref[n, start : start + part, :].astype(f32)
            mark = jnp.broadcast_to(marks[n][far + k : far + k + 1, :], (part, targets))
            back = [back[a] + jnp.where(mark == float(a), term, 0.0) for a in range(far)]
    for a in range(far):
        total = jnp.zeros((targets, targets), f32)
        degree = jnp.zeros((8, targets), f32)
        for h in range(near // lanes):
            chosen = jnp.where(slots[h][a : a + 1, :] == nodes, 1.0, 0.0).astype(bf16)
            rows = [
                got_ref[h * lanes + n, a * capacity : (a + 1) * capacity, :] for n in range(lanes)
            ]
            total += dot(chosen, jnp.concatenate(rows, axis=0), ((1,), (0,)))
            degree += dot(ones, chosen, ((1,), (1,)))
        sent_ref[a] = jnp.concatenate([total, back[a], degree], axis=0).astype(bf16)


def first_kernel(came_ref, rows_ref, self_ref, other_ref, sent_ref, mean_ref, *, part):
    targets = rows_ref.shape[0]
    came = came_ref[0].astype(f32)
    for a in range(1, came_ref.shape[0]):
        came += came_ref[a].astype(f32)
    degree = jnp.broadcast_to(came[targets + part : targets + part + 1, :], (targets, targets)).T
    high, low = halve(came[:targets] / (degree + 1.0))
    mean_ref[...] = high
    pre = dot(rows_ref[...], self_ref[...], ((1,), (0,)))
    pre += dot(high, other_ref[...], ((1,), (0,)))
    pre += dot(low, other_ref[...], ((1,), (0,)))
    back = halve(came[targets : targets + part])
    all_rows = jnp.concatenate([pre.T.astype(bf16), *back], axis=0)
    for y in range(sent_ref.shape[0]):
        sent_ref[y] = all_rows


def pair_kernel(got_ref, sent_ref, *, hidden):
    pre = got_ref[0, :hidden, :].astype(f32)
    for y in range(1, got_ref.shape[0]):
        pre += got_ref[y, :hidden, :].astype(f32)
    back = [got_ref[y, hidden:, :] for y in range(got_ref.shape[0])]
    sent_ref[...] = jnp.concatenate([*halve(pre), *back], axis=0)


def grads_kernel(
    got_ref,
    self_ref,
    other_ref,
    grad_ref,
    rows_t_ref,
    mean_ref,
    sent_ref,
    hidden_ref,
    mine_ref,
    scratch,
    *,
    part,
    slice_at,
):
    cores, near = got_ref.shape[0], sent_ref.shape[0]
    hidden = self_ref.shape[0]
    pre = got_ref[0, :hidden, :].astype(f32) + got_ref[0, hidden : 2 * hidden, :].astype(f32)
    for c in range(1, cores):
        pre += got_ref[c, :hidden, :].astype(f32)
        pre += got_ref[c, hidden : 2 * hidden, :].astype(f32)
    sigma = 1.0 / (1.0 + jnp.exp(-pre))
    slope = sigma * (1.0 + pre * (1.0 - sigma))
    scratch[...] = pre * sigma
    hidden_ref[...] = scratch[...].astype(bf16)
    mine = scratch[pl.ds(pl.multiple_of(slice_at() * part, part), part), :].astype(bf16)
    mine_ref[...] = mine
    back_high, back_low = [], []
    for y in range(hidden // part // cores):
        at = 2 * (hidden + y * part)
        for c in range(cores):
            back_high.append(got_ref[c, at : at + part, :])
            back_low.append(got_ref[c, at + part : at + 2 * part, :])
    back_high = jnp.concatenate(back_high, axis=0)
    back_low = jnp.concatenate(back_low, axis=0)
    grad = dot(self_ref[...], grad_ref[...], ((1,), (1,)))
    grad += dot(other_ref[...], back_high, ((1,), (0,)))
    grad += dot(other_ref[...], back_low, ((1,), (0,)))
    grad = (grad * slope).astype(bf16)
    mean_t = mean_ref[...].astype(f32).T.astype(bf16)
    lower = quarters(dot(rows_t_ref[...], grad, ((1,), (1,))), dot(mean_t, grad, ((1,), (1,))))
    upper = quarters(
        dot(mine, grad_ref[...], ((1,), (0,))),
        dot(mine, back_high, ((1,), (1,))) + dot(mine, back_low, ((1,), (1,))),
    )
    rows_each, share = lower.shape[0] // near, upper.shape[0] // near
    for n in range(near):
        sent_ref[n, :rows_each, :] = lower[n * rows_each : (n + 1) * rows_each]
        sent_ref[n, rows_each:, :] = upper[n * share : (n + 1) * share]


def far_kernel(got_ref, hidden_ref, sent_ref):
    total = got_ref[0].astype(f32)
    for n in range(1, got_ref.shape[0]):
        total += got_ref[n].astype(f32)
    total = total.astype(bf16)
    sums = total.shape[0]
    for a in range(sent_ref.shape[0]):
        sent_ref[a, :sums, :] = total
        sent_ref[a, sums:, :] = hidden_ref[...]


def near_kernel(got_ref, marks_ref, sent_ref, *, sums, part, count, where):
    far = got_ref.shape[0]
    total = got_ref[0, :sums, :].astype(f32)
    for a in range(1, far):
        total += got_ref[a, :sums, :].astype(f32)
    total = total.astype(bf16)
    here = where().astype(f32)
    blocks = [got_ref[a, sums:, :].astype(f32) for a in range(far)]
    for n in range(sent_ref.shape[0]):
        sent_ref[n, :sums, :] = total
        marks = marks_ref[n].astype(f32)
        for k in range(count):
            mark = jnp.where(marks[far + count + k :][:1] == here, marks[far + k :][:1], -1.0)
            mark = jnp.broadcast_to(mark, blocks[0].shape)
            block = jnp.zeros_like(blocks[0])
            for a in range(far):
                block = jnp.where(mark == float(a), blocks[a], block)
            at = sums + k * part
            sent_ref[n, at : at + part, :] = block.astype(bf16)


def second_kernel(got_ref, tiles_ref, sent_ref, *, rows_each, share, part):
    near = got_ref.shape[0]
    agg = jnp.zeros((part, tiles_ref.shape[1]), f32)
    for k in range(tiles_ref.shape[0]):
        at = rows_each + share + k * part
        block = got_ref[0, at : at + part, :].astype(f32)
        for n in range(1, near):
            block += got_ref[n, at : at + part, :].astype(f32)
        agg += dot(block.astype(bf16), tiles_ref[k], ((1,), (1,)))
    rows = [got_ref[n, rows_each : rows_each + share, :] for n in range(near)]
    both = jnp.concatenate([agg.astype(bf16)] + rows, axis=0)
    for f in range(sent_ref.shape[0]):
        sent_ref[f] = both


def last_kernel(
    got_ref,
    hidden_ref,
    self_ref,
    other_ref,
    lower_ref,
    out_ref,
    low_first_ref,
    low_second_ref,
    first_ref,
    second_ref,
    *,
    part,
    rows_each,
):
    cores = got_ref.shape[0]
    feats = first_ref.shape[0] // part
    rows = got_ref.shape[1] // (feats // cores)

    def slice_rows(f, start):
        at = f // cores * rows + start
        return got_ref[f % cores, at : at + part, :]

    half = first_ref.shape[1] // 2
    agg = jnp.concatenate([slice_rows(f, 0) for f in range(feats)], axis=0)
    out = dot(hidden_ref[...], self_ref[...], ((0,), (0,))) + dot(agg, other_ref[...], ((0,), (0,)))
    out_ref[...] = out.astype(bf16)
    for f in range(feats):
        at = f * part
        for n, ref in enumerate([first_ref, second_ref]):
            start = part * (1 + 2 * n)
            ref[at : at + part, :half] = slice_rows(f, start).astype(f32)
            ref[at : at + part, half:] = slice_rows(f, start + part).astype(f32)
    width = low_first_ref.shape[0]
    for n in range(lower_ref.shape[0]):
        quarter, at = divmod(n * rows_each, width)
        ref = (low_first_ref, low_second_ref)[quarter // 2]
        left = quarter % 2 * half
        part_rows = lower_ref[n, :rows_each, :].astype(f32)
        ref[at : at + rows_each, left : left + half] = part_rows


def shards(
    features,
    self_one,
    neighbour_one,
    sample_ids,
    dest_slots,
    send_counts,
    self_ids,
    tile_blocks,
    tile_weights,
    self_two,
    neighbour_two,
    out_grad,
):
    feats = lax.axis_size("feat")
    nodes = lax.axis_size("node")
    nx, nb = 4, 2
    na = nodes // (nx * nb)
    near = nx * nb
    near_ids = [(x * na + a) * nb + b for a in range(na) for x in range(nx) for b in range(nb)]
    near_groups = [near_ids[a * near : (a + 1) * near] for a in range(na)]
    far_groups = [list(group) for group in zip(*near_groups)]
    cores = 2
    core_groups = [[y * cores + c for c in range(cores)] for y in range(feats // cores)]
    y_groups = [list(group) for group in zip(*core_groups)]
    capacity = sample_ids.shape[2]
    targets = self_ids.shape[1]
    width = features.shape[1]
    hidden = neighbour_one.shape[1]
    part = hidden // feats
    tiles = tile_weights[0]
    count = tiles.shape[0]

    sent = pack(
        sample_ids[0].T,
        dest_slots[0].T,
        send_counts,
        tile_blocks,
        features,
        tiles,
        out_grad,
        nx,
        na,
        nb,
        part,
        where_am_i,
    )
    got = exchange(sent, "node", near_groups)
    self_rows = pick(features, self_ids[0])

    sent, marks, self_rows_t = in_vmem(
        functools.partial(gather_kernel, capacity=capacity, part=part, count=count),
        [
            jax.ShapeDtypeStruct((na, targets + part + 8, width), bf16),
            jax.ShapeDtypeStruct((near, na + 8, targets), bf16),
            jax.ShapeDtypeStruct((width, targets), bf16),
        ],
        got,
        self_rows,
    )
    came = exchange(sent, "node", far_groups)

    sent, mean_high = in_vmem(
        functools.partial(first_kernel, part=part),
        [
            jax.ShapeDtypeStruct((feats // cores, hidden + 2 * part, targets), bf16),
            jax.ShapeDtypeStruct((targets, width), bf16),
        ],
        came,
        self_rows,
        self_one,
        neighbour_one,
    )
    got = exchange(sent, "feat", y_groups)
    sent = in_vmem(
        functools.partial(pair_kernel, hidden=hidden),
        jax.ShapeDtypeStruct((2 * hidden + 2 * part * feats // cores, targets), bf16),
        got,
    )
    got = lax.all_gather(sent, "feat", axis_index_groups=core_groups)

    half = hidden // 2
    rows_each, share = 4 * width // near, 4 * part // near
    sent, hidden_t, hidden_part = in_vmem(
        functools.partial(grads_kernel, part=part, slice_at=lambda: lax.axis_index("feat")),
        [
            jax.ShapeDtypeStruct((near, rows_each + share, half), bf16),
            jax.ShapeDtypeStruct((hidden, targets), bf16),
            jax.ShapeDtypeStruct((part, targets), bf16),
        ],
        got,
        self_two,
        neighbour_two,
        out_grad,
        self_rows_t,
        mean_high,
        scratch_shapes=[pltpu.VMEM((hidden, targets), f32)],
    )
    got = exchange(sent, "node", near_groups)
    sent = in_vmem(
        far_kernel,
        jax.ShapeDtypeStruct((na, rows_each + share + part, half), bf16),
        got,
        hidden_part,
    )
    got = exchange(sent, "node", far_groups)
    sums = rows_each + share
    sent = in_vmem(
        functools.partial(
            near_kernel,
            sums=sums,
            part=part,
            count=count,
            where=lambda: near_index(lax.axis_index("node"), na, nb),
        ),
        jax.ShapeDtypeStruct((near, sums + count * part, half), bf16),
        got,
        marks,
    )
    got = exchange(sent, "node", near_groups)
    lower = got

    sent = in_vmem(
        functools.partial(second_kernel, rows_each=rows_each, share=share, part=part),
        jax.ShapeDtypeStruct((feats // cores, part + near * share, targets), bf16),
        got,
        tiles,
    )
    got = exchange(sent, "feat", y_groups).reshape(-1, targets)
    got = lax.all_gather(got, "feat", axis_index_groups=core_groups)
    return in_vmem(
        functools.partial(last_kernel, part=part, rows_each=rows_each),
        [
            jax.ShapeDtypeStruct((targets, hidden), bf16),
            jax.ShapeDtypeStruct((width, hidden), f32),
            jax.ShapeDtypeStruct((width, hidden), f32),
            jax.ShapeDtypeStruct((hidden, hidden), f32),
            jax.ShapeDtypeStruct((hidden, hidden), f32),
        ],
        got,
        hidden_t,
        self_two,
        neighbour_two,
        lower,
    )


def solution(mesh):
    placed = (
        P("node", "feat"),
        P("feat", None),
        P("feat", None),
        P("node", None, None),
        P("node", None, None),
        P(),
        P("node", None),
        P("node", None),
        P("node", None, None, None),
        P(),
        P(),
        P("node", None),
    )
    return jax.shard_map(
        shards,
        mesh=mesh,
        in_specs=placed,
        out_specs=(P("node", None), P("feat", None), P("feat", None), P(), P()),
        check_vma=False,
    )
```

```python
import functools

import jax
import jax.numpy as jnp
from jax import lax
from jax.experimental import pallas as pl
from jax.experimental.pallas import tpu as pltpu
from jax.sharding import PartitionSpec as P

bf16 = jnp.bfloat16
f32 = jnp.float32
VMEM_LIMIT = 16 * 1024 * 1024
PACK_LIMIT = 60 * 1024 * 1024


def dot(a, b, dims):
    return lax.dot_general(a, b, (dims, ((), ())), preferred_element_type=f32)


def exchange(values, axis, groups=None):
    return lax.all_to_all(
        values, axis, split_axis=0, concat_axis=0, tiled=True, axis_index_groups=groups
    )


def pick(table, row_ids):
    local_ids = jnp.arange(table.shape[0], dtype=jnp.int32)
    chosen = (row_ids[:, None] == local_ids[None, :]).astype(table.dtype)
    return dot(chosen, table, ((1,), (0,))).astype(table.dtype)


def quarters(first, second):
    half = first.shape[1] // 2
    parts = [first[:, :half], first[:, half:], second[:, :half], second[:, half:]]
    return jnp.concatenate(parts, axis=0).astype(bf16)


def near_index(device, na, nb):
    return device // (na * nb) * nb + device % nb


def where_am_i():
    return lax.axis_index("node"), lax.axis_index("feat")


def pack_kernel(
    ids_hbm,
    slots_hbm,
    counts_hbm,
    blocks_hbm,
    features_hbm,
    tiles_hbm,
    grad_hbm,
    sent_hbm,
    ids_ref,
    slots_ref,
    counts_ref,
    blocks_ref,
    features_ref,
    tiles_ref,
    grad_ref,
    sent_ref,
    slots_scratch,
    grad_scratch,
    sems,
    out_sems,
    *,
    nx,
    na,
    nb,
    place,
):
    copies = [
        pltpu.make_async_copy(source, target, sems.at[n])
        for n, (source, target) in enumerate(
            [
                (ids_hbm, ids_ref),
                (slots_hbm, slots_ref),
                (counts_hbm, counts_ref),
                (blocks_hbm, blocks_ref),
                (features_hbm, features_ref),
                (tiles_hbm, tiles_ref),
                (grad_hbm, grad_ref),
            ]
        )
    ]
    for copy in copies:
        copy.start()
    for copy in copies:
        copy.wait()
    device, feat = place()
    near = nx * nb
    capacity, nodes = ids_ref.shape
    locals_, width = features_ref.shape
    count, targets, _ = tiles_ref.shape
    part = sent_ref.shape[1] - na * capacity - na - 8
    part = part // count
    lanes = targets // capacity
    near_at = near_index(device, na, nb)

    used = lax.broadcasted_iota(jnp.int32, (capacity, nodes), 0) < counts_ref[pl.ds(device, 1), :]
    slots = jnp.where(used, slots_ref[...], targets).astype(f32)
    slots = jnp.concatenate([slots] * lanes, axis=0)
    slots = jnp.concatenate([slots, jnp.zeros((targets, targets - nodes), f32)], axis=1).T
    group = lax.broadcasted_iota(jnp.int32, (targets, targets), 1) // capacity
    slots_scratch[...] = jnp.where(group == near_at % lanes, slots, 0.0)
    grad_scratch[...] = grad_ref[...].astype(f32).T
    grad_t = grad_scratch[pl.ds(pl.multiple_of(feat * part, part), part), :].astype(bf16)
    terms = [dot(grad_t, tiles_ref[k], ((1,), (0,))) for k in range(count)]
    blocks = [blocks_ref[0, k] for k in range(count)]
    row = lax.broadcasted_iota(jnp.int32, (8, targets), 0)
    far_rows = jnp.zeros((8, targets), jnp.int32)
    for k in range(count):
        far_rows = jnp.where(row == k, blocks[k] % (na * nb) // nb, far_rows)
        far_rows = jnp.where(row == count + k, blocks[k] // (na * nb) * nb + blocks[k] % nb, far_rows)
    far_rows = far_rows.astype(f32)
    local_ids = lax.broadcasted_iota(jnp.int32, (capacity, locals_), 1)
    outs = []
    for x in range(nx):
        for b in range(nb):
            to = x * nb + b
            owners = [(x * na + a) * nb + b for a in range(na)]
            chosen = jnp.concatenate(
                [jnp.where(ids_ref[:, o : o + 1] == local_ids, 1.0, 0.0).astype(bf16) for o in owners],
                axis=0,
            )
            rows = dot(chosen, features_ref[...], ((1,), (0,)))
            sent_ref[to, : na * capacity, :] = rows.astype(bf16)
            at = na * capacity
            for k in range(count):
                there = blocks[k] // (na * nb) * nb + blocks[k] % nb == to
                term = jnp.where(there, terms[k], 0.0)
                sent_ref[to, at : at + part, :] = term.astype(bf16)
                at += part
            slot_rows = slots_scratch[pl.ds(owners[0], na, stride=nb), :]
            sent_ref[to, at : at + na + 8, :] = jnp.concatenate([slot_rows, far_rows], 0).astype(bf16)
            out = pltpu.make_async_copy(sent_ref.at[to], sent_hbm.at[to], out_sems.at[to])
            out.start()
            outs.append(out)
    for out in outs:
        out.wait()


def pack(sample_ids, dest_slots, counts, blocks, features, tiles, grad, nx, na, nb, part, place):
    count, targets, _ = tiles.shape
    capacity, nodes = sample_ids.shape
    total = na * capacity + count * part + na + 8
    kernel = functools.partial(pack_kernel, nx=nx, na=na, nb=nb, place=place)
    args = (sample_ids, dest_slots, counts, blocks, features, tiles, grad)
    held = [pltpu.VMEM(arg.shape, arg.dtype) for arg in args]
    held[3] = pltpu.SMEM(blocks.shape, blocks.dtype)
    return pl.pallas_call(
        kernel,
        out_shape=jax.ShapeDtypeStruct((nx * nb, total, features.shape[1]), bf16),
        in_specs=[pl.BlockSpec(memory_space=pltpu.HBM)] * len(args),
        out_specs=pl.BlockSpec(memory_space=pltpu.HBM),
        scratch_shapes=held
        + [
            pltpu.VMEM((nx * nb, total, features.shape[1]), bf16),
            pltpu.VMEM((targets, targets), f32),
            pltpu.VMEM((grad.shape[1], targets), f32),
            pltpu.SemaphoreType.DMA((len(args),)),
            pltpu.SemaphoreType.DMA((nx * nb,)),
        ],
        compiler_params=pltpu.CompilerParams(vmem_limit_bytes=PACK_LIMIT),
    )(*args)


def in_vmem(kernel, out_shape, *args, scratch_shapes=()):
    vmem = pl.BlockSpec(memory_space=pltpu.VMEM)
    many = isinstance(out_shape, (list, tuple))
    return pl.pallas_call(
        kernel,
        out_shape=out_shape,
        in_specs=[vmem] * len(args),
        out_specs=[vmem] * len(out_shape) if many else vmem,
        scratch_shapes=scratch_shapes,
        compiler_params=pltpu.CompilerParams(vmem_limit_bytes=VMEM_LIMIT),
    )(*args)


def halve(values):
    high = values.astype(bf16)
    return high, (values - high.astype(f32)).astype(bf16)


def gather_kernel(
    got_ref, rows_ref, sent_ref, marks_ref, rows_t_ref, *, capacity, part, count
):
    rows_t_ref[...] = rows_ref[...].astype(f32).T.astype(bf16)
    near = got_ref.shape[0]
    far, _, targets = sent_ref.shape
    lanes = targets // capacity
    at = far * capacity + count * part
    marks = [got_ref[n, at : at + far + 8, :].astype(f32) for n in range(near)]
    for n in range(near):
        marks_ref[n] = got_ref[n, at : at + far + 8, :]
    slots = [sum(marks[h : h + lanes])[:far] for h in range(0, near, lanes)]
    nodes = lax.broadcasted_iota(jnp.int32, (targets, targets), 0).astype(f32)
    ones = jnp.ones((8, targets), bf16)
    back = [jnp.zeros((part, targets), f32) for _ in range(far)]
    for n in range(near):
        for k in range(count):
            start = far * capacity + k * part
            term = got_ref[n, start : start + part, :].astype(f32)
            mark = marks[n][far + k : far + k + 1, :]
            back = [
                back[a] + jnp.where(mark == float(a), 1.0, 0.0) * term for a in range(far)
            ]
    for a in range(far):
        total = jnp.zeros((targets, targets), f32)
        degree = jnp.zeros((8, targets), f32)
        for h in range(near // lanes):
            chosen = jnp.where(slots[h][a : a + 1, :] == nodes, 1.0, 0.0).astype(bf16)
            rows = [
                got_ref[h * lanes + n, a * capacity : (a + 1) * capacity, :] for n in range(lanes)
            ]
            total += dot(chosen, jnp.concatenate(rows, axis=0), ((1,), (0,)))
            degree += dot(ones, chosen, ((1,), (1,)))
        sent_ref[a] = jnp.concatenate([total, back[a], degree], axis=0).astype(bf16)


def first_kernel(came_ref, rows_ref, self_ref, other_ref, sent_ref, mean_ref, *, part):
    targets = rows_ref.shape[0]
    came = came_ref[0].astype(f32)
    for a in range(1, came_ref.shape[0]):
        came += came_ref[a].astype(f32)
    degree = jnp.broadcast_to(came[targets + part : targets + part + 1, :], (targets, targets)).T
    high, low = halve(came[:targets] / (degree + 1.0))
    mean_ref[...] = high
    pre = dot(rows_ref[...], self_ref[...], ((1,), (0,)))
    pre += dot(high, other_ref[...], ((1,), (0,)))
    pre += dot(low, other_ref[...], ((1,), (0,)))
    back = halve(came[targets : targets + part])
    all_rows = jnp.concatenate([pre.T.astype(bf16), *back], axis=0)
    for y in range(sent_ref.shape[0]):
        sent_ref[y] = all_rows


def pair_kernel(got_ref, sent_ref, *, hidden):
    pre = got_ref[0, :hidden, :].astype(f32)
    for y in range(1, got_ref.shape[0]):
        pre += got_ref[y, :hidden, :].astype(f32)
    back = [got_ref[y, hidden:, :] for y in range(got_ref.shape[0])]
    sent_ref[...] = jnp.concatenate([*halve(pre), *back], axis=0)


def grads_kernel(
    got_ref,
    self_ref,
    other_ref,
    grad_ref,
    rows_t_ref,
    mean_ref,
    sent_ref,
    hidden_ref,
    mine_ref,
    scratch,
    *,
    part,
    slice_at,
):
    cores, near = got_ref.shape[0], sent_ref.shape[0]
    hidden = self_ref.shape[0]
    pre = got_ref[0, :hidden, :].astype(f32) + got_ref[0, hidden : 2 * hidden, :].astype(f32)
    for c in range(1, cores):
        pre += got_ref[c, :hidden, :].astype(f32)
        pre += got_ref[c, hidden : 2 * hidden, :].astype(f32)
    sigma = 1.0 / (1.0 + jnp.exp(-pre))
    slope = sigma * (1.0 + pre * (1.0 - sigma))
    scratch[...] = pre * sigma
    hidden_ref[...] = scratch[...].astype(bf16)
    mine = scratch[pl.ds(pl.multiple_of(slice_at() * part, part), part), :].astype(bf16)
    mine_ref[...] = mine
    back_high, back_low = [], []
    for y in range(hidden // part // cores):
        at = 2 * (hidden + y * part)
        for c in range(cores):
            back_high.append(got_ref[c, at : at + part, :])
            back_low.append(got_ref[c, at + part : at + 2 * part, :])
    back_high = jnp.concatenate(back_high, axis=0)
    back_low = jnp.concatenate(back_low, axis=0)
    grad = dot(self_ref[...], grad_ref[...], ((1,), (1,)))
    grad += dot(other_ref[...], back_high, ((1,), (0,)))
    grad += dot(other_ref[...], back_low, ((1,), (0,)))
    grad = (grad * slope).astype(bf16)
    mean_t = mean_ref[...].astype(f32).T.astype(bf16)
    lower = quarters(dot(rows_t_ref[...], grad, ((1,), (1,))), dot(mean_t, grad, ((1,), (1,))))
    upper = quarters(
        dot(mine, grad_ref[...], ((1,), (0,))),
        dot(mine, back_high, ((1,), (1,))) + dot(mine, back_low, ((1,), (1,))),
    )
    rows_each, share = lower.shape[0] // near, upper.shape[0] // near
    for n in range(near):
        sent_ref[n, :rows_each, :] = lower[n * rows_each : (n + 1) * rows_each]
        sent_ref[n, rows_each:, :] = upper[n * share : (n + 1) * share]


def far_kernel(got_ref, hidden_ref, sent_ref):
    total = got_ref[0].astype(f32)
    for n in range(1, got_ref.shape[0]):
        total += got_ref[n].astype(f32)
    total = total.astype(bf16)
    sums = total.shape[0]
    for a in range(sent_ref.shape[0]):
        sent_ref[a, :sums, :] = total
        sent_ref[a, sums:, :] = hidden_ref[...]


def near_kernel(got_ref, marks_ref, sent_ref, *, sums, part, count, where):
    far = got_ref.shape[0]
    total = got_ref[0, :sums, :].astype(f32)
    for a in range(1, far):
        total += got_ref[a, :sums, :].astype(f32)
    total = total.astype(bf16)
    here = where().astype(f32)
    blocks = [got_ref[a, sums:, :].astype(f32) for a in range(far)]
    for n in range(sent_ref.shape[0]):
        sent_ref[n, :sums, :] = total
        marks = marks_ref[n].astype(f32)
        for k in range(count):
            mark = jnp.where(marks[far + count + k :][:1] == here, marks[far + k :][:1], -1.0)
            mark = jnp.broadcast_to(mark, blocks[0].shape)
            block = jnp.zeros_like(blocks[0])
            for a in range(far):
                block = jnp.where(mark == float(a), blocks[a], block)
            at = sums + k * part
            sent_ref[n, at : at + part, :] = block.astype(bf16)


def second_kernel(got_ref, tiles_ref, sent_ref, *, rows_each, share, part):
    near = got_ref.shape[0]
    agg = jnp.zeros((part, tiles_ref.shape[1]), f32)
    for k in range(tiles_ref.shape[0]):
        at = rows_each + share + k * part
        block = got_ref[0, at : at + part, :].astype(f32)
        for n in range(1, near):
            block += got_ref[n, at : at + part, :].astype(f32)
        agg += dot(block.astype(bf16), tiles_ref[k], ((1,), (1,)))
    rows = [got_ref[n, rows_each : rows_each + share, :] for n in range(near)]
    both = jnp.concatenate([agg.astype(bf16)] + rows, axis=0)
    for f in range(sent_ref.shape[0]):
        sent_ref[f] = both


def last_kernel(
    got_ref,
    hidden_ref,
    self_ref,
    other_ref,
    lower_ref,
    out_ref,
    low_first_ref,
    low_second_ref,
    first_ref,
    second_ref,
    *,
    part,
    rows_each,
):
    cores = got_ref.shape[0]
    feats = first_ref.shape[0] // part
    rows = got_ref.shape[1] // (feats // cores)

    def slice_rows(f, start):
        at = f // cores * rows + start
        return got_ref[f % cores, at : at + part, :]

    half = first_ref.shape[1] // 2
    agg = jnp.concatenate([slice_rows(f, 0) for f in range(feats)], axis=0)
    out = dot(hidden_ref[...], self_ref[...], ((0,), (0,))) + dot(agg, other_ref[...], ((0,), (0,)))
    out_ref[...] = out.astype(bf16)
    for f in range(feats):
        at = f * part
        for n, ref in enumerate([first_ref, second_ref]):
            start = part * (1 + 2 * n)
            ref[at : at + part, :half] = slice_rows(f, start).astype(f32)
            ref[at : at + part, half:] = slice_rows(f, start + part).astype(f32)
    width = low_first_ref.shape[0]
    for n in range(lower_ref.shape[0]):
        quarter, at = divmod(n * rows_each, width)
        ref = (low_first_ref, low_second_ref)[quarter // 2]
        left = quarter % 2 * half
        part_rows = lower_ref[n, :rows_each, :].astype(f32)
        ref[at : at + rows_each, left : left + half] = part_rows


def shards(
    features,
    self_one,
    neighbour_one,
    sample_ids,
    dest_slots,
    send_counts,
    self_ids,
    tile_blocks,
    tile_weights,
    self_two,
    neighbour_two,
    out_grad,
):
    feats = lax.axis_size("feat")
    nodes = lax.axis_size("node")
    nx, nb = 4, 2
    na = nodes // (nx * nb)
    near = nx * nb
    near_ids = [(x * na + a) * nb + b for a in range(na) for x in range(nx) for b in range(nb)]
    near_groups = [near_ids[a * near : (a + 1) * near] for a in range(na)]
    far_groups = [list(group) for group in zip(*near_groups)]
    cores = 2
    core_groups = [[y * cores + c for c in range(cores)] for y in range(feats // cores)]
    y_groups = [list(group) for group in zip(*core_groups)]
    capacity = sample_ids.shape[2]
    targets = self_ids.shape[1]
    width = features.shape[1]
    hidden = neighbour_one.shape[1]
    part = hidden // feats
    tiles = tile_weights[0]
    count = tiles.shape[0]

    sent = pack(
        sample_ids[0].T,
        dest_slots[0].T,
        send_counts,
        tile_blocks,
        features,
        tiles,
        out_grad,
        nx,
        na,
        nb,
        part,
        where_am_i,
    )
    got = exchange(sent, "node", near_groups)
    self_rows = pick(features, self_ids[0])

    sent, marks, self_rows_t = in_vmem(
        functools.partial(gather_kernel, capacity=capacity, part=part, count=count),
        [
            jax.ShapeDtypeStruct((na, targets + part + 8, width), bf16),
            jax.ShapeDtypeStruct((near, na + 8, targets), bf16),
            jax.ShapeDtypeStruct((width, targets), bf16),
        ],
        got,
        self_rows,
    )
    came = exchange(sent, "node", far_groups)

    sent, mean_high = in_vmem(
        functools.partial(first_kernel, part=part),
        [
            jax.ShapeDtypeStruct((feats // cores, hidden + 2 * part, targets), bf16),
            jax.ShapeDtypeStruct((targets, width), bf16),
        ],
        came,
        self_rows,
        self_one,
        neighbour_one,
    )
    got = exchange(sent, "feat", y_groups)
    sent = in_vmem(
        functools.partial(pair_kernel, hidden=hidden),
        jax.ShapeDtypeStruct((2 * hidden + 2 * part * feats // cores, targets), bf16),
        got,
    )
    got = lax.all_gather(sent, "feat", axis_index_groups=core_groups)

    half = hidden // 2
    rows_each, share = 4 * width // near, 4 * part // near
    sent, hidden_t, hidden_part = in_vmem(
        functools.partial(grads_kernel, part=part, slice_at=lambda: lax.axis_index("feat")),
        [
            jax.ShapeDtypeStruct((near, rows_each + share, half), bf16),
            jax.ShapeDtypeStruct((hidden, targets), bf16),
            jax.ShapeDtypeStruct((part, targets), bf16),
        ],
        got,
        self_two,
        neighbour_two,
        out_grad,
        self_rows_t,
        mean_high,
        scratch_shapes=[pltpu.VMEM((hidden, targets), f32)],
    )
    got = exchange(sent, "node", near_groups)
    sent = in_vmem(
        far_kernel,
        jax.ShapeDtypeStruct((na, rows_each + share + part, half), bf16),
        got,
        hidden_part,
    )
    got = exchange(sent, "node", far_groups)
    sums = rows_each + share
    sent = in_vmem(
        functools.partial(
            near_kernel,
            sums=sums,
            part=part,
            count=count,
            where=lambda: near_index(lax.axis_index("node"), na, nb),
        ),
        jax.ShapeDtypeStruct((near, sums + count * part, half), bf16),
        got,
        marks,
    )
    got = exchange(sent, "node", near_groups)
    lower = got

    sent = in_vmem(
        functools.partial(second_kernel, rows_each=rows_each, share=share, part=part),
        jax.ShapeDtypeStruct((feats // cores, part + near * share, targets), bf16),
        got,
        tiles,
    )
    got = exchange(sent, "feat", y_groups).reshape(-1, targets)
    got = lax.all_gather(got, "feat", axis_index_groups=core_groups)
    return in_vmem(
        functools.partial(last_kernel, part=part, rows_each=rows_each),
        [
            jax.ShapeDtypeStruct((targets, hidden), bf16),
            jax.ShapeDtypeStruct((width, hidden), f32),
            jax.ShapeDtypeStruct((width, hidden), f32),
            jax.ShapeDtypeStruct((hidden, hidden), f32),
            jax.ShapeDtypeStruct((hidden, hidden), f32),
        ],
        got,
        hidden_t,
        self_two,
        neighbour_two,
        lower,
    )


def solution(mesh):
    placed = (
        P("node", "feat"),
        P("feat", None),
        P("feat", None),
        P("node", None, None),
        P("node", None, None),
        P(),
        P("node", None),
        P("node", None),
        P("node", None, None, None),
        P(),
        P(),
        P("node", None),
    )
    return jax.shard_map(
        shards,
        mesh=mesh,
        in_specs=placed,
        out_specs=(P("node", None), P("feat", None), P("feat", None), P(), P()),
        check_vma=False,
    )
```
